32 devices in a mesh: parts: 2 (over y), gx: 4 (over z), gy: 2 (over x), gz: 2 (over core).
Axes of the slice: x: 2, y: 2, z: 4, core: 2. Of those that a mesh axis runs over, the one named last changes fastest.
Arguments:
- forward_pops: bfloat16 [19, 256, 16, 256], P(None, ('parts', 'gx'), 'gy', 'gz'), parts along dimension 1, as said below
- adjoint_pops: bfloat16 [19, 256, 16, 256], P(None, ('parts', 'gx'), 'gy', 'gz'), parts along dimension 1, may hold values from -6 to 6
- coefficients: float32 [64, 4, 64], P(('parts', 'gx'), 'gy', 'gz'), parts along dimension 0, may hold values from -3 to 3
- node_kind: int32 [256, 16, 256], P(('parts', 'gx'), 'gy', 'gz'), parts along dimension 0, may hold values from 0 to 3, as said below
Outputs:
- prior_adjoint: bfloat16 [19, 256, 16, 256], P(None, ('parts', 'gx'), 'gy', 'gz'), parts along dimension 1
- coef_gradient: float32 [64, 4, 64], P(('parts', 'gx'), 'gy', 'gz'), parts along dimension 0
The draws below stay inside these ranges and needn't reach their ends.
There are 2 independent parts, one for each index of `parts`. The reference program is written for one: setup_inputs(seed, part) draws one part's arguments, and reference() takes and returns one part's arrays. A program takes and returns all parts, laid end to end along the dimension named above; each array names one. Nothing has to cross between parts.
Inputs may be any that keep to these rules, and one draw needn't show every extreme that they name: `node_kind`: node kinds: 0 fluid, 1 solid, 2 inlet, 3 outlet. `forward_pops`: every population lies between 0.4 and 1.7 times the lattice weight of its velocity.
All inputs are finite; a program needn't handle non-finite values.
Results may differ from the reference program's by a relative error of at most 0.001.
Values may be sent and summed in bfloat16 or wider, within the bound.
No kernel may reach another device: no remote copies, remote signals or barrier semaphores. Data moves between devices by JAX's collectives and lax.ppermute only.
A program may use at most 64 MiB of HBM per device.

```python
import jax
import jax.numpy as jnp
from jax import lax

CX = 32
NX = 128
NY = 16
NZ = 256
N_GX = 4


WEIGHTS = (1.0 / 3.0,) + (1.0 / 18.0,) * 6 + (1.0 / 36.0,) * 12


EASTWARD = (0.0, 1.0, -1.0, 0.0, 0.0, 0.0, 0.0, 1.0, -1.0, 1.0, -1.0, 1.0, -1.0, 1.0, -1.0, 0.0, 0.0, 0.0, 0.0)


def draw_forward_pops(key, part):
    weights = jnp.array(WEIGHTS, jnp.float32)[:, None, None, None]
    eastward = jnp.array(EASTWARD, jnp.float32)[:, None, None, None]
    noise = jax.random.uniform(key, (19, NX, NY, NZ), jnp.float32, -1.0, 1.0)
    values = weights * (1.0 + 0.15 * eastward + 0.45 * noise)
    return values.astype(jnp.bfloat16)


def draw_node_kind(key, part):
    roll = jax.random.randint(key, (NX, NY, NZ), 0, 20, dtype=jnp.int32)
    return jnp.where(roll < 3, 1, jnp.where(roll == 3, 2, jnp.where(roll == 4, 3, 0))).astype(jnp.int32)


def levels(key, dims, shards, smallest, largest):
    level = 1.0
    for axis_at, parts in shards:
        draws = jax.random.uniform(jax.random.fold_in(jax.random.fold_in(key, 6), axis_at), (parts,), jnp.float32, smallest / len(shards), largest / len(shards))
        level = level * jnp.repeat(jnp.exp(draws), dims[axis_at] // parts).reshape((-1,) + (1,) * (len(dims) - 1 - axis_at))
    return level


def normal_values(own_key, extent, deviation, most, pieces=(), kind=jnp.bfloat16):
    entries = deviation * jax.random.normal(own_key, extent, jnp.float32)
    if pieces:
        entries = entries * levels(own_key, extent, pieces, -0.22, 0.18)
    return jnp.clip(entries, -most, most).astype(kind)


def setup_inputs(seed: int = 0, part: int = 0) -> dict:
    seeds = jax.random.split(jax.random.key(seed), 5)
    part_keys = jax.random.split(jax.random.fold_in(seeds[4], part), 5)
    forward_pops = draw_forward_pops(jax.random.fold_in(jax.random.fold_in(seeds[4], part), 71), part)
    adjoint_pops = normal_values(part_keys[1], (19, NX, NY, NZ), 1.0, 6.0, ((1, 4), (2, 2), (3, 2)))
    coefficients = normal_values(part_keys[2], (NX // 4, NY // 4, NZ // 4), 0.5, 3.0, ((0, 4), (1, 2), (2, 2)), jnp.float32)
    node_kind = draw_node_kind(jax.random.fold_in(jax.random.fold_in(seeds[4], part), 71), part)
    return {"forward_pops": forward_pops, "adjoint_pops": adjoint_pops, "coefficients": coefficients, "node_kind": node_kind}


VELOCITY = ((0, 0, 0), (1, 0, 0), (-1, 0, 0), (0, 1, 0), (0, -1, 0), (0, 0, 1), (0, 0, -1), (1, 1, 0), (-1, -1, 0), (1, -1, 0), (-1, 1, 0), (1, 0, 1), (-1, 0, -1), (1, 0, -1), (-1, 0, 1), (0, 1, 1), (0, -1, -1), (0, 1, -1), (0, -1, 1))
OPPOSITE = (0, 2, 1, 4, 3, 6, 5, 8, 7, 10, 9, 12, 11, 14, 13, 16, 15, 18, 17)
WEIGHTS = (1.0 / 3.0,) + (1.0 / 18.0,) * 6 + (1.0 / 36.0,) * 12
relaxation = 1.6
inlet_speed = 0.05
highest = lax.Precision.HIGHEST

def equilibrium(density, flow_x, flow_y, flow_z):
    square = flow_x * flow_x + flow_y * flow_y + flow_z * flow_z
    layers = []
    for component in range(19):
        step_x, step_y, step_z = VELOCITY[component]
        projection = step_x * flow_x + step_y * flow_y + step_z * flow_z
        layers.append(WEIGHTS[component] * density * (1.0 + 3.0 * projection + 4.5 * projection * projection - 1.5 * square))
    return jnp.stack(layers)

def moment(populations, dimension):
    total = jnp.zeros_like(populations[0])
    for component in range(19):
        factor = VELOCITY[component][dimension]
        if factor != 0:
            total = total + factor * populations[component]
    return total

def collide(populations, porosity, node_kind):
    density = lax.optimization_barrier(jnp.sum(populations, axis=0))
    flow_x = moment(populations, 0) / density
    flow_y = moment(populations, 1) / density
    flow_z = moment(populations, 2) / density
    retained = 1.0 - porosity
    fluid_post = populations - relaxation * (populations - equilibrium(density, retained * flow_x, retained * flow_y, retained * flow_z))
    solid_post = jnp.stack([populations[OPPOSITE[component]] for component in range(19)])
    unit_density = jnp.ones_like(density)
    inlet_post = equilibrium(unit_density, inlet_speed * unit_density, jnp.zeros_like(density), jnp.zeros_like(density))
    outlet_post = equilibrium(unit_density, flow_x, flow_y, flow_z)
    kind_here = node_kind[None]
    return jnp.where(kind_here == 0, fluid_post, jnp.where(kind_here == 1, solid_post, jnp.where(kind_here == 2, inlet_post, outlet_post)))

def basis_matrix(fine_count, coarse_count, fine_offset, coarse_offset):
    fine_pos = jnp.arange(fine_count, dtype=jnp.float32) + fine_offset
    coarse_pos = jnp.arange(coarse_count, dtype=jnp.float32) + coarse_offset
    distance = fine_pos[:, None] - 4.0 * coarse_pos[None, :] - 1.5
    radius = jnp.abs(distance) / 6.0
    return jnp.where(radius < 1.0, (1.0 - radius) ** 4 * (1.0 + 4.0 * radius), 0.0)

def reference(forward_pops, adjoint_pops, coefficients, node_kind):
    basis_x = basis_matrix(NX, NX // 4, 0, 0)
    basis_y = basis_matrix(NY, NY // 4, 0, 0)
    basis_z = basis_matrix(NZ, NZ // 4, 0, 0)
    partway = jnp.einsum('ijk,zk->ijz', coefficients, basis_z, precision=highest)
    partway = jnp.einsum('ijz,yj->iyz', partway, basis_y, precision=highest)
    level_set = jnp.einsum('iyz,xi->xyz', partway, basis_x, precision=highest)
    bent = jnp.tanh(4.0 * level_set)
    porosity = 0.45 * (1.0 - bent)
    slope_phi = -1.8 * (1.0 - bent * bent)
    padded = jnp.pad(adjoint_pops, ((0, 0), (1, 1), (1, 1), (1, 1)))

    def block_step(block_index):
        row_start = (block_index * CX).astype(jnp.int32)
        anchor = jnp.zeros((), jnp.int32)
        piece = lax.dynamic_slice(padded, (anchor, row_start, anchor, anchor), (19, CX + 2, NY + 2, NZ + 2)).astype(jnp.float32)
        pulled = jnp.stack([piece[component, 1 + VELOCITY[component][0]:1 + VELOCITY[component][0] + CX, 1 + VELOCITY[component][1]:1 + VELOCITY[component][1] + NY, 1 + VELOCITY[component][2]:1 + VELOCITY[component][2] + NZ] for component in range(19)])
        forward = lax.dynamic_slice(forward_pops, (anchor, row_start, anchor, anchor), (19, CX, NY, NZ)).astype(jnp.float32)
        local_porosity = lax.dynamic_slice(porosity, (row_start, anchor, anchor), (CX, NY, NZ))
        local_kind = lax.dynamic_slice(node_kind, (row_start, anchor, anchor), (CX, NY, NZ))

        def local_collide(populations, porosity_here):
            return collide(populations, porosity_here, local_kind)
        unused, pullback = jax.vjp(local_collide, forward, local_porosity)
        prior, porosity_bar = pullback(pulled)
        return (prior.astype(jnp.bfloat16), porosity_bar)
    priors, bars = lax.map(block_step, jnp.arange(N_GX, dtype=jnp.int32))
    prior_adjoint = jnp.moveaxis(priors, 1, 0).reshape(19, NX, NY, NZ)
    sensitivity = bars.reshape(NX, NY, NZ) * slope_phi
    gradient = jnp.einsum('xyz,xi->iyz', sensitivity, basis_x, precision=highest)
    gradient = jnp.einsum('iyz,yj->ijz', gradient, basis_y, precision=highest)
    gradient = jnp.einsum('ijz,zk->ijk', gradient, basis_z, precision=highest)
    return (prior_adjoint, gradient)
```

```python
import functools

import jax
import jax.numpy as jnp
import numpy as np
from jax import lax
from jax.experimental import pallas as pl
from jax.experimental.pallas import tpu as pltpu
from jax.sharding import PartitionSpec as P

VELOCITY = (
    (0, 0, 0),
    (1, 0, 0),
    (-1, 0, 0),
    (0, 1, 0),
    (0, -1, 0),
    (0, 0, 1),
    (0, 0, -1),
    (1, 1, 0),
    (-1, -1, 0),
    (1, -1, 0),
    (-1, 1, 0),
    (1, 0, 1),
    (-1, 0, -1),
    (1, 0, -1),
    (-1, 0, 1),
    (0, 1, 1),
    (0, -1, -1),
    (0, 1, -1),
    (0, -1, 1),
)
OPPOSITE = (0, 2, 1, 4, 3, 6, 5, 8, 7, 10, 9, 12, 11, 14, 13, 16, 15, 18, 17)
highest = lax.Precision.HIGHEST
f32 = jnp.float32
bf16 = jnp.bfloat16


def going(dimension, sign):
    return [q for q in range(19) if VELOCITY[q][dimension] == sign]


XP, XM = going(0, 1), going(0, -1)
YP, YM = going(1, 1), going(1, -1)
ZP, ZM = going(2, 1), going(2, -1)

FACE, ALPHA, BETA, FIELD, COARSE, BUNDLE = 0, 5, 9, 13, 17, 19


def spline(distance):
    radius = np.abs(distance) / 6.0
    return np.where(radius < 1.0, (1.0 - radius) ** 4 * (1.0 + 4.0 * radius), 0.0)


def kernel_call(body, out_shape, scratch_shapes=(), cost=(0, 0)):
    return pl.pallas_call(
        body,
        out_shape=out_shape,
        scratch_shapes=list(scratch_shapes),
        compiler_params=pltpu.CompilerParams(vmem_limit_bytes=40 * 1024 * 1024),
        cost_estimate=pl.CostEstimate(flops=cost[0], bytes_accessed=cost[1], transcendentals=0),
    )


def iota(dimension):
    return lax.broadcasted_iota(jnp.int32, (8, 128), dimension)


def pulled_z(q, tile, x, columns):
    step = VELOCITY[q][2]
    if step == 0:
        return tile
    slot = (ZP if step > 0 else ZM).index(q) * 32
    group, lane = slot // 128, slot % 128
    lanes = iota(1)
    edge = columns[0 if step > 0 else 1, group]
    if step > 0:
        edge = pltpu.roll(edge, 127 - lane - x, 1)
        return jnp.where(lanes == 127, edge, pltpu.roll(tile, 127, 1))
    edge = pltpu.roll(edge, (128 - lane - x) & 127, 1)
    return jnp.where(lanes == 0, edge, pltpu.roll(tile, 1, 1))


def pulled_y(q, tile, x, rows):
    step = VELOCITY[q][1]
    if step == 0:
        return tile
    slot = (YP if step > 0 else YM).index(q) * 32
    row = rows[0 if step > 0 else 1, pl.ds(slot + x, 1), :]
    edge = jnp.broadcast_to(row, (8, 128))
    sublanes = iota(0)
    if step > 0:
        return jnp.where(sublanes == 7, edge, pltpu.roll(tile, 7, 0))
    return jnp.where(sublanes == 0, edge, pltpu.roll(tile, 1, 0))


def load_columns(core, received, columns):
    for group in range(2):
        tile = received[group]
        columns[0, group] = jnp.where(core == 0, tile, 0.0)
        columns[1, group] = jnp.where(core == 1, tile, 0.0)


def pair_moments(populations):
    sums, diffs = {}, {}
    for q in range(1, 19, 2):
        a, b = populations.get(q), populations.get(q + 1)
        if a is None and b is None:
            continue
        if b is None:
            sums[q], diffs[q] = a, a
        elif a is None:
            sums[q], diffs[q] = b, -b
        else:
            sums[q], diffs[q] = a + b, a - b

    def total(terms):
        value = None
        for sign, table, q in terms:
            if q not in table:
                continue
            item = table[q]
            if value is None:
                value = item if sign > 0 else -item
            else:
                value = value + item if sign > 0 else value - item
        return value

    def plus(a, b):
        return b if a is None else (a if b is None else a + b)

    def twice(a):
        return None if a is None else a + a

    xx = total([(1, sums, 7), (1, sums, 9), (1, sums, 11), (1, sums, 13)])
    edge_yz = total([(1, sums, 15), (1, sums, 17)])
    edge_xy = total([(1, sums, 7), (1, sums, 9)])
    edge_xz = total([(1, sums, 11), (1, sums, 13)])
    sx, sy, sz = (twice(sums.get(q)) for q in (1, 3, 5))
    zeroth = plus(plus(xx, edge_yz), plus(plus(sx, sy), sz))
    if 0 in populations:
        zeroth = zeroth + 12.0 * populations[0]
    mx = plus(twice(diffs.get(1)), total([(1, diffs, 7), (1, diffs, 9), (1, diffs, 11), (1, diffs, 13)]))
    my = plus(twice(diffs.get(3)), total([(1, diffs, 7), (-1, diffs, 9), (1, diffs, 15), (1, diffs, 17)]))
    mz = plus(twice(diffs.get(5)), total([(1, diffs, 11), (-1, diffs, 13), (1, diffs, 15), (-1, diffs, 17)]))
    mxx = plus(sx, xx)
    myy = plus(sy, plus(edge_xy, edge_yz))
    mzz = plus(sz, plus(edge_xz, edge_yz))
    mxy = total([(1, sums, 7), (-1, sums, 9)])
    mxz = total([(1, sums, 11), (-1, sums, 13)])
    myz = total([(1, sums, 15), (-1, sums, 17)])
    return zeroth, (mx, my, mz), (mxx, myy, mzz, mxy, mxz, myz)


def flow_moments(populations):
    sums = {q: populations[q] + populations[q + 1] for q in range(1, 19, 2)}
    diffs = {q: populations[q] - populations[q + 1] for q in range(1, 19, 2)}
    rho = populations[0]
    for q in range(1, 19, 2):
        rho = rho + sums[q]
    jx = (diffs[1] + diffs[7]) + (diffs[9] + diffs[11]) + diffs[13]
    jy = (diffs[3] + diffs[7]) + (diffs[15] - diffs[9]) + diffs[17]
    jz = (diffs[5] + diffs[11]) + (diffs[15] - diffs[13]) - diffs[17]
    return rho, (jx, jy, jz)


def dot3(a, b):
    return a[0] * b[0] + a[1] * b[1] + a[2] * b[2]


def second_times(second, v):
    mxx, myy, mzz, mxy, mxz, myz = second

    def row(terms):
        value = None
        for coefficient, component in terms:
            if coefficient is None:
                continue
            product = coefficient * component
            value = product if value is None else value + product
        return value

    return (
        row([(mxx, v[0]), (mxy, v[1]), (mxz, v[2])]),
        row([(mxy, v[0]), (myy, v[1]), (myz, v[2])]),
        row([(mxz, v[0]), (myz, v[1]), (mzz, v[2])]),
    )


def alpha_beta(moments, flow, flow_mass):
    zeroth, first, second = moments
    scale = flow_mass * (-1.6 / 36.0)
    alpha = scale * 3.0 * dot3(first, flow)
    beta = scale * (9.0 * dot3(second_times(second, flow), flow) - 3.0 * zeroth * dot3(flow, flow))
    return alpha, beta


def pack_z(adjoint, coefficients, out):
    core = lax.axis_index("gz")
    lanes = iota(1)
    count = coefficients.shape[2]
    out[2] = jnp.zeros((8, 128), f32)
    for which, (components, source) in enumerate(((ZM, 127), (ZP, 0))):

        @pl.when(core == which)
        def _():
            tiles = [jnp.zeros((8, 128), f32) for _ in range(2)]
            for k, q in enumerate(components):
                for x in range(32):
                    group, lane = divmod(k * 32 + x, 128)
                    column = pltpu.roll(adjoint[q, x].astype(f32), (lane - source) % 128, 1)
                    tiles[group] = jnp.where(lanes == lane, column, tiles[group])
            out[0] = tiles[0]
            out[1] = tiles[1]
            for j in range(2):
                start = 2 * count * j + count * which
                out[2, :, start : start + count] = coefficients[:, j, :]


def pack_y(directions, adjoint, sent, received, *refs):
    outs, (columns, plane, rows) = refs[:-3], refs[-3:]
    core = lax.axis_index("gz")
    load_columns(core, received, columns)
    coarse = sent[2] + received[2]
    high = coarse.astype(bf16)
    rest = coarse - high.astype(f32)
    middle = rest.astype(bf16)
    low = (rest - middle.astype(f32)).astype(bf16)

    def emit(components, row, out):
        for k, q in enumerate(components):

            def step(x, carry):
                tile = pulled_z(q, adjoint[q, x].astype(f32), x, columns)
                plane[pl.ds(pl.multiple_of(x * 8, 8), 8), :] = tile
                return carry

            lax.fori_loop(0, 32, step, 0, unroll=8)
            out[k * 32 : k * 32 + 32, :] = plane[pl.ds(row, 32, stride=8), :].astype(bf16)
        out[160:176, :] = jnp.concatenate([high, middle], axis=0)
        out[176:192, :] = jnp.concatenate([low, jnp.zeros((8, 128), bf16)], axis=0)

    if directions == 1:
        side = lax.axis_index("gy")
        pl.when(side == 0)(lambda: emit(YM, 7, outs[0]))
        pl.when(side == 1)(lambda: emit(YP, 0, outs[0]))
    else:
        emit(YM, 7, outs[0])
        emit(YP, 0, outs[1])


def pull_zy(directions, adjoint, forward, kind, sent_z, received_z, *refs):
    received_y = refs[:directions]
    pulled, to_low, to_high, columns, rows, coarse_ref = refs[directions:]
    core = lax.axis_index("gz")
    load_columns(core, received_z, columns)
    if directions == 1:
        side = lax.axis_index("gy")
        values = received_y[0][...].astype(f32)
        from_high = jnp.where(side == 0, values, 0.0)
        from_low = jnp.where(side == 1, values, 0.0)
    else:
        from_low = received_y[0][...].astype(f32)
        from_high = received_y[1][...].astype(f32)
    rows[0] = from_high
    rows[1] = from_low

    def coarse_of(values):
        return values[160:168] + values[168:176] + values[176:184]

    lanes = iota(1)
    rim = jnp.where(
        lanes < 64, pltpu.roll(coarse_of(from_low), 64, 1), pltpu.roll(coarse_of(from_high), 64, 1)
    )
    own = sent_z[2] + received_z[2]
    for out in (to_low, to_high):
        out[COARSE] = own
        out[COARSE + 1] = rim

    def step(x, carry):
        for q in range(19):
            if VELOCITY[q][1] == 0 and VELOCITY[q][2] == 0:
                pulled[q, x] = adjoint[q, x]
                continue
            tile = pulled_z(q, adjoint[q, x].astype(f32), x, columns)
            pulled[q, x] = pulled_y(q, tile, x, rows).astype(bf16)
        return carry

    lax.fori_loop(0, 32, step, 0)

    for out, base, faces, boundary in ((to_low, 0, XP, 0), (to_high, 28, XM, 31)):
        for k, q in enumerate(faces):
            out[FACE + k] = pulled[q, boundary].astype(f32)

        def edge(position, carry):
            x = base + position
            values = {}
            for q in range(19):
                target = x + VELOCITY[q][0]
                if VELOCITY[q][0] == 0:
                    values[q] = pulled[q, x].astype(f32)
                else:
                    inside = jnp.logical_and(target >= 0, target < 32)
                    tile = pulled[q, jnp.clip(target, 0, 31)].astype(f32)
                    values[q] = jnp.where(inside, tile, 0.0)
            rho, mass = flow_moments([forward[q, x].astype(f32) for q in range(19)])
            inverse = 1.0 / rho
            flow = tuple(component * inverse for component in mass)
            fluid_mass = jnp.where(kind[x] == 0, rho, 0.0)
            alpha, beta = alpha_beta(pair_moments(values), flow, fluid_mass)
            out[ALPHA + position] = alpha
            out[BETA + position] = beta

            @pl.when(x == boundary)
            def _():
                for dimension in range(3):
                    out[FIELD + dimension] = flow[dimension]
                out[FIELD + 3] = fluid_mass

            return carry

        lax.fori_loop(0, 4, edge, 0)


def collide_back(
    pulled, forward, kind, own, low, high, basis_z, basis_y, fold_y, fold_z,
    gradient, fields, window, lines, levels, totals,
):
    core = lax.axis_index("gz")
    zeros = jnp.zeros((16, 128), f32)
    for part in range(2):
        window[part * 16 : part * 16 + 16, :] = zeros
        window[part * 16 : part * 16 + 2, :] = low[COARSE + part, 6:8, :]
        window[part * 16 + 2 : part * 16 + 10, :] = own[COARSE + part]
        window[part * 16 + 10 : part * 16 + 12, :] = high[COARSE + part, 0:2, :]
    lines[...] = jnp.dot(
        window[...], basis_z[core], precision=highest, preferred_element_type=f32
    )
    weights = [basis_y[j] for j in range(4)]
    for i in range(12):
        level = None
        for j, (row, lane) in enumerate(((16, 0), (0, 0), (0, 128), (16, 128))):
            line = jnp.broadcast_to(lines[row + i : row + i + 1, lane : lane + 128], (8, 128))
            term = weights[j] * line
            level = term if level is None else level + term
        levels[i] = level
    totals[...] = jnp.zeros((10, 8, 128), f32)

    def level_set(block, position):
        value = None
        for shift in (-1, 0, 1):
            term = float(spline(position - 4.0 * shift - 1.5)) * levels[block + 2 + shift]
            value = term if value is None else value + term
        return jnp.tanh(4.0 * value)

    def spread(block, position, sensitivity):
        for shift in (-1, 0, 1):
            weight = float(spline(position - 4.0 * shift - 1.5))
            totals[block + 1 + shift] += weight * sensitivity

    def slope_of(bent):
        return -1.8 * (1.0 - bent * bent)

    def plane(x, block, position, fetch):
        bent = level_set(block, position)
        retained = 0.55 + 0.45 * bent
        rho, mass = flow_moments([forward[q, x].astype(f32) for q in range(19)])
        inverse = 1.0 / rho
        flow = tuple(component * inverse for component in mass)
        here = kind[x]
        fluid = here == 0
        share = jnp.where(fluid, retained, 1.0)
        speed = tuple(share * component for component in flow)
        zeroth, first, second = pair_moments({q: fetch(q) for q in range(19)})
        curved = second_times(second, speed)
        slopes = tuple(
            3.0 * first[n] + 9.0 * curved[n] - 3.0 * zeroth * speed[n] for n in range(3)
        )
        along = dot3(slopes, flow)
        value = zeroth + 0.5 * (3.0 * dot3(first, speed) + dot3(slopes, speed))
        factor = jnp.where(fluid, (1.6 / 36.0) * retained, jnp.where(here == 3, inverse * (1.0 / 36.0), 0.0))
        fields[0, x] = jnp.where(fluid, (1.6 / 36.0) * value, 0.0) - factor * along
        for n in range(3):
            fields[1 + n, x] = factor * slopes[n]
        bar = jnp.where(fluid, (-1.6 / 36.0) * rho * along, 0.0)
        spread(block, position, bar * slope_of(bent))

    def inside(q, x):
        return pulled[q, x + VELOCITY[q][0]].astype(f32)

    def at_low(q, x):
        if q in XM:
            return low[FACE + XM.index(q)]
        return inside(q, x)

    def at_high(q, x):
        if q in XP:
            return high[FACE + XP.index(q)]
        return inside(q, x)

    plane(0, 0, 0, lambda q: at_low(q, 0))
    for x in (1, 2, 3):
        plane(x, 0, x, lambda q: inside(q, x))

    def middle(block, carry):
        for position in range(4):
            x = block * 4 + position
            plane(x, block, position, lambda q: inside(q, x))
        return carry

    lax.fori_loop(1, 7, middle, 0)
    for x in (28, 29, 30):
        plane(x, 7, x - 28, lambda q: inside(q, x))
    plane(31, 7, 3, lambda q: at_high(q, 31))

    for ref, block, boundary, faces in ((low, -1, 3, XP), (high, 8, 0, XM)):
        source = 31 if block == 8 else 0
        flow = tuple(ref[FIELD + n] for n in range(3))
        missing = alpha_beta(
            pair_moments({q: pulled[q, source].astype(f32) for q in faces}), flow, ref[FIELD + 3]
        )
        for position in range(4):
            alpha, beta = ref[ALPHA + position], ref[BETA + position]
            if position == boundary:
                alpha, beta = alpha + missing[0], beta + missing[1]
            bent = level_set(block, position)
            sensitivity = (alpha + (0.55 + 0.45 * bent) * beta) * slope_of(bent)
            shift = 1 if block < 0 else -1
            weight = float(spline(position - 4.0 * shift - 1.5))
            totals[block + 1 + shift] += weight * sensitivity

    folded = jnp.dot(
        fold_y[...], totals[1:9].reshape(64, 128), precision=highest, preferred_element_type=f32
    )
    result = jnp.dot(folded, fold_z[core], precision=highest, preferred_element_type=f32)
    for part in range(2):
        for j in range(4):
            gradient[part, j] = result[j * 8 : j * 8 + 8, part * 32 : part * 32 + 32]


def write_prior(pulled, kind, low, high, fields, out):
    def plane(x, fetch):
        here = kind[x]
        solid = here == 1
        keep = jnp.where(here == 0, -0.6, 0.0)
        base, bx, by, bz = (fields[n, x] for n in range(4))
        along = {(0, 0): (base, base)}
        shifts = {}
        for step_x in (-1, 0, 1):
            row = base if step_x == 0 else (base + bx if step_x > 0 else base - bx)
            for step_y in (-1, 0, 1):
                both = row if step_y == 0 else (row + by if step_y > 0 else row - by)
                shifts[step_x, step_y] = both
        values = [fetch(q) for q in range(19)]
        for q in range(19):
            step_x, step_y, step_z = VELOCITY[q]
            shift = shifts[step_x, step_y]
            if step_z:
                shift = shift + bz if step_z > 0 else shift - bz
            kept = jnp.where(solid, values[OPPOSITE[q]], keep * values[q])
            out[q, x] = (kept + shift).astype(bf16)

    def inside(q, x):
        return pulled[q, x + VELOCITY[q][0]].astype(f32)

    plane(0, lambda q: low[FACE + XM.index(q)] if q in XM else inside(q, 0))

    def middle(x, carry):
        plane(x, lambda q: inside(q, x))
        return carry

    lax.fori_loop(1, 31, middle, 0)
    plane(31, lambda q: high[FACE + XP.index(q)] if q in XP else inside(q, 31))


def bases():
    fine = np.arange(128.0)
    basis_z = np.zeros((2, 128, 256))
    fold_z = np.zeros((2, 128, 64))
    for core in range(2):
        full = spline(fine[None, :] + 128 * core - 4.0 * np.arange(64)[:, None] - 1.5)
        basis_z[core, 0:64, 0:128] = full
        basis_z[core, 64:128, 128:256] = full
        fold_z[core, :, 0:32] = full[32 * core : 32 * core + 32].T
        fold_z[core, :, 32:64] = full[32 * (1 - core) : 32 * (1 - core) + 32].T
    across = spline(np.arange(8.0)[None, :] - 4.0 * np.arange(-1, 3)[:, None] - 1.5)
    basis_y = np.broadcast_to(across[:, :, None], (4, 8, 128))
    fold_y = np.zeros((4, 8, 8, 8))
    for i in range(8):
        fold_y[:, i, i, :] = across
    return [
        jnp.asarray(np.ascontiguousarray(a), f32)
        for a in (basis_z, basis_y, fold_y.reshape(32, 64), fold_z)
    ]


def pairs(count, first):
    result = []
    for i in range(first, count - 1, 2):
        result += [(i, i + 1), (i + 1, i)]
    return result


def per_device(forward, adjoint, coefficients, kind):
    count_y = lax.axis_size("gy")
    count_x = lax.axis_size("gx")
    swap = [(0, 1), (1, 0)]
    side = lax.axis_index("gy")
    directions = 1 if count_y == 2 else 2
    tile = (8, 128)

    sent_z = kernel_call(pack_z, jax.ShapeDtypeStruct((3,) + tile, f32))(adjoint, coefficients)
    received_z = lax.ppermute(sent_z, "gz", swap)

    strip = jax.ShapeDtypeStruct((192, 128), bf16)
    sent_y = kernel_call(
        functools.partial(pack_y, directions),
        [strip] * directions,
        [pltpu.VMEM((2, 2) + tile, f32), pltpu.VMEM((256, 128), f32), pltpu.VMEM((32, 128), f32)],
    )(adjoint, sent_z, received_z)
    up = [(i, i + 1) for i in range(count_y - 1)]
    down = [(i + 1, i) for i in range(count_y - 1)]
    if directions == 1:
        received_y = [lax.ppermute(sent_y[0], "gy", swap)]
    else:
        received_y = [lax.ppermute(sent_y[0], "gy", up), lax.ppermute(sent_y[1], "gy", down)]

    bundle = jax.ShapeDtypeStruct((BUNDLE,) + tile, f32)
    pulled, to_low, to_high = kernel_call(
        functools.partial(pull_zy, directions),
        [jax.ShapeDtypeStruct(adjoint.shape, bf16), bundle, bundle],
        [
            pltpu.VMEM((2, 2) + tile, f32),
            pltpu.VMEM((2, 192, 128), f32),
            pltpu.VMEM(tile, f32),
        ],
    )(adjoint, forward, kind, sent_z, received_z, *received_y)
    low = lax.ppermute(to_high, "gx", [(i, i + 1) for i in range(count_x - 1)])
    high = lax.ppermute(to_low, "gx", [(i + 1, i) for i in range(count_x - 1)])

    gradient, fields = kernel_call(
        collide_back,
        [
            jax.ShapeDtypeStruct((2, 4, 8, 32), f32),
            jax.ShapeDtypeStruct((4,) + kind.shape, f32),
        ],
        [
            pltpu.VMEM((32, 128), f32),
            pltpu.VMEM((32, 256), f32),
            pltpu.VMEM((12,) + tile, f32),
            pltpu.VMEM((10,) + tile, f32),
        ],
    )(pulled, forward, kind, to_low, low, high, *bases())

    whole = gradient[0] + lax.ppermute(gradient[1], "gz", swap)
    if directions == 1:
        other = lax.ppermute(jnp.where(side == 0, whole[3], whole[0]), "gy", swap)
        from_low = jnp.where(side == 1, other, 0.0)
        from_high = jnp.where(side == 0, other, 0.0)
    else:
        from_low = lax.ppermute(whole[3], "gy", up)
        from_high = lax.ppermute(whole[0], "gy", down)
    prior = kernel_call(write_prior, jax.ShapeDtypeStruct(adjoint.shape, bf16))(
        pulled, kind, low, high, fields
    )
    return prior, jnp.stack([whole[1] + from_low, whole[2] + from_high], axis=1)


def solution(mesh):
    in_specs = (
        P(None, ("parts", "gx"), "gy", "gz"),
        P(None, ("parts", "gx"), "gy", "gz"),
        P(("parts", "gx"), "gy", "gz"),
        P(("parts", "gx"), "gy", "gz"),
    )
    out_specs = (P(None, ("parts", "gx"), "gy", "gz"), P(("parts", "gx"), "gy", "gz"))
    return jax.shard_map(
        per_device, mesh=mesh, in_specs=in_specs, out_specs=out_specs, check_vma=False
    )
```

```python
import functools

import jax
import jax.numpy as jnp
import numpy as np
from jax import lax
from jax.experimental import pallas as pl
from jax.experimental.pallas import tpu as pltpu
from jax.sharding import PartitionSpec as P

VELOCITY = (
    (0, 0, 0),
    (1, 0, 0),
    (-1, 0, 0),
    (0, 1, 0),
    (0, -1, 0),
    (0, 0, 1),
    (0, 0, -1),
    (1, 1, 0),
    (-1, -1, 0),
    (1, -1, 0),
    (-1, 1, 0),
    (1, 0, 1),
    (-1, 0, -1),
    (1, 0, -1),
    (-1, 0, 1),
    (0, 1, 1),
    (0, -1, -1),
    (0, 1, -1),
    (0, -1, 1),
)
OPPOSITE = (0, 2, 1, 4, 3, 6, 5, 8, 7, 10, 9, 12, 11, 14, 13, 16, 15, 18, 17)
highest = lax.Precision.HIGHEST
f32 = jnp.float32
bf16 = jnp.bfloat16


def going(dimension, sign):
    return [q for q in range(19) if VELOCITY[q][dimension] == sign]


XP, XM = going(0, 1), going(0, -1)
YP, YM = going(1, 1), going(1, -1)
ZP, ZM = going(2, 1), going(2, -1)

FACE, ALPHA, BETA, FIELD, LEVEL, BUNDLE = 0, 5, 9, 13, 17, 19
COARSE_ROWS, STRIP = 160, 192
MASS, INVERSE = 3, 4
EDGE_PLANES = (0, 1, 2, 3, 28, 29, 30, 31)


def spline(distance):
    radius = np.abs(distance) / 6.0
    return np.where(radius < 1.0, (1.0 - radius) ** 4 * (1.0 + 4.0 * radius), 0.0)


def kernel_call(body, out_shape, scratch_shapes=(), aliases=None, **specs):
    return pl.pallas_call(
        body,
        out_shape=out_shape,
        scratch_shapes=list(scratch_shapes),
        compiler_params=pltpu.CompilerParams(vmem_limit_bytes=12 * 1024 * 1024),
        input_output_aliases=aliases or {},
        **specs,
    )


def iota(dimension):
    return lax.broadcasted_iota(jnp.int32, (8, 128), dimension)


def pulled_z(q, tile, x, columns):
    step = VELOCITY[q][2]
    if step == 0:
        return tile
    slot = (ZP if step > 0 else ZM).index(q) * 32
    group, lane = slot // 128, slot % 128
    lanes = iota(1)
    edge = columns[0 if step > 0 else 1, group]
    if step > 0:
        edge = pltpu.roll(edge, 127 - lane - x, 1)
        return jnp.where(lanes == 127, edge, pltpu.roll(tile, 127, 1))
    edge = pltpu.roll(edge, (128 - lane - x) & 127, 1)
    return jnp.where(lanes == 0, edge, pltpu.roll(tile, 1, 1))


def load_columns(core, received, columns):
    for group in range(2):
        tile = received[group]
        columns[0, group] = jnp.where(core == 0, tile, 0.0)
        columns[1, group] = jnp.where(core == 1, tile, 0.0)


def pair_moments(populations):
    sums, diffs = {}, {}
    for q in range(1, 19, 2):
        a, b = populations.get(q), populations.get(q + 1)
        if a is None and b is None:
            continue
        if b is None:
            sums[q], diffs[q] = a, a
        elif a is None:
            sums[q], diffs[q] = b, -b
        else:
            sums[q], diffs[q] = a + b, a - b

    def total(terms):
        value = None
        for sign, table, q in terms:
            if q not in table:
                continue
            item = table[q]
            if value is None:
                value = item if sign > 0 else -item
            else:
                value = value + item if sign > 0 else value - item
        return value

    def plus(a, b):
        return b if a is None else (a if b is None else a + b)

    def twice(a):
        return None if a is None else a + a

    xx = total([(1, sums, 7), (1, sums, 9), (1, sums, 11), (1, sums, 13)])
    edge_yz = total([(1, sums, 15), (1, sums, 17)])
    edge_xy = total([(1, sums, 7), (1, sums, 9)])
    edge_xz = total([(1, sums, 11), (1, sums, 13)])
    sx, sy, sz = (twice(sums.get(q)) for q in (1, 3, 5))
    zeroth = plus(plus(xx, edge_yz), plus(plus(sx, sy), sz))
    if 0 in populations:
        zeroth = zeroth + 12.0 * populations[0]
    mx = plus(twice(diffs.get(1)), total([(1, diffs, 7), (1, diffs, 9), (1, diffs, 11), (1, diffs, 13)]))
    my = plus(twice(diffs.get(3)), total([(1, diffs, 7), (-1, diffs, 9), (1, diffs, 15), (1, diffs, 17)]))
    mz = plus(twice(diffs.get(5)), total([(1, diffs, 11), (-1, diffs, 13), (1, diffs, 15), (-1, diffs, 17)]))
    mxx = plus(sx, xx)
    myy = plus(sy, plus(edge_xy, edge_yz))
    mzz = plus(sz, plus(edge_xz, edge_yz))
    mxy = total([(1, sums, 7), (-1, sums, 9)])
    mxz = total([(1, sums, 11), (-1, sums, 13)])
    myz = total([(1, sums, 15), (-1, sums, 17)])
    return zeroth, (mx, my, mz), (mxx, myy, mzz, mxy, mxz, myz)


def flow_moments(populations):
    sums = {q: populations[q] + populations[q + 1] for q in range(1, 19, 2)}
    diffs = {q: populations[q] - populations[q + 1] for q in range(1, 19, 2)}
    rho = populations[0]
    for q in range(1, 19, 2):
        rho = rho + sums[q]
    jx = (diffs[1] + diffs[7]) + (diffs[9] + diffs[11]) + diffs[13]
    jy = (diffs[3] + diffs[7]) + (diffs[15] - diffs[9]) + diffs[17]
    jz = (diffs[5] + diffs[11]) + (diffs[15] - diffs[13]) - diffs[17]
    return rho, (jx, jy, jz)


def dot3(a, b):
    return a[0] * b[0] + a[1] * b[1] + a[2] * b[2]


def second_times(second, v):
    mxx, myy, mzz, mxy, mxz, myz = second

    def row(terms):
        value = None
        for coefficient, component in terms:
            if coefficient is None:
                continue
            product = coefficient * component
            value = product if value is None else value + product
        return value

    return (
        row([(mxx, v[0]), (mxy, v[1]), (mxz, v[2])]),
        row([(mxy, v[0]), (myy, v[1]), (myz, v[2])]),
        row([(mxz, v[0]), (myz, v[1]), (mzz, v[2])]),
    )


def alpha_beta(moments, flow, flow_mass):
    zeroth, first, second = moments
    scale = flow_mass * (-1.6 / 36.0)
    alpha = scale * 3.0 * dot3(first, flow)
    beta = scale * (9.0 * dot3(second_times(second, flow), flow) - 3.0 * zeroth * dot3(flow, flow))
    return alpha, beta


def rows_of(x):
    return pl.ds(pl.multiple_of(x * 8, 8), 8) if not isinstance(x, int) else slice(x * 8, x * 8 + 8)


def pack_z(adjoint, coefficients, out, faces, coarse, semaphores):
    core = lax.axis_index("gz")
    copies = [pltpu.make_async_copy(coefficients, coarse, semaphores.at[5])]
    for k in range(5):
        q = ZM[k] + core * (ZP[k] - ZM[k])
        copies.append(pltpu.make_async_copy(adjoint.at[q], faces.at[k], semaphores.at[k]))
    for copy in copies:
        copy.start()
    lanes = iota(1)
    count = coefficients.shape[2]
    out[2] = jnp.zeros((8, 128), f32)
    out[3] = jnp.zeros((8, 128), f32)
    for copy in copies:
        copy.wait()
    for which, source in enumerate((127, 0)):

        @pl.when(core == which)
        def _():
            for j in range(2):
                out[2 + j, :, count * which : count * which + count] = coarse[:, j, :]
            chains = {}
            for k in range(5):
                for x in range(32):
                    group, lane = divmod(k * 32 + x, 128)
                    column = pltpu.roll(faces[k, x].astype(f32), (lane - source) % 128, 1)
                    chain = group, lane // 16
                    if chain in chains:
                        column = jnp.where(lanes >= lane, column, chains[chain])
                    chains[chain] = column
            for group in range(2):
                tile = chains[group, 0]
                for part in range(1, 8 if group == 0 else 2):
                    tile = jnp.where(lanes >= part * 16, chains[group, part], tile)
                out[group] = tile


def y_sides(directions):
    return ((YM, 7), (YP, 0))


def gather_rows(directions, adjoint, *refs):
    outs, plane = refs[:-1], refs[-1]
    lanes = lax.broadcasted_iota(jnp.int32, (32, 128), 1)

    def emit(components, row, out):
        for k, q in enumerate(components):
            for x in range(32):
                plane[x * 8 : x * 8 + 8, :] = adjoint[q, x].astype(f32)
            rows = plane[pl.ds(row, 32, stride=8), :]
            step = VELOCITY[q][2]
            if step > 0:
                rows = jnp.where(lanes == 127, 0.0, pltpu.roll(rows, 127, 1))
            elif step < 0:
                rows = jnp.where(lanes == 0, 0.0, pltpu.roll(rows, 1, 1))
            out[k * 32 : k * 32 + 32, :] = rows

    sides = y_sides(directions)
    if directions == 1:
        side = lax.axis_index("gy")
        for n in range(2):
            pl.when(side == n)(functools.partial(emit, *sides[n], outs[0]))
    else:
        for n in range(2):
            emit(*sides[n], outs[n])


def pack_y(directions, sent, received, *refs):
    sources, outs = refs[:directions], refs[directions:]
    core = lax.axis_index("gz")
    lanes = lax.broadcasted_iota(jnp.int32, (32, 128), 1)
    sublanes = lax.broadcasted_iota(jnp.int32, (32, 128), 0)

    def emit(components, row, coarse_row, source, out):
        for k, q in enumerate(components):
            rows = source[k * 32 : k * 32 + 32, :]
            step = VELOCITY[q][2]
            if step:
                slot = (ZP if step > 0 else ZM).index(q) * 32
                group, lane = slot // 128, slot % 128
                spread = jnp.broadcast_to(received[group, row : row + 1, :], (32, 128))
                column = jnp.sum(jnp.where(lanes == sublanes + lane, spread, 0.0), axis=1, keepdims=True)
                column = jnp.where(core == (0 if step > 0 else 1), column, 0.0)
                rows = rows + jnp.where(lanes == (127 if step > 0 else 0), column, 0.0)
            out[k * 32 : k * 32 + 32, :] = rows.astype(bf16)
        coarse = sent[coarse_row] + received[coarse_row]
        high = coarse.astype(bf16)
        rest = coarse - high.astype(f32)
        middle = rest.astype(bf16)
        low = (rest - middle.astype(f32)).astype(bf16)
        out[COARSE_ROWS : COARSE_ROWS + 16, :] = jnp.concatenate([high, middle], axis=0)
        out[COARSE_ROWS + 16 : STRIP, :] = jnp.concatenate([low, jnp.zeros((8, 128), bf16)], axis=0)

    sides = y_sides(directions)
    if directions == 1:
        side = lax.axis_index("gy")
        for n in range(2):
            pl.when(side == n)(functools.partial(emit, *sides[n], 3 - n, sources[0], outs[0]))
    else:
        for n in range(2):
            emit(*sides[n], 3 - n, sources[n], outs[n])


def pull_zy(adjoint, forward, kind, sent, received, basis_z, pulled, flows, lines, columns):
    core = lax.axis_index("gz")
    load_columns(core, received, columns)
    sublanes = iota(0)
    coarse = jnp.concatenate([sent[2] + received[2], sent[3] + received[3]], axis=0)
    lines[...] = jnp.dot(coarse, basis_z[core], precision=highest, preferred_element_type=f32)

    def step(x, carry):
        for q in range(19):
            tile = pulled_z(q, adjoint[q, x].astype(f32), x, columns)
            step_y = VELOCITY[q][1]
            if step_y > 0:
                tile = jnp.where(sublanes == 7, 0.0, pltpu.roll(tile, 7, 0))
            elif step_y < 0:
                tile = jnp.where(sublanes == 0, 0.0, pltpu.roll(tile, 1, 0))
            pulled[q, rows_of(x), :] = tile
        rho, mass = flow_moments([forward[q, x].astype(f32) for q in range(19)])
        inverse = 1.0 / rho
        for n in range(3):
            flows[n, x] = mass[n] * inverse
        flows[MASS, x] = jnp.where(kind[x] == 0, rho, 0.0)
        flows[INVERSE, x] = inverse
        return carry

    lax.fori_loop(0, 32, step, 0, unroll=4)


def pack_x(directions, unpatched, flows, lines, basis_z, basis_y, *refs):
    received = refs[:directions]
    pulled, out_a, out_b, edges, levels, extra = refs[directions:]
    del unpatched
    core = lax.axis_index("gz")
    side = lax.axis_index("gy")
    even = lax.rem(lax.axis_index("gx"), 2) == 0

    def patch(components, row, strip):
        for k, q in enumerate(components):
            pulled[q, pl.ds(row, 32, stride=8), :] = strip[k * 32 : k * 32 + 32, :].astype(f32)

    def outer_line(strip):
        parts = strip[COARSE_ROWS:STRIP, :].astype(f32)
        coarse = parts[0:8] + parts[8:16] + parts[16:24]
        return jnp.dot(coarse, basis_z[core], precision=highest, preferred_element_type=f32)

    if directions == 1:
        pl.when(side == 0)(lambda: patch(YP, 7, received[0]))
        pl.when(side == 1)(lambda: patch(YM, 0, received[0]))
        outer = [(outer_line(received[0]), basis_y[3 - 3 * side])]
    else:
        patch(YM, 0, received[0])
        patch(YP, 7, received[1])
        outer = [(outer_line(received[0]), basis_y[0]), (outer_line(received[1]), basis_y[3])]
    terms = [(lines[0:8, :], basis_y[1]), (lines[8:16, :], basis_y[2])] + outer
    for n, (line, _) in enumerate(terms):
        extra[n * 8 : n * 8 + 8, :] = line
    for i in range(8):
        level = None
        for n, (_, weight) in enumerate(terms):
            term = weight * jnp.broadcast_to(extra[n * 8 + i : n * 8 + i + 1, :], (8, 128))
            level = term if level is None else level + term
        levels[i] = level

    def put(slot, low, high):
        out_a[slot] = jnp.where(even, high, low)
        out_b[slot] = jnp.where(even, low, high)

    for k in range(5):
        put(FACE + k, pulled[XP[k], rows_of(0), :], pulled[XM[k], rows_of(31), :])
    for n in range(4):
        put(FIELD + n, flows[n, 0], flows[n, 31])
    for n in range(2):
        put(LEVEL + n, levels[n], levels[6 + n])
    results = []
    for x in EDGE_PLANES:
        values = {}
        for q in range(19):
            target = x + VELOCITY[q][0]
            if 0 <= target < 32:
                values[q] = pulled[q, rows_of(target), :]
        flow = tuple(flows[n, x] for n in range(3))
        results.append(alpha_beta(pair_moments(values), flow, flows[MASS, x]))
    for position in range(4):
        for n, slot in enumerate((ALPHA, BETA)):
            low, high = results[position][n], results[4 + position][n]
            edges[n, position] = low
            edges[n, 4 + position] = high
            put(slot + position, low, high)


def slope_of(bent):
    return -1.8 * (1.0 - bent * bent)


def bent_level(around, position):
    value = None
    for shift, level in zip((-1, 0, 1), around):
        term = float(spline(position - 4.0 * shift - 1.5)) * level
        value = term if value is None else value + term
    return jnp.tanh(4.0 * value)


def weight_of(position, shift):
    return float(spline(position - 4.0 * shift - 1.5))


def prior_fields(bent, here, flow, inverse, moments):
    zeroth, first, second = moments
    fluid = here == 0
    retained = 0.55 + 0.45 * bent
    share = jnp.where(fluid, retained, 1.0)
    speed = tuple(share * component for component in flow)
    curved = second_times(second, speed)
    slopes = tuple(3.0 * first[n] + 9.0 * curved[n] - 3.0 * zeroth * speed[n] for n in range(3))
    along = dot3(slopes, flow)
    value = zeroth + 0.5 * (3.0 * dot3(first, speed) + dot3(slopes, speed))
    factor = jnp.where(
        fluid, (1.6 / 36.0) * retained, jnp.where(here == 3, inverse * (1.0 / 36.0), 0.0)
    )
    base = jnp.where(fluid, (1.6 / 36.0) * value, 0.0) - factor * along
    return (base,) + tuple(factor * slope for slope in slopes), along


def emit_prior(stage, slot, here, values, result):
    solid = here == 1
    keep = jnp.where(here == 0, -0.6, 0.0)
    base, bx, by, bz = result
    shifts = {}
    for step_x in (-1, 0, 1):
        row = base if step_x == 0 else (base + bx if step_x > 0 else base - bx)
        for step_y in (-1, 0, 1):
            both = row if step_y == 0 else (row + by if step_y > 0 else row - by)
            shifts[step_x, step_y] = both
    for q in range(19):
        step_x, step_y, step_z = VELOCITY[q]
        shift = shifts[step_x, step_y]
        if step_z:
            shift = shift + bz if step_z > 0 else shift - bz
        kept = jnp.where(solid, values[OPPOSITE[q]], keep * values[q])
        stage[q, slot] = (kept + shift).astype(bf16)


def collide_inside(pulled, flows, kind, levels, out, totals, stage, semaphores):
    totals[...] = jnp.zeros((8, 8, 128), f32)

    def middle(block, carry):
        around = [levels[block - 1], levels[block], levels[block + 1]]
        sums = [None] * 3
        for position in range(4):
            x = block * 4 + position
            bent = bent_level(around, position)
            flow = tuple(flows[n, x] for n in range(3))
            values = {q: pulled[q, rows_of(x + VELOCITY[q][0]), :] for q in range(19)}
            result, along = prior_fields(bent, kind[x], flow, flows[INVERSE, x], pair_moments(values))
            emit_prior(stage, x - 4, kind[x], values, result)
            sensitivity = (-1.6 / 36.0) * flows[MASS, x] * along * slope_of(bent)
            for n in range(3):
                term = weight_of(position, n - 1) * sensitivity
                sums[n] = term if sums[n] is None else sums[n] + term
        for n in range(3):
            totals[block + n - 1] += sums[n]
        return carry

    copies = []
    for part in range(3):
        lax.fori_loop(1 + 2 * part, 3 + 2 * part, middle, 0)
        copies.append(
            pltpu.make_async_copy(
                stage.at[:, pl.ds(8 * part, 8)], out.at[:, pl.ds(4 + 8 * part, 8)], semaphores.at[part]
            )
        )
        copies[part].start()
    for copy in copies:
        copy.wait()


def along_x(received_a, received_b):
    even = lax.rem(lax.axis_index("gx"), 2) == 0

    def low(slot):
        return jnp.where(even, received_b[slot], received_a[slot])

    def high(slot):
        return jnp.where(even, received_a[slot], received_b[slot])

    return low, high


def project(pulled, flows, edges, levels, received_a, received_b, inner, fold_y, fold_z, gradient):
    core = lax.axis_index("gz")
    low, high = along_x(received_a, received_b)
    totals = [inner[i] for i in range(8)]
    lower = [low(LEVEL), low(LEVEL + 1)] + [levels[i] for i in range(3)]
    upper = [levels[i] for i in range(5, 8)] + [high(LEVEL), high(LEVEL + 1)]

    def add(block, position, alpha, beta):
        start = block + 1 if block < 4 else block - 6
        around = (lower if block < 4 else upper)[start : start + 3]
        bent = bent_level(around, position)
        sensitivity = (alpha + (0.55 + 0.45 * bent) * beta) * slope_of(bent)
        for shift in (-1, 0, 1):
            if 0 <= block + shift < 8:
                totals[block + shift] = totals[block + shift] + weight_of(position, shift) * sensitivity

    def faces(ref, components):
        return pair_moments({q: ref(FACE + k) for k, q in enumerate(components)})

    def own(x, components):
        return pair_moments({q: pulled[q, rows_of(x), :] for q in components})

    def flow_at(x):
        return tuple(flows[n, x] for n in range(3))

    missing = {
        (0, 0): alpha_beta(faces(low, XM), flow_at(0), flows[MASS, 0]),
        (7, 3): alpha_beta(faces(high, XP), flow_at(31), flows[MASS, 31]),
        (-1, 3): alpha_beta(own(0, XP), tuple(low(FIELD + n) for n in range(3)), low(FIELD + 3)),
        (8, 0): alpha_beta(own(31, XM), tuple(high(FIELD + n) for n in range(3)), high(FIELD + 3)),
    }
    for block in (-1, 0, 7, 8):
        for position in range(4):
            if block in (0, 7):
                index = position + (4 if block else 0)
                alpha, beta = edges[0, index], edges[1, index]
            else:
                ref = low if block < 0 else high
                alpha, beta = ref(ALPHA + position), ref(BETA + position)
            if (block, position) in missing:
                more = missing[block, position]
                alpha, beta = alpha + more[0], beta + more[1]
            add(block, position, alpha, beta)
    stacked = jnp.concatenate(totals, axis=0)
    folded = jnp.dot(fold_y[...], stacked, precision=highest, preferred_element_type=f32)
    result = jnp.dot(folded, fold_z[core], precision=highest, preferred_element_type=f32)
    for part in range(2):
        for j in range(4):
            gradient[part, j] = result[j * 8 : j * 8 + 8, part * 32 : part * 32 + 32]


def collide_outside(pulled, flows, kind, levels, received_a, received_b, inner, out, stage, semaphores):
    del inner
    low, high = along_x(received_a, received_b)
    copies = []
    for part, planes in enumerate((EDGE_PLANES[:4], EDGE_PLANES[4:])):
        for slot, x in enumerate(planes):
            values = {}
            for q in range(19):
                target = x + VELOCITY[q][0]
                if target < 0:
                    values[q] = low(FACE + XM.index(q))
                elif target > 31:
                    values[q] = high(FACE + XP.index(q))
                else:
                    values[q] = pulled[q, rows_of(target), :]
            around = (
                [levels[6], levels[7], high(LEVEL)] if part else [low(LEVEL + 1), levels[0], levels[1]]
            )
            flow = tuple(flows[n, x] for n in range(3))
            result, _ = prior_fields(
                bent_level(around, slot), kind[x], flow, flows[INVERSE, x], pair_moments(values)
            )
            emit_prior(stage, 4 * part + slot, kind[x], values, result)
        copies.append(
            pltpu.make_async_copy(
                stage.at[:, pl.ds(4 * part, 4)], out.at[:, pl.ds(28 * part, 4)], semaphores.at[part]
            )
        )
        copies[part].start()
    for copy in copies:
        copy.wait()


def bases():
    fine = np.arange(128.0)
    basis_z = np.zeros((2, 128, 128))
    fold_z = np.zeros((2, 128, 64))
    for core in range(2):
        full = spline(fine[None, :] + 128 * core - 4.0 * np.arange(64)[:, None] - 1.5)
        basis_z[core, 0:64] = full
        fold_z[core, :, 0:32] = full[32 * core : 32 * core + 32].T
        fold_z[core, :, 32:64] = full[32 * (1 - core) : 32 * (1 - core) + 32].T
    across = spline(np.arange(8.0)[None, :] - 4.0 * np.arange(-1, 3)[:, None] - 1.5)
    basis_y = np.broadcast_to(across[:, :, None], (4, 8, 128))
    fold_y = np.zeros((4, 8, 8, 8))
    for i in range(8):
        fold_y[:, i, i, :] = across
    return [
        jnp.asarray(np.ascontiguousarray(a), f32)
        for a in (basis_z, basis_y, fold_y.reshape(32, 64), fold_z)
    ]


def pairs(count, first):
    result = []
    for i in range(first, count - 1, 2):
        result += [(i, i + 1), (i + 1, i)]
    return result


def per_device(forward, adjoint, coefficients, kind):
    count_y = lax.axis_size("gy")
    count_x = lax.axis_size("gx")
    swap = [(0, 1), (1, 0)]
    side = lax.axis_index("gy")
    directions = 1 if count_y == 2 else 2
    tile = (8, 128)
    shape = jax.ShapeDtypeStruct
    basis_z, basis_y, fold_y, fold_z = bases()
    up = [(i, i + 1) for i in range(count_y - 1)]
    down = [(i + 1, i) for i in range(count_y - 1)]

    sent_z = kernel_call(
        pack_z,
        shape((4,) + tile, f32),
        [
            pltpu.VMEM((5,) + adjoint.shape[1:], bf16),
            pltpu.VMEM(coefficients.shape, f32),
            pltpu.SemaphoreType.DMA((6,)),
        ],
        in_specs=[pl.BlockSpec(memory_space=pltpu.HBM)] * 2,
    )(*(pltpu.with_memory_space_constraint(a, pltpu.HBM) for a in (adjoint, coefficients)))
    received_z = lax.ppermute(sent_z, "gz", swap)
    rows = kernel_call(
        functools.partial(gather_rows, directions),
        [shape((COARSE_ROWS, 128), f32)] * directions,
        [pltpu.VMEM((256, 128), f32)],
    )(adjoint)
    sent_y = kernel_call(
        functools.partial(pack_y, directions), [shape((STRIP, 128), bf16)] * directions
    )(sent_z, received_z, *rows)
    if directions == 1:
        received_y = [lax.ppermute(sent_y[0], "gy", swap)]
    else:
        received_y = [lax.ppermute(sent_y[0], "gy", up), lax.ppermute(sent_y[1], "gy", down)]

    pulled, flows, lines = kernel_call(
        pull_zy,
        [shape((19, 256, 128), f32), shape((5,) + kind.shape, f32), shape((16, 128), f32)],
        [pltpu.VMEM((2, 2) + tile, f32)],
    )(adjoint, forward, kind, sent_z, received_z, basis_z)

    bundle = shape((BUNDLE,) + tile, f32)
    pulled, sent_a, sent_b, edges, levels = kernel_call(
        functools.partial(pack_x, directions),
        [pulled, bundle, bundle, shape((2, 8) + tile, f32), shape((8,) + tile, f32)],
        [pltpu.VMEM((32, 128), f32)],
        aliases={0: 0},
    )(pulled, flows, lines, basis_z, basis_y, *received_y)
    received_b = lax.ppermute(sent_b, "gx", pairs(count_x, 1))
    received_a = lax.ppermute(sent_a, "gx", pairs(count_x, 0))

    prior, totals = kernel_call(
        collide_inside,
        [shape(adjoint.shape, bf16), shape((8,) + tile, f32)],
        [pltpu.VMEM((19, 24) + tile, bf16), pltpu.SemaphoreType.DMA((3,))],
        out_specs=[pl.BlockSpec(memory_space=pltpu.HBM), pl.BlockSpec(memory_space=pltpu.VMEM)],
    )(pulled, flows, kind, levels)
    gradient = kernel_call(project, shape((2, 4, 8, 32), f32))(
        pulled, flows, edges, levels, received_a, received_b, totals, fold_y, fold_z
    )

    whole = gradient[0] + lax.ppermute(gradient[1], "gz", swap)
    if directions == 1:
        other = lax.ppermute(jnp.where(side == 0, whole[3], whole[0]), "gy", swap)
        from_low = jnp.where(side == 1, other, 0.0)
        from_high = jnp.where(side == 0, other, 0.0)
    else:
        from_low = lax.ppermute(whole[3], "gy", up)
        from_high = lax.ppermute(whole[0], "gy", down)
    in_hbm = pl.BlockSpec(memory_space=pltpu.HBM)
    prior = kernel_call(
        collide_outside,
        shape(adjoint.shape, bf16),
        [pltpu.VMEM((19, 8) + tile, bf16), pltpu.SemaphoreType.DMA((2,))],
        aliases={6: 0},
        in_specs=[pl.BlockSpec(memory_space=pltpu.VMEM)] * 6 + [in_hbm],
        out_specs=in_hbm,
    )(pulled, flows, kind, levels, received_a, received_b, prior)
    return prior, jnp.stack([whole[1] + from_low, whole[2] + from_high], axis=1)


def solution(mesh):
    in_specs = (
        P(None, ("parts", "gx"), "gy", "gz"),
        P(None, ("parts", "gx"), "gy", "gz"),
        P(("parts", "gx"), "gy", "gz"),
        P(("parts", "gx"), "gy", "gz"),
    )
    out_specs = (P(None, ("parts", "gx"), "gy", "gz"), P(("parts", "gx"), "gy", "gz"))
    return jax.shard_map(
        per_device, mesh=mesh, in_specs=in_specs, out_specs=out_specs, check_vma=False
    )
```

```python
import functools

import jax
import jax.numpy as jnp
import numpy as np
from jax import lax
from jax.experimental import pallas as pl
from jax.experimental.pallas import tpu as pltpu
from jax.sharding import PartitionSpec as P

VELOCITY = (
    (0, 0, 0),
    (1, 0, 0),
    (-1, 0, 0),
    (0, 1, 0),
    (0, -1, 0),
    (0, 0, 1),
    (0, 0, -1),
    (1, 1, 0),
    (-1, -1, 0),
    (1, -1, 0),
    (-1, 1, 0),
    (1, 0, 1),
    (-1, 0, -1),
    (1, 0, -1),
    (-1, 0, 1),
    (0, 1, 1),
    (0, -1, -1),
    (0, 1, -1),
    (0, -1, 1),
)
OPPOSITE = (0, 2, 1, 4, 3, 6, 5, 8, 7, 10, 9, 12, 11, 14, 13, 16, 15, 18, 17)
highest = lax.Precision.HIGHEST
f32 = jnp.float32
bf16 = jnp.bfloat16


def going(dimension, sign):
    return [q for q in range(19) if VELOCITY[q][dimension] == sign]


XP, XM = going(0, 1), going(0, -1)
YP, YM = going(1, 1), going(1, -1)
ZP, ZM = going(2, 1), going(2, -1)

FACE, ALPHA, BETA, FIELD, LEVEL, BUNDLE = 0, 5, 9, 13, 17, 19
COARSE_ROWS, STRIP = 160, 192
MASS, INVERSE = 3, 4
EDGE_PLANES = (0, 1, 2, 3, 28, 29, 30, 31)


def spline(distance):
    radius = np.abs(distance) / 6.0
    return np.where(radius < 1.0, (1.0 - radius) ** 4 * (1.0 + 4.0 * radius), 0.0)


def kernel_call(body, out_shape, scratch_shapes=(), aliases=None, **specs):
    return pl.pallas_call(
        body,
        out_shape=out_shape,
        scratch_shapes=list(scratch_shapes),
        compiler_params=pltpu.CompilerParams(vmem_limit_bytes=12 * 1024 * 1024),
        input_output_aliases=aliases or {},
        **specs,
    )


def iota(dimension):
    return lax.broadcasted_iota(jnp.int32, (8, 128), dimension)


def pulled_z(q, tile, x, columns):
    step = VELOCITY[q][2]
    if step == 0:
        return tile
    slot = (ZP if step > 0 else ZM).index(q) * 32
    group, lane = slot // 128, slot % 128
    lanes = iota(1)
    edge = columns[0 if step > 0 else 1, group]
    if step > 0:
        edge = pltpu.roll(edge, 127 - lane - x, 1)
        return jnp.where(lanes == 127, edge, pltpu.roll(tile, 127, 1))
    edge = pltpu.roll(edge, (128 - lane - x) & 127, 1)
    return jnp.where(lanes == 0, edge, pltpu.roll(tile, 1, 1))


def load_columns(core, received, columns):
    for group in range(2):
        tile = received[group]
        columns[0, group] = jnp.where(core == 0, tile, 0.0)
        columns[1, group] = jnp.where(core == 1, tile, 0.0)


def pair_moments(populations):
    sums, diffs = {}, {}
    for q in range(1, 19, 2):
        a, b = populations.get(q), populations.get(q + 1)
        if a is None and b is None:
            continue
        if b is None:
            sums[q], diffs[q] = a, a
        elif a is None:
            sums[q], diffs[q] = b, -b
        else:
            sums[q], diffs[q] = a + b, a - b

    def total(terms):
        value = None
        for sign, table, q in terms:
            if q not in table:
                continue
            item = table[q]
            if value is None:
                value = item if sign > 0 else -item
            else:
                value = value + item if sign > 0 else value - item
        return value

    def plus(a, b):
        return b if a is None else (a if b is None else a + b)

    def twice(a):
        return None if a is None else a + a

    xx = total([(1, sums, 7), (1, sums, 9), (1, sums, 11), (1, sums, 13)])
    edge_yz = total([(1, sums, 15), (1, sums, 17)])
    edge_xy = total([(1, sums, 7), (1, sums, 9)])
    edge_xz = total([(1, sums, 11), (1, sums, 13)])
    sx, sy, sz = (twice(sums.get(q)) for q in (1, 3, 5))
    zeroth = plus(plus(xx, edge_yz), plus(plus(sx, sy), sz))
    if 0 in populations:
        zeroth = zeroth + 12.0 * populations[0]
    mx = plus(twice(diffs.get(1)), total([(1, diffs, 7), (1, diffs, 9), (1, diffs, 11), (1, diffs, 13)]))
    my = plus(twice(diffs.get(3)), total([(1, diffs, 7), (-1, diffs, 9), (1, diffs, 15), (1, diffs, 17)]))
    mz = plus(twice(diffs.get(5)), total([(1, diffs, 11), (-1, diffs, 13), (1, diffs, 15), (-1, diffs, 17)]))
    mxx = plus(sx, xx)
    myy = plus(sy, plus(edge_xy, edge_yz))
    mzz = plus(sz, plus(edge_xz, edge_yz))
    mxy = total([(1, sums, 7), (-1, sums, 9)])
    mxz = total([(1, sums, 11), (-1, sums, 13)])
    myz = total([(1, sums, 15), (-1, sums, 17)])
    return zeroth, (mx, my, mz), (mxx, myy, mzz, mxy, mxz, myz)


def flow_moments(populations):
    sums = {q: populations[q] + populations[q + 1] for q in range(1, 19, 2)}
    diffs = {q: populations[q] - populations[q + 1] for q in range(1, 19, 2)}
    rho = populations[0]
    for q in range(1, 19, 2):
        rho = rho + sums[q]
    jx = (diffs[1] + diffs[7]) + (diffs[9] + diffs[11]) + diffs[13]
    jy = (diffs[3] + diffs[7]) + (diffs[15] - diffs[9]) + diffs[17]
    jz = (diffs[5] + diffs[11]) + (diffs[15] - diffs[13]) - diffs[17]
    return rho, (jx, jy, jz)


def dot3(a, b):
    return a[0] * b[0] + a[1] * b[1] + a[2] * b[2]


def second_times(second, v):
    mxx, myy, mzz, mxy, mxz, myz = second

    def row(terms):
        value = None
        for coefficient, component in terms:
            if coefficient is None:
                continue
            product = coefficient * component
            value = product if value is None else value + product
        return value

    return (
        row([(mxx, v[0]), (mxy, v[1]), (mxz, v[2])]),
        row([(mxy, v[0]), (myy, v[1]), (myz, v[2])]),
        row([(mxz, v[0]), (myz, v[1]), (mzz, v[2])]),
    )


def alpha_beta(moments, flow, flow_mass):
    zeroth, first, second = moments
    scale = flow_mass * (-1.6 / 36.0)
    alpha = scale * 3.0 * dot3(first, flow)
    beta = scale * (9.0 * dot3(second_times(second, flow), flow) - 3.0 * zeroth * dot3(flow, flow))
    return alpha, beta


def rows_of(x):
    return pl.ds(pl.multiple_of(x * 8, 8), 8) if not isinstance(x, int) else slice(x * 8, x * 8 + 8)


def pack_z(adjoint, coefficients, out, faces, coarse, semaphores):
    core = lax.axis_index("gz")
    copies = [pltpu.make_async_copy(coefficients, coarse, semaphores.at[5])]
    for k in range(5):
        q = ZM[k] + core * (ZP[k] - ZM[k])
        copies.append(pltpu.make_async_copy(adjoint.at[q], faces.at[k], semaphores.at[k]))
    for copy in copies:
        copy.start()
    lanes = iota(1)
    count = coefficients.shape[2]
    out[2] = jnp.zeros((8, 128), f32)
    out[3] = jnp.zeros((8, 128), f32)
    for copy in copies:
        copy.wait()
    for which, source in enumerate((127, 0)):

        @pl.when(core == which)
        def _():
            for j in range(2):
                out[2 + j, :, count * which : count * which + count] = coarse[:, j, :]
            chains = {}
            for k in range(5):
                for x in range(32):
                    group, lane = divmod(k * 32 + x, 128)
                    column = pltpu.roll(faces[k, x].astype(f32), (lane - source) % 128, 1)
                    chain = group, lane // 16
                    if chain in chains:
                        column = jnp.where(lanes >= lane, column, chains[chain])
                    chains[chain] = column
            for group in range(2):
                tile = chains[group, 0]
                for part in range(1, 8 if group == 0 else 2):
                    tile = jnp.where(lanes >= part * 16, chains[group, part], tile)
                out[group] = tile


def y_sides(directions):
    return ((YM, 7), (YP, 0))


def gather_rows(directions, adjoint, *refs):
    outs, plane = refs[:-1], refs[-1]
    lanes = lax.broadcasted_iota(jnp.int32, (32, 128), 1)

    def emit(components, row, out):
        for k, q in enumerate(components):
            for x in range(32):
                plane[x * 8 : x * 8 + 8, :] = adjoint[q, x].astype(f32)
            rows = plane[pl.ds(row, 32, stride=8), :]
            step = VELOCITY[q][2]
            if step > 0:
                rows = jnp.where(lanes == 127, 0.0, pltpu.roll(rows, 127, 1))
            elif step < 0:
                rows = jnp.where(lanes == 0, 0.0, pltpu.roll(rows, 1, 1))
            out[k * 32 : k * 32 + 32, :] = rows

    sides = y_sides(directions)
    if directions == 1:
        side = lax.axis_index("gy")
        for n in range(2):
            pl.when(side == n)(functools.partial(emit, *sides[n], outs[0]))
    else:
        for n in range(2):
            emit(*sides[n], outs[n])


def pack_y(directions, sent, received, *refs):
    sources, outs = refs[:directions], refs[directions:]
    core = lax.axis_index("gz")
    lanes = lax.broadcasted_iota(jnp.int32, (32, 128), 1)
    sublanes = lax.broadcasted_iota(jnp.int32, (32, 128), 0)

    def emit(components, row, coarse_row, source, out):
        for k, q in enumerate(components):
            rows = source[k * 32 : k * 32 + 32, :]
            step = VELOCITY[q][2]
            if step:
                slot = (ZP if step > 0 else ZM).index(q) * 32
                group, lane = slot // 128, slot % 128
                spread = jnp.broadcast_to(received[group, row : row + 1, :], (32, 128))
                column = jnp.sum(jnp.where(lanes == sublanes + lane, spread, 0.0), axis=1, keepdims=True)
                column = jnp.where(core == (0 if step > 0 else 1), column, 0.0)
                rows = rows + jnp.where(lanes == (127 if step > 0 else 0), column, 0.0)
            out[k * 32 : k * 32 + 32, :] = rows.astype(bf16)
        coarse = sent[coarse_row] + received[coarse_row]
        high = coarse.astype(bf16)
        rest = coarse - high.astype(f32)
        middle = rest.astype(bf16)
        low = (rest - middle.astype(f32)).astype(bf16)
        out[COARSE_ROWS : COARSE_ROWS + 16, :] = jnp.concatenate([high, middle], axis=0)
        out[COARSE_ROWS + 16 : STRIP, :] = jnp.concatenate([low, jnp.zeros((8, 128), bf16)], axis=0)

    sides = y_sides(directions)
    if directions == 1:
        side = lax.axis_index("gy")
        for n in range(2):
            pl.when(side == n)(functools.partial(emit, *sides[n], 3 - n, sources[0], outs[0]))
    else:
        for n in range(2):
            emit(*sides[n], 3 - n, sources[n], outs[n])


def pull_zy(adjoint, forward, kind, sent, received, basis_z, pulled, flows, lines, columns):
    core = lax.axis_index("gz")
    load_columns(core, received, columns)
    sublanes = iota(0)
    coarse = jnp.concatenate([sent[2] + received[2], sent[3] + received[3]], axis=0)
    lines[...] = jnp.dot(coarse, basis_z[core], precision=highest, preferred_element_type=f32)

    def step(x, carry):
        for q in range(19):
            tile = pulled_z(q, adjoint[q, x].astype(f32), x, columns)
            step_y = VELOCITY[q][1]
            if step_y > 0:
                tile = jnp.where(sublanes == 7, 0.0, pltpu.roll(tile, 7, 0))
            elif step_y < 0:
                tile = jnp.where(sublanes == 0, 0.0, pltpu.roll(tile, 1, 0))
            pulled[q, rows_of(x), :] = tile
        rho, mass = flow_moments([forward[q, x].astype(f32) for q in range(19)])
        inverse = 1.0 / rho
        for n in range(3):
            flows[n, x] = mass[n] * inverse
        flows[MASS, x] = jnp.where(kind[x] == 0, rho, 0.0)
        flows[INVERSE, x] = inverse
        return carry

    lax.fori_loop(0, 32, step, 0, unroll=4)


def pack_x(directions, unpatched, flows, lines, basis_z, basis_y, *refs):
    received = refs[:directions]
    pulled, out_a, out_b, edges, levels, extra = refs[directions:]
    del unpatched
    core = lax.axis_index("gz")
    side = lax.axis_index("gy")
    even = lax.rem(lax.axis_index("gx"), 2) == 0

    def patch(components, row, strip):
        for k, q in enumerate(components):
            pulled[q, pl.ds(row, 32, stride=8), :] = strip[k * 32 : k * 32 + 32, :].astype(f32)

    def outer_line(strip):
        parts = strip[COARSE_ROWS:STRIP, :].astype(f32)
        coarse = parts[0:8] + parts[8:16] + parts[16:24]
        return jnp.dot(coarse, basis_z[core], precision=highest, preferred_element_type=f32)

    if directions == 1:
        pl.when(side == 0)(lambda: patch(YP, 7, received[0]))
        pl.when(side == 1)(lambda: patch(YM, 0, received[0]))
        outer = [(outer_line(received[0]), basis_y[3 - 3 * side])]
    else:
        patch(YM, 0, received[0])
        patch(YP, 7, received[1])
        outer = [(outer_line(received[0]), basis_y[0]), (outer_line(received[1]), basis_y[3])]
    terms = [(lines[0:8, :], basis_y[1]), (lines[8:16, :], basis_y[2])] + outer
    for n, (line, _) in enumerate(terms):
        extra[n * 8 : n * 8 + 8, :] = line
    for i in range(8):
        level = None
        for n, (_, weight) in enumerate(terms):
            term = weight * jnp.broadcast_to(extra[n * 8 + i : n * 8 + i + 1, :], (8, 128))
            level = term if level is None else level + term
        levels[i] = level

    def put(slot, low, high):
        out_a[slot] = jnp.where(even, high, low)
        out_b[slot] = jnp.where(even, low, high)

    for k in range(5):
        put(FACE + k, pulled[XP[k], rows_of(0), :], pulled[XM[k], rows_of(31), :])
    for n in range(4):
        put(FIELD + n, flows[n, 0], flows[n, 31])
    for n in range(2):
        put(LEVEL + n, levels[n], levels[6 + n])
    results = []
    for x in EDGE_PLANES:
        values = {}
        for q in range(19):
            target = x + VELOCITY[q][0]
            if 0 <= target < 32:
                values[q] = pulled[q, rows_of(target), :]
        flow = tuple(flows[n, x] for n in range(3))
        results.append(alpha_beta(pair_moments(values), flow, flows[MASS, x]))
    for position in range(4):
        for n, slot in enumerate((ALPHA, BETA)):
            low, high = results[position][n], results[4 + position][n]
            edges[n, position] = low
            edges[n, 4 + position] = high
            put(slot + position, low, high)


def slope_of(bent):
    return -1.8 * (1.0 - bent * bent)


def bent_level(around, position):
    value = None
    for shift, level in zip((-1, 0, 1), around):
        term = float(spline(position - 4.0 * shift - 1.5)) * level
        value = term if value is None else value + term
    return jnp.tanh(4.0 * value)


def weight_of(position, shift):
    return float(spline(position - 4.0 * shift - 1.5))


def prior_fields(bent, here, flow, inverse, moments):
    zeroth, first, second = moments
    fluid = here == 0
    retained = 0.55 + 0.45 * bent
    share = jnp.where(fluid, retained, 1.0)
    speed = tuple(share * component for component in flow)
    curved = second_times(second, speed)
    slopes = tuple(3.0 * first[n] + 9.0 * curved[n] - 3.0 * zeroth * speed[n] for n in range(3))
    along = dot3(slopes, flow)
    value = zeroth + 0.5 * (3.0 * dot3(first, speed) + dot3(slopes, speed))
    factor = jnp.where(
        fluid, (1.6 / 36.0) * retained, jnp.where(here == 3, inverse * (1.0 / 36.0), 0.0)
    )
    base = jnp.where(fluid, (1.6 / 36.0) * value, 0.0) - factor * along
    return (base,) + tuple(factor * slope for slope in slopes), along


def emit_prior(stage, slot, here, values, result):
    solid = here == 1
    keep = jnp.where(here == 0, -0.6, 0.0)
    base, bx, by, bz = result
    shifts = {}
    for step_x in (-1, 0, 1):
        row = base if step_x == 0 else (base + bx if step_x > 0 else base - bx)
        for step_y in (-1, 0, 1):
            both = row if step_y == 0 else (row + by if step_y > 0 else row - by)
            shifts[step_x, step_y] = both
    for q in range(19):
        step_x, step_y, step_z = VELOCITY[q]
        shift = shifts[step_x, step_y]
        if step_z:
            shift = shift + bz if step_z > 0 else shift - bz
        kept = jnp.where(solid, values[OPPOSITE[q]], keep * values[q])
        stage[q, slot] = (kept + shift).astype(bf16)


def collide_inside(pulled, flows, kind, levels, out, totals, stage, semaphores):
    totals[...] = jnp.zeros((8, 8, 128), f32)

    def middle(block, carry):
        around = [levels[block - 1], levels[block], levels[block + 1]]
        sums = [None] * 3
        for position in range(4):
            x = block * 4 + position
            bent = bent_level(around, position)
            flow = tuple(flows[n, x] for n in range(3))
            values = {q: pulled[q, rows_of(x + VELOCITY[q][0]), :] for q in range(19)}
            result, along = prior_fields(bent, kind[x], flow, flows[INVERSE, x], pair_moments(values))
            emit_prior(stage, x - 4, kind[x], values, result)
            sensitivity = (-1.6 / 36.0) * flows[MASS, x] * along * slope_of(bent)
            for n in range(3):
                term = weight_of(position, n - 1) * sensitivity
                sums[n] = term if sums[n] is None else sums[n] + term
        for n in range(3):
            totals[block + n - 1] += sums[n]
        return carry

    copies = []
    for part in range(3):
        lax.fori_loop(1 + 2 * part, 3 + 2 * part, middle, 0)
        copies.append(
            pltpu.make_async_copy(
                stage.at[:, pl.ds(8 * part, 8)], out.at[:, pl.ds(4 + 8 * part, 8)], semaphores.at[part]
            )
        )
        copies[part].start()
    for copy in copies:
        copy.wait()


def along_x(received_a, received_b):
    place = lax.axis_index("gx")
    even = lax.rem(place, 2) == 0
    has_low, has_high = place > 0, place < lax.axis_size("gx") - 1

    def low(slot):
        return jnp.where(has_low, jnp.where(even, received_b[slot], received_a[slot]), 0.0)

    def high(slot):
        return jnp.where(has_high, jnp.where(even, received_a[slot], received_b[slot]), 0.0)

    return low, high


def project(pulled, flows, edges, levels, received_a, received_b, inner, fold_y, fold_z, gradient):
    core = lax.axis_index("gz")
    low, high = along_x(received_a, received_b)
    totals = [inner[i] for i in range(8)]
    lower = [low(LEVEL), low(LEVEL + 1)] + [levels[i] for i in range(3)]
    upper = [levels[i] for i in range(5, 8)] + [high(LEVEL), high(LEVEL + 1)]

    def add(block, position, alpha, beta):
        start = block + 1 if block < 4 else block - 6
        around = (lower if block < 4 else upper)[start : start + 3]
        bent = bent_level(around, position)
        sensitivity = (alpha + (0.55 + 0.45 * bent) * beta) * slope_of(bent)
        for shift in (-1, 0, 1):
            if 0 <= block + shift < 8:
                totals[block + shift] = totals[block + shift] + weight_of(position, shift) * sensitivity

    def faces(ref, components):
        return pair_moments({q: ref(FACE + k) for k, q in enumerate(components)})

    def own(x, components):
        return pair_moments({q: pulled[q, rows_of(x), :] for q in components})

    def flow_at(x):
        return tuple(flows[n, x] for n in range(3))

    missing = {
        (0, 0): alpha_beta(faces(low, XM), flow_at(0), flows[MASS, 0]),
        (7, 3): alpha_beta(faces(high, XP), flow_at(31), flows[MASS, 31]),
        (-1, 3): alpha_beta(own(0, XP), tuple(low(FIELD + n) for n in range(3)), low(FIELD + 3)),
        (8, 0): alpha_beta(own(31, XM), tuple(high(FIELD + n) for n in range(3)), high(FIELD + 3)),
    }
    for block in (-1, 0, 7, 8):
        for position in range(4):
            if block in (0, 7):
                index = position + (4 if block else 0)
                alpha, beta = edges[0, index], edges[1, index]
            else:
                ref = low if block < 0 else high
                alpha, beta = ref(ALPHA + position), ref(BETA + position)
            if (block, position) in missing:
                more = missing[block, position]
                alpha, beta = alpha + more[0], beta + more[1]
            add(block, position, alpha, beta)
    stacked = jnp.concatenate(totals, axis=0)
    folded = jnp.dot(fold_y[...], stacked, precision=highest, preferred_element_type=f32)
    result = jnp.dot(folded, fold_z[core], precision=highest, preferred_element_type=f32)
    for part in range(2):
        for j in range(4):
            gradient[part, j] = result[j * 8 : j * 8 + 8, part * 32 : part * 32 + 32]


def collide_outside(pulled, flows, kind, levels, received_a, received_b, inner, out, stage, semaphores):
    del inner
    low, high = along_x(received_a, received_b)
    copies = []
    for part, planes in enumerate((EDGE_PLANES[:4], EDGE_PLANES[4:])):
        for slot, x in enumerate(planes):
            values = {}
            for q in range(19):
                target = x + VELOCITY[q][0]
                if target < 0:
                    values[q] = low(FACE + XM.index(q))
                elif target > 31:
                    values[q] = high(FACE + XP.index(q))
                else:
                    values[q] = pulled[q, rows_of(target), :]
            around = (
                [levels[6], levels[7], high(LEVEL)] if part else [low(LEVEL + 1), levels[0], levels[1]]
            )
            flow = tuple(flows[n, x] for n in range(3))
            result, _ = prior_fields(
                bent_level(around, slot), kind[x], flow, flows[INVERSE, x], pair_moments(values)
            )
            emit_prior(stage, 4 * part + slot, kind[x], values, result)
        copies.append(
            pltpu.make_async_copy(
                stage.at[:, pl.ds(4 * part, 4)], out.at[:, pl.ds(28 * part, 4)], semaphores.at[part]
            )
        )
        copies[part].start()
    for copy in copies:
        copy.wait()


def bases():
    fine = np.arange(128.0)
    basis_z = np.zeros((2, 128, 128))
    fold_z = np.zeros((2, 128, 64))
    for core in range(2):
        full = spline(fine[None, :] + 128 * core - 4.0 * np.arange(64)[:, None] - 1.5)
        basis_z[core, 0:64] = full
        fold_z[core, :, 0:32] = full[32 * core : 32 * core + 32].T
        fold_z[core, :, 32:64] = full[32 * (1 - core) : 32 * (1 - core) + 32].T
    across = spline(np.arange(8.0)[None, :] - 4.0 * np.arange(-1, 3)[:, None] - 1.5)
    basis_y = np.broadcast_to(across[:, :, None], (4, 8, 128))
    fold_y = np.zeros((4, 8, 8, 8))
    for i in range(8):
        fold_y[:, i, i, :] = across
    return [
        jnp.asarray(np.ascontiguousarray(a), f32)
        for a in (basis_z, basis_y, fold_y.reshape(32, 64), fold_z)
    ]


def pairs(count, first):
    partner = {}
    for i in range(first, count - 1, 2):
        partner[i], partner[i + 1] = i + 1, i
    result = []
    for i in range(count):
        for core in range(2):
            target = (partner[i], core) if i in partner else (i, 1 - core)
            result.append((i * 2 + core, target[0] * 2 + target[1]))
    return result


def per_device(forward, adjoint, coefficients, kind):
    count_y = lax.axis_size("gy")
    count_x = lax.axis_size("gx")
    swap = [(0, 1), (1, 0)]
    side = lax.axis_index("gy")
    directions = 1 if count_y == 2 else 2
    tile = (8, 128)
    shape = jax.ShapeDtypeStruct
    basis_z, basis_y, fold_y, fold_z = bases()
    up = [(i, i + 1) for i in range(count_y - 1)]
    down = [(i + 1, i) for i in range(count_y - 1)]

    sent_z = kernel_call(
        pack_z,
        shape((4,) + tile, f32),
        [
            pltpu.VMEM((5,) + adjoint.shape[1:], bf16),
            pltpu.VMEM(coefficients.shape, f32),
            pltpu.SemaphoreType.DMA((6,)),
        ],
        in_specs=[pl.BlockSpec(memory_space=pltpu.HBM)] * 2,
    )(*(pltpu.with_memory_space_constraint(a, pltpu.HBM) for a in (adjoint, coefficients)))
    received_z = lax.ppermute(sent_z, "gz", swap)
    rows = kernel_call(
        functools.partial(gather_rows, directions),
        [shape((COARSE_ROWS, 128), f32)] * directions,
        [pltpu.VMEM((256, 128), f32)],
    )(adjoint)
    sent_y = kernel_call(
        functools.partial(pack_y, directions), [shape((STRIP, 128), bf16)] * directions
    )(sent_z, received_z, *rows)
    if directions == 1:
        received_y = [lax.ppermute(sent_y[0], "gy", swap)]
    else:
        received_y = [lax.ppermute(sent_y[0], "gy", up), lax.ppermute(sent_y[1], "gy", down)]

    pulled, flows, lines = kernel_call(
        pull_zy,
        [shape((19, 256, 128), f32), shape((5,) + kind.shape, f32), shape((16, 128), f32)],
        [pltpu.VMEM((2, 2) + tile, f32)],
    )(adjoint, forward, kind, sent_z, received_z, basis_z)

    bundle = shape((BUNDLE,) + tile, f32)
    pulled, sent_a, sent_b, edges, levels = kernel_call(
        functools.partial(pack_x, directions),
        [pulled, bundle, bundle, shape((2, 8) + tile, f32), shape((8,) + tile, f32)],
        [pltpu.VMEM((32, 128), f32)],
        aliases={0: 0},
    )(pulled, flows, lines, basis_z, basis_y, *received_y)
    received_b = lax.ppermute(sent_b, ("gx", "gz"), pairs(count_x, 1))
    received_a = lax.ppermute(sent_a, ("gx", "gz"), pairs(count_x, 0))

    prior, totals = kernel_call(
        collide_inside,
        [shape(adjoint.shape, bf16), shape((8,) + tile, f32)],
        [pltpu.VMEM((19, 24) + tile, bf16), pltpu.SemaphoreType.DMA((3,))],
        out_specs=[pl.BlockSpec(memory_space=pltpu.HBM), pl.BlockSpec(memory_space=pltpu.VMEM)],
    )(pulled, flows, kind, levels)
    gradient = kernel_call(project, shape((2, 4, 8, 32), f32))(
        pulled, flows, edges, levels, received_a, received_b, totals, fold_y, fold_z
    )

    whole = gradient[0] + lax.ppermute(gradient[1], "gz", swap)
    if directions == 1:
        other = lax.ppermute(jnp.where(side == 0, whole[3], whole[0]), "gy", swap)
        from_low = jnp.where(side == 1, other, 0.0)
        from_high = jnp.where(side == 0, other, 0.0)
    else:
        from_low = lax.ppermute(whole[3], "gy", up)
        from_high = lax.ppermute(whole[0], "gy", down)
    in_hbm = pl.BlockSpec(memory_space=pltpu.HBM)
    prior = kernel_call(
        collide_outside,
        shape(adjoint.shape, bf16),
        [pltpu.VMEM((19, 8) + tile, bf16), pltpu.SemaphoreType.DMA((2,))],
        aliases={6: 0},
        in_specs=[pl.BlockSpec(memory_space=pltpu.VMEM)] * 6 + [in_hbm],
        out_specs=in_hbm,
    )(pulled, flows, kind, levels, received_a, received_b, prior)
    return prior, jnp.stack([whole[1] + from_low, whole[2] + from_high], axis=1)


def solution(mesh):
    in_specs = (
        P(None, ("parts", "gx"), "gy", "gz"),
        P(None, ("parts", "gx"), "gy", "gz"),
        P(("parts", "gx"), "gy", "gz"),
        P(("parts", "gx"), "gy", "gz"),
    )
    out_specs = (P(None, ("parts", "gx"), "gy", "gz"), P(("parts", "gx"), "gy", "gz"))
    return jax.shard_map(
        per_device, mesh=mesh, in_specs=in_specs, out_specs=out_specs, check_vma=False
    )
```

```python
import functools

import jax
import jax.numpy as jnp
import numpy as np
from jax import lax
from jax.experimental import pallas as pl
from jax.experimental.pallas import tpu as pltpu
from jax.sharding import PartitionSpec as P

VELOCITY = (
    (0, 0, 0),
    (1, 0, 0),
    (-1, 0, 0),
    (0, 1, 0),
    (0, -1, 0),
    (0, 0, 1),
    (0, 0, -1),
    (1, 1, 0),
    (-1, -1, 0),
    (1, -1, 0),
    (-1, 1, 0),
    (1, 0, 1),
    (-1, 0, -1),
    (1, 0, -1),
    (-1, 0, 1),
    (0, 1, 1),
    (0, -1, -1),
    (0, 1, -1),
    (0, -1, 1),
)
OPPOSITE = (0, 2, 1, 4, 3, 6, 5, 8, 7, 10, 9, 12, 11, 14, 13, 16, 15, 18, 17)
highest = lax.Precision.HIGHEST
f32 = jnp.float32
bf16 = jnp.bfloat16


def going(dimension, sign):
    return [q for q in range(19) if VELOCITY[q][dimension] == sign]


XP, XM = going(0, 1), going(0, -1)
YP, YM = going(1, 1), going(1, -1)
ZP, ZM = going(2, 1), going(2, -1)

FACE, NEAR, FAR, FIELD, LEVEL, BUNDLE = 0, 5, 9, 15, 19, 23
SLOTS = 3
COARSE_ROWS, STRIP = 160, 176
MASS, INVERSE = 3, 4
EDGE_PLANES = (0, 1, 2, 3, 28, 29, 30, 31)


def spline(distance):
    radius = np.abs(distance) / 6.0
    return np.where(radius < 1.0, (1.0 - radius) ** 4 * (1.0 + 4.0 * radius), 0.0)


def kernel_call(body, out_shape, scratch_shapes=(), aliases=None, **specs):
    return pl.pallas_call(
        body,
        out_shape=out_shape,
        scratch_shapes=list(scratch_shapes),
        compiler_params=pltpu.CompilerParams(vmem_limit_bytes=12 * 1024 * 1024),
        input_output_aliases=aliases or {},
        **specs,
    )


def iota(dimension):
    return lax.broadcasted_iota(jnp.int32, (8, 128), dimension)


def pulled_z(q, tile, x, columns):
    step = VELOCITY[q][2]
    if step == 0:
        return tile
    slot = (ZP if step > 0 else ZM).index(q) * 32
    group, lane = slot // 128, slot % 128
    lanes = iota(1)
    edge = columns[0 if step > 0 else 1, group]
    if step > 0:
        edge = pltpu.roll(edge, 127 - lane - x, 1)
        return jnp.where(lanes == 127, edge, pltpu.roll(tile, 127, 1))
    edge = pltpu.roll(edge, (128 - lane - x) & 127, 1)
    return jnp.where(lanes == 0, edge, pltpu.roll(tile, 1, 1))


def load_columns(core, received, columns):
    for group in range(2):
        tile = received[group]
        columns[0, group] = jnp.where(core == 0, tile, 0.0)
        columns[1, group] = jnp.where(core == 1, tile, 0.0)


def pair_moments(populations):
    sums, diffs = {}, {}
    for q in range(1, 19, 2):
        a, b = populations.get(q), populations.get(q + 1)
        if a is None and b is None:
            continue
        if b is None:
            sums[q], diffs[q] = a, a
        elif a is None:
            sums[q], diffs[q] = b, -b
        else:
            sums[q], diffs[q] = a + b, a - b

    def total(terms):
        value = None
        for sign, table, q in terms:
            if q not in table:
                continue
            item = table[q]
            if value is None:
                value = item if sign > 0 else -item
            else:
                value = value + item if sign > 0 else value - item
        return value

    def plus(a, b):
        return b if a is None else (a if b is None else a + b)

    def twice(a):
        return None if a is None else a + a

    xx = total([(1, sums, 7), (1, sums, 9), (1, sums, 11), (1, sums, 13)])
    edge_yz = total([(1, sums, 15), (1, sums, 17)])
    edge_xy = total([(1, sums, 7), (1, sums, 9)])
    edge_xz = total([(1, sums, 11), (1, sums, 13)])
    sx, sy, sz = (twice(sums.get(q)) for q in (1, 3, 5))
    zeroth = plus(plus(xx, edge_yz), plus(plus(sx, sy), sz))
    if 0 in populations:
        zeroth = zeroth + 12.0 * populations[0]
    mx = plus(twice(diffs.get(1)), total([(1, diffs, 7), (1, diffs, 9), (1, diffs, 11), (1, diffs, 13)]))
    my = plus(twice(diffs.get(3)), total([(1, diffs, 7), (-1, diffs, 9), (1, diffs, 15), (1, diffs, 17)]))
    mz = plus(twice(diffs.get(5)), total([(1, diffs, 11), (-1, diffs, 13), (1, diffs, 15), (-1, diffs, 17)]))
    mxx = plus(sx, xx)
    myy = plus(sy, plus(edge_xy, edge_yz))
    mzz = plus(sz, plus(edge_xz, edge_yz))
    mxy = total([(1, sums, 7), (-1, sums, 9)])
    mxz = total([(1, sums, 11), (-1, sums, 13)])
    myz = total([(1, sums, 15), (-1, sums, 17)])
    return zeroth, (mx, my, mz), (mxx, myy, mzz, mxy, mxz, myz)


def flow_moments(populations):
    sums = {q: populations[q] + populations[q + 1] for q in range(1, 19, 2)}
    diffs = {q: populations[q] - populations[q + 1] for q in range(1, 19, 2)}
    rho = populations[0]
    for q in range(1, 19, 2):
        rho = rho + sums[q]
    jx = (diffs[1] + diffs[7]) + (diffs[9] + diffs[11]) + diffs[13]
    jy = (diffs[3] + diffs[7]) + (diffs[15] - diffs[9]) + diffs[17]
    jz = (diffs[5] + diffs[11]) + (diffs[15] - diffs[13]) - diffs[17]
    return rho, (jx, jy, jz)


def dot3(a, b):
    return a[0] * b[0] + a[1] * b[1] + a[2] * b[2]


def second_times(second, v):
    mxx, myy, mzz, mxy, mxz, myz = second

    def row(terms):
        value = None
        for coefficient, component in terms:
            if coefficient is None:
                continue
            product = coefficient * component
            value = product if value is None else value + product
        return value

    return (
        row([(mxx, v[0]), (mxy, v[1]), (mxz, v[2])]),
        row([(mxy, v[0]), (myy, v[1]), (myz, v[2])]),
        row([(mxz, v[0]), (myz, v[1]), (mzz, v[2])]),
    )


def alpha_beta(moments, flow, flow_mass):
    zeroth, first, second = moments
    scale = flow_mass * (-1.6 / 36.0)
    alpha = scale * 3.0 * dot3(first, flow)
    beta = scale * (9.0 * dot3(second_times(second, flow), flow) - 3.0 * zeroth * dot3(flow, flow))
    return alpha, beta


def rows_of(x):
    return pl.ds(pl.multiple_of(x * 8, 8), 8) if not isinstance(x, int) else slice(x * 8, x * 8 + 8)


def pack_z(adjoint, coefficients, out, faces, coarse, semaphores):
    core = lax.axis_index("gz")
    copies = [pltpu.make_async_copy(coefficients, coarse, semaphores.at[5])]
    for k in range(5):
        q = ZM[k] + core * (ZP[k] - ZM[k])
        copies.append(pltpu.make_async_copy(adjoint.at[q], faces.at[k], semaphores.at[k]))
    for copy in copies:
        copy.start()
    lanes = iota(1)
    count = coefficients.shape[2]
    out[2] = jnp.zeros((8, 128), f32)
    out[3] = jnp.zeros((8, 128), f32)
    for copy in copies:
        copy.wait()
    for which, source in enumerate((127, 0)):

        @pl.when(core == which)
        def _():
            for j in range(2):
                out[2 + j, :, count * which : count * which + count] = coarse[:, j, :]
            chains = {}
            for k in range(5):
                for x in range(32):
                    group, lane = divmod(k * 32 + x, 128)
                    column = pltpu.roll(faces[k, x].astype(f32), (lane - source) % 128, 1)
                    chain = group, lane // 16
                    if chain in chains:
                        column = jnp.where(lanes >= lane, column, chains[chain])
                    chains[chain] = column
            for group in range(2):
                tile = chains[group, 0]
                for part in range(1, 8 if group == 0 else 2):
                    tile = jnp.where(lanes >= part * 16, chains[group, part], tile)
                out[group] = tile


def y_sides(directions):
    return ((YM, 7), (YP, 0))


def gather_rows(directions, adjoint, *refs):
    outs, plane = refs[:-1], refs[-1]
    lanes = lax.broadcasted_iota(jnp.int32, (32, 128), 1)

    def emit(components, row, out):
        for k, q in enumerate(components):
            for x in range(32):
                plane[x * 8 : x * 8 + 8, :] = adjoint[q, x].astype(f32)
            rows = plane[pl.ds(row, 32, stride=8), :]
            step = VELOCITY[q][2]
            if step > 0:
                rows = jnp.where(lanes == 127, 0.0, pltpu.roll(rows, 127, 1))
            elif step < 0:
                rows = jnp.where(lanes == 0, 0.0, pltpu.roll(rows, 1, 1))
            out[k * 32 : k * 32 + 32, :] = rows

    sides = y_sides(directions)
    if directions == 1:
        side = lax.axis_index("gy")
        for n in range(2):
            pl.when(side == n)(functools.partial(emit, *sides[n], outs[0]))
    else:
        for n in range(2):
            emit(*sides[n], outs[n])


def pack_y(directions, sent, received, *refs):
    sources, outs = refs[:directions], refs[directions:]
    core = lax.axis_index("gz")
    lanes = lax.broadcasted_iota(jnp.int32, (32, 128), 1)
    sublanes = lax.broadcasted_iota(jnp.int32, (32, 128), 0)

    def emit(components, row, coarse_row, source, out):
        for k, q in enumerate(components):
            rows = source[k * 32 : k * 32 + 32, :]
            step = VELOCITY[q][2]
            if step:
                slot = (ZP if step > 0 else ZM).index(q) * 32
                group, lane = slot // 128, slot % 128
                spread = jnp.broadcast_to(received[group, row : row + 1, :], (32, 128))
                column = jnp.sum(jnp.where(lanes == sublanes + lane, spread, 0.0), axis=1, keepdims=True)
                column = jnp.where(core == (0 if step > 0 else 1), column, 0.0)
                rows = rows + jnp.where(lanes == (127 if step > 0 else 0), column, 0.0)
            out[k * 32 : k * 32 + 32, :] = rows.astype(bf16)
        coarse = sent[coarse_row] + received[coarse_row]
        high = coarse.astype(bf16)
        out[COARSE_ROWS:STRIP, :] = jnp.concatenate(
            [high, (coarse - high.astype(f32)).astype(bf16)], axis=0
        )

    sides = y_sides(directions)
    if directions == 1:
        side = lax.axis_index("gy")
        for n in range(2):
            pl.when(side == n)(functools.partial(emit, *sides[n], 3 - n, sources[0], outs[0]))
    else:
        for n in range(2):
            emit(*sides[n], 3 - n, sources[n], outs[n])


def pull_zy(
    adjoint, forward_far, kind, sent, received, basis_z, pulled, flows, lines, columns, forward, semaphores
):
    copies = [
        pltpu.make_async_copy(
            forward_far.at[:, pl.ds(8 * n, 8)], forward.at[:, pl.ds(8 * n, 8)], semaphores.at[n]
        )
        for n in range(4)
    ]
    for copy in copies:
        copy.start()
    core = lax.axis_index("gz")
    load_columns(core, received, columns)
    sublanes = iota(0)
    coarse = jnp.concatenate([sent[2] + received[2], sent[3] + received[3]], axis=0)
    lines[...] = jnp.dot(coarse, basis_z[core], precision=highest, preferred_element_type=f32)

    def step(x, carry):
        for q in range(19):
            tile = pulled_z(q, adjoint[q, x].astype(f32), x, columns)
            step_y = VELOCITY[q][1]
            if step_y > 0:
                tile = jnp.where(sublanes == 7, 0.0, pltpu.roll(tile, 7, 0))
            elif step_y < 0:
                tile = jnp.where(sublanes == 0, 0.0, pltpu.roll(tile, 1, 0))
            pulled[q, rows_of(x), :] = tile
        return carry

    def flow(x, carry):
        rho, mass = flow_moments([forward[q, x].astype(f32) for q in range(19)])
        inverse = 1.0 / rho
        for n in range(3):
            flows[n, x] = mass[n] * inverse
        flows[MASS, x] = jnp.where(kind[x] == 0, rho, 0.0)
        flows[INVERSE, x] = inverse
        return carry

    lax.fori_loop(0, 32, step, 0, unroll=4)
    for n, copy in enumerate(copies):
        copy.wait()
        lax.fori_loop(8 * n, 8 * n + 8, flow, 0, unroll=4)


def pack_x(directions, unpatched, flows, lines, basis_z, basis_y, *refs):
    received = refs[:directions]
    pulled, *outs, edges, levels, extra = refs[directions:]
    del unpatched
    core = lax.axis_index("gz")
    side = lax.axis_index("gy")
    place = lax.rem(lax.axis_index("gx"), SLOTS)

    def patch(components, row, strip):
        for k, q in enumerate(components):
            pulled[q, pl.ds(row, 32, stride=8), :] = strip[k * 32 : k * 32 + 32, :].astype(f32)

    def outer_line(strip):
        parts = strip[COARSE_ROWS:STRIP, :].astype(f32)
        coarse = parts[0:8] + parts[8:16]
        return jnp.dot(coarse, basis_z[core], precision=highest, preferred_element_type=f32)

    if directions == 1:
        pl.when(side == 0)(lambda: patch(YP, 7, received[0]))
        pl.when(side == 1)(lambda: patch(YM, 0, received[0]))
        outer = [(outer_line(received[0]), basis_y[3 - 3 * side])]
    else:
        patch(YM, 0, received[0])
        patch(YP, 7, received[1])
        outer = [(outer_line(received[0]), basis_y[0]), (outer_line(received[1]), basis_y[3])]
    terms = [(lines[0:8, :], basis_y[1]), (lines[8:16, :], basis_y[2])] + outer
    for n, (line, _) in enumerate(terms):
        extra[n * 8 : n * 8 + 8, :] = line
    for i in range(8):
        level = None
        for n, (_, weight) in enumerate(terms):
            term = weight * jnp.broadcast_to(extra[n * 8 + i : n * 8 + i + 1, :], (8, 128))
            level = term if level is None else level + term
        levels[i] = level

    def put(slot, low, high):
        for n, out in enumerate(outs):
            out[slot] = jnp.where(place == n, high, low).astype(bf16)

    def put_split(slot, low, high):
        put(slot, low, high)
        put(slot + 2, low - low.astype(bf16).astype(f32), high - high.astype(bf16).astype(f32))

    for k in range(5):
        put(FACE + k, pulled[XP[k], rows_of(0), :], pulled[XM[k], rows_of(31), :])
    for n in range(4):
        put(FIELD + n, flows[n, 0], flows[n, 31])
    for n in range(2):
        put_split(LEVEL + n, levels[n], levels[7 - n])
    results = []
    for x in EDGE_PLANES:
        values = {}
        for q in range(19):
            target = x + VELOCITY[q][0]
            if 0 <= target < 32:
                values[q] = pulled[q, rows_of(target), :]
        flow = tuple(flows[n, x] for n in range(3))
        results.append(alpha_beta(pair_moments(values), flow, flows[MASS, x]))
    for away in range(4):
        for n in range(2):
            low, high = results[away][n], results[7 - away][n]
            edges[n, away] = low
            edges[n, 7 - away] = high
            if away == 0:
                put_split(NEAR + n, low, high)
            else:
                put(FAR + 2 * (away - 1) + n, low, high)


def slope_of(bent):
    return -1.8 * (1.0 - bent * bent)


def bent_level(around, position):
    value = None
    for shift, level in zip((-1, 0, 1), around):
        term = float(spline(position - 4.0 * shift - 1.5)) * level
        value = term if value is None else value + term
    return jnp.tanh(4.0 * value)


def weight_of(position, shift):
    return float(spline(position - 4.0 * shift - 1.5))


def prior_fields(bent, here, flow, inverse, moments):
    zeroth, first, second = moments
    fluid = here == 0
    retained = 0.55 + 0.45 * bent
    share = jnp.where(fluid, retained, 1.0)
    speed = tuple(share * component for component in flow)
    curved = second_times(second, speed)
    slopes = tuple(3.0 * first[n] + 9.0 * curved[n] - 3.0 * zeroth * speed[n] for n in range(3))
    along = dot3(slopes, flow)
    value = zeroth + 0.5 * (3.0 * dot3(first, speed) + dot3(slopes, speed))
    factor = jnp.where(
        fluid, (1.6 / 36.0) * retained, jnp.where(here == 3, inverse * (1.0 / 36.0), 0.0)
    )
    base = jnp.where(fluid, (1.6 / 36.0) * value, 0.0) - factor * along
    return (base,) + tuple(factor * slope for slope in slopes), along


def emit_prior(stage, slot, here, values, result):
    solid = here == 1
    keep = jnp.where(here == 0, -0.6, 0.0)
    base, bx, by, bz = result
    shifts = {}
    for step_x in (-1, 0, 1):
        row = base if step_x == 0 else (base + bx if step_x > 0 else base - bx)
        for step_y in (-1, 0, 1):
            both = row if step_y == 0 else (row + by if step_y > 0 else row - by)
            shifts[step_x, step_y] = both
    for q in range(19):
        step_x, step_y, step_z = VELOCITY[q]
        shift = shifts[step_x, step_y]
        if step_z:
            shift = shift + bz if step_z > 0 else shift - bz
        kept = jnp.where(solid, values[OPPOSITE[q]], keep * values[q])
        stage[q, slot] = (kept + shift).astype(bf16)


def collide_inside(pulled, flows, kind, levels, out, totals, stage, semaphores):
    totals[...] = jnp.zeros((8, 8, 128), f32)

    def middle(block, carry):
        around = [levels[block - 1], levels[block], levels[block + 1]]
        sums = [None] * 3
        for position in range(4):
            x = block * 4 + position
            bent = bent_level(around, position)
            flow = tuple(flows[n, x] for n in range(3))
            values = {q: pulled[q, rows_of(x + VELOCITY[q][0]), :] for q in range(19)}
            result, along = prior_fields(bent, kind[x], flow, flows[INVERSE, x], pair_moments(values))
            emit_prior(stage, x - 4, kind[x], values, result)
            sensitivity = (-1.6 / 36.0) * flows[MASS, x] * along * slope_of(bent)
            for n in range(3):
                term = weight_of(position, n - 1) * sensitivity
                sums[n] = term if sums[n] is None else sums[n] + term
        for n in range(3):
            totals[block + n - 1] += sums[n]
        return carry

    copies = []
    for part in range(3):
        lax.fori_loop(1 + 2 * part, 3 + 2 * part, middle, 0)
        copies.append(
            pltpu.make_async_copy(
                stage.at[:, pl.ds(8 * part, 8)], out.at[:, pl.ds(4 + 8 * part, 8)], semaphores.at[part]
            )
        )
        copies[part].start()
    for copy in copies:
        copy.wait()


def along_x(received):
    place = lax.axis_index("gx")
    has_low, has_high = place > 0, place < lax.axis_size("gx") - 1
    turn = lax.rem(place, SLOTS)

    def reader(present, first):
        def read(slot):
            value = received[first][slot].astype(f32)
            for n in range(1, SLOTS):
                value = jnp.where(turn == n, received[(n + first) % SLOTS][slot].astype(f32), value)
            return jnp.where(present, value, 0.0)

        return read

    return reader(has_low, SLOTS - 1), reader(has_high, 0)


def levels_along_x(read):
    return [read(LEVEL + n) + read(LEVEL + 2 + n) for n in range(2)]


def in_parts(values, axis):
    high = values.astype(bf16)
    low = (values - high.astype(f32)).astype(bf16)
    return jnp.concatenate([high, high, low] if axis == 0 else [high, low, high], axis=axis)


def project(pulled, flows, edges, levels, *refs):
    inner, fold_y, fold_z, gradient = refs[SLOTS:]
    core = lax.axis_index("gz")
    low, high = along_x(refs[:SLOTS])
    totals = [inner[i] for i in range(8)]
    lower = levels_along_x(low)[::-1] + [levels[i] for i in range(3)]
    upper = [levels[i] for i in range(5, 8)] + levels_along_x(high)

    def add(block, position, alpha, beta):
        start = block + 1 if block < 4 else block - 6
        around = (lower if block < 4 else upper)[start : start + 3]
        bent = bent_level(around, position)
        sensitivity = (alpha + (0.55 + 0.45 * bent) * beta) * slope_of(bent)
        for shift in (-1, 0, 1):
            if 0 <= block + shift < 8:
                totals[block + shift] = totals[block + shift] + weight_of(position, shift) * sensitivity

    def faces(ref, components):
        return pair_moments({q: ref(FACE + k) for k, q in enumerate(components)})

    def own(x, components):
        return pair_moments({q: pulled[q, rows_of(x), :] for q in components})

    def flow_at(x):
        return tuple(flows[n, x] for n in range(3))

    missing = {
        (0, 0): alpha_beta(faces(low, XM), flow_at(0), flows[MASS, 0]),
        (7, 3): alpha_beta(faces(high, XP), flow_at(31), flows[MASS, 31]),
        (-1, 3): alpha_beta(own(0, XP), tuple(low(FIELD + n) for n in range(3)), low(FIELD + 3)),
        (8, 0): alpha_beta(own(31, XM), tuple(high(FIELD + n) for n in range(3)), high(FIELD + 3)),
    }
    for block in (-1, 0, 7, 8):
        for position in range(4):
            if block in (0, 7):
                index = position + (4 if block else 0)
                alpha, beta = edges[0, index], edges[1, index]
            else:
                ref, away = (low, 3 - position) if block < 0 else (high, position)
                alpha, beta = (
                    ref(NEAR + n) + ref(NEAR + 2 + n) if away == 0 else ref(FAR + 2 * (away - 1) + n)
                    for n in range(2)
                )
            if (block, position) in missing:
                more = missing[block, position]
                alpha, beta = alpha + more[0], beta + more[1]
            add(block, position, alpha, beta)
    stacked = jnp.concatenate(totals, axis=0)
    folded = jnp.dot(fold_y[...], in_parts(stacked, 0), preferred_element_type=f32)
    result = jnp.dot(in_parts(folded, 1), fold_z[core], preferred_element_type=f32)
    for part in range(2):
        for j in range(4):
            gradient[part, j] = result[j * 8 : j * 8 + 8, part * 32 : part * 32 + 32]


def collide_outside(pulled, flows, kind, levels, *refs):
    out, stage, semaphores = refs[SLOTS + 1 :]
    low, high = along_x(refs[:SLOTS])
    copies = []
    for part, planes in enumerate((EDGE_PLANES[:4], EDGE_PLANES[4:])):
        for slot, x in enumerate(planes):
            values = {}
            for q in range(19):
                target = x + VELOCITY[q][0]
                if target < 0:
                    values[q] = low(FACE + XM.index(q))
                elif target > 31:
                    values[q] = high(FACE + XP.index(q))
                else:
                    values[q] = pulled[q, rows_of(target), :]
            around = (
                [levels[6], levels[7], levels_along_x(high)[0]]
                if part
                else [levels_along_x(low)[0], levels[0], levels[1]]
            )
            flow = tuple(flows[n, x] for n in range(3))
            result, _ = prior_fields(
                bent_level(around, slot), kind[x], flow, flows[INVERSE, x], pair_moments(values)
            )
            emit_prior(stage, 4 * part + slot, kind[x], values, result)
        copies.append(
            pltpu.make_async_copy(
                stage.at[:, pl.ds(4 * part, 4)], out.at[:, pl.ds(28 * part, 4)], semaphores.at[part]
            )
        )
        copies[part].start()
    for copy in copies:
        copy.wait()


def bases():
    fine = np.arange(128.0)
    basis_z = np.zeros((2, 128, 128))
    fold_z = np.zeros((2, 128, 64))
    for core in range(2):
        full = spline(fine[None, :] + 128 * core - 4.0 * np.arange(64)[:, None] - 1.5)
        basis_z[core, 0:64] = full
        fold_z[core, :, 0:32] = full[32 * core : 32 * core + 32].T
        fold_z[core, :, 32:64] = full[32 * (1 - core) : 32 * (1 - core) + 32].T
    across = spline(np.arange(8.0)[None, :] - 4.0 * np.arange(-1, 3)[:, None] - 1.5)
    basis_y = np.broadcast_to(across[:, :, None], (4, 8, 128))
    fold_y = np.zeros((4, 8, 8, 8))
    for i in range(8):
        fold_y[:, i, i, :] = across
    parts = []
    for values, axis in ((fold_y.reshape(32, 64), 1), (fold_z, 1)):
        high = values.astype(bf16)
        low = (values - high.astype(np.float64)).astype(bf16)
        parts.append(np.concatenate([high, low, high] if values.ndim == 2 else [high, high, low], axis=axis))
    return [jnp.asarray(np.ascontiguousarray(a), f32) for a in (basis_z, basis_y)] + [
        jnp.asarray(a) for a in parts
    ]


def pairs(count, slot):
    partner = {}
    for i in range(slot, count - 1, SLOTS):
        partner[i], partner[i + 1] = i + 1, i
    result = []
    for i in range(count):
        for core in range(2):
            target = (partner[i], core) if i in partner else (i, 1 - core)
            result.append((i * 2 + core, target[0] * 2 + target[1]))
    return result


def per_device(forward, adjoint, coefficients, kind):
    count_y = lax.axis_size("gy")
    count_x = lax.axis_size("gx")
    swap = [(0, 1), (1, 0)]
    side = lax.axis_index("gy")
    directions = 1 if count_y == 2 else 2
    tile = (8, 128)
    shape = jax.ShapeDtypeStruct
    basis_z, basis_y, fold_y, fold_z = bases()
    up = [(i, i + 1) for i in range(count_y - 1)]
    down = [(i + 1, i) for i in range(count_y - 1)]

    sent_z = kernel_call(
        pack_z,
        shape((4,) + tile, f32),
        [
            pltpu.VMEM((5,) + adjoint.shape[1:], bf16),
            pltpu.VMEM(coefficients.shape, f32),
            pltpu.SemaphoreType.DMA((6,)),
        ],
        in_specs=[pl.BlockSpec(memory_space=pltpu.HBM)] * 2,
    )(*(pltpu.with_memory_space_constraint(a, pltpu.HBM) for a in (adjoint, coefficients)))
    received_z = lax.ppermute(sent_z, "gz", swap)
    rows = kernel_call(
        functools.partial(gather_rows, directions),
        [shape((COARSE_ROWS, 128), f32)] * directions,
        [pltpu.VMEM((256, 128), f32)],
    )(adjoint)
    sent_y = kernel_call(
        functools.partial(pack_y, directions), [shape((STRIP, 128), bf16)] * directions
    )(sent_z, received_z, *rows)
    if directions == 1:
        received_y = [lax.ppermute(sent_y[0], "gy", swap)]
    else:
        received_y = [lax.ppermute(sent_y[0], "gy", up), lax.ppermute(sent_y[1], "gy", down)]

    pulled, flows, lines = kernel_call(
        pull_zy,
        [shape((19, 256, 128), f32), shape((5,) + kind.shape, f32), shape((16, 128), f32)],
        [
            pltpu.VMEM((2, 2) + tile, f32),
            pltpu.VMEM(forward.shape, bf16),
            pltpu.SemaphoreType.DMA((4,)),
        ],
        in_specs=[
            pl.BlockSpec(memory_space=pltpu.HBM if n == 1 else pltpu.VMEM) for n in range(6)
        ],
    )(
        adjoint,
        pltpu.with_memory_space_constraint(forward, pltpu.HBM),
        kind,
        sent_z,
        received_z,
        basis_z,
    )

    pulled, *sent_x, edges, levels = kernel_call(
        functools.partial(pack_x, directions),
        [pulled]
        + [shape((BUNDLE,) + tile, bf16)] * SLOTS
        + [shape((2, 8) + tile, f32), shape((8,) + tile, f32)],
        [pltpu.VMEM((32, 128), f32)],
        aliases={0: 0},
    )(pulled, flows, lines, basis_z, basis_y, *received_y)
    received_x = [
        lax.ppermute(sent, ("gx", "gz"), pairs(count_x, slot)) for slot, sent in enumerate(sent_x)
    ]

    prior, totals = kernel_call(
        collide_inside,
        [shape(adjoint.shape, bf16), shape((8,) + tile, f32)],
        [pltpu.VMEM((19, 24) + tile, bf16), pltpu.SemaphoreType.DMA((3,))],
        out_specs=[pl.BlockSpec(memory_space=pltpu.HBM), pl.BlockSpec(memory_space=pltpu.VMEM)],
    )(pulled, flows, kind, levels)
    gradient = kernel_call(project, shape((2, 4, 8, 32), f32))(
        pulled, flows, edges, levels, *received_x, totals, fold_y, fold_z
    )

    whole = gradient[0] + lax.ppermute(gradient[1], "gz", swap)
    if directions == 1:
        other = lax.ppermute(jnp.where(side == 0, whole[3], whole[0]), "gy", swap)
        from_low = jnp.where(side == 1, other, 0.0)
        from_high = jnp.where(side == 0, other, 0.0)
    else:
        from_low = lax.ppermute(whole[3], "gy", up)
        from_high = lax.ppermute(whole[0], "gy", down)
    in_hbm = pl.BlockSpec(memory_space=pltpu.HBM)
    prior = kernel_call(
        collide_outside,
        shape(adjoint.shape, bf16),
        [pltpu.VMEM((19, 8) + tile, bf16), pltpu.SemaphoreType.DMA((2,))],
        aliases={4 + SLOTS: 0},
        in_specs=[pl.BlockSpec(memory_space=pltpu.VMEM)] * (4 + SLOTS) + [in_hbm],
        out_specs=in_hbm,
    )(pulled, flows, kind, levels, *received_x, prior)
    return prior, jnp.stack([whole[1] + from_low, whole[2] + from_high], axis=1)


def solution(mesh):
    in_specs = (
        P(None, ("parts", "gx"), "gy", "gz"),
        P(None, ("parts", "gx"), "gy", "gz"),
        P(("parts", "gx"), "gy", "gz"),
        P(("parts", "gx"), "gy", "gz"),
    )
    out_specs = (P(None, ("parts", "gx"), "gy", "gz"), P(("parts", "gx"), "gy", "gz"))
    return jax.shard_map(
        per_device, mesh=mesh, in_specs=in_specs, out_specs=out_specs, check_vma=False
    )
```

```python
import functools

import jax
import jax.numpy as jnp
import numpy as np
from jax import lax
from jax.experimental import pallas as pl
from jax.experimental.pallas import tpu as pltpu
from jax.sharding import PartitionSpec as P

VELOCITY = (
    (0, 0, 0),
    (1, 0, 0),
    (-1, 0, 0),
    (0, 1, 0),
    (0, -1, 0),
    (0, 0, 1),
    (0, 0, -1),
    (1, 1, 0),
    (-1, -1, 0),
    (1, -1, 0),
    (-1, 1, 0),
    (1, 0, 1),
    (-1, 0, -1),
    (1, 0, -1),
    (-1, 0, 1),
    (0, 1, 1),
    (0, -1, -1),
    (0, 1, -1),
    (0, -1, 1),
)
OPPOSITE = (0, 2, 1, 4, 3, 6, 5, 8, 7, 10, 9, 12, 11, 14, 13, 16, 15, 18, 17)
highest = lax.Precision.HIGHEST
f32 = jnp.float32
bf16 = jnp.bfloat16


def going(dimension, sign):
    return [q for q in range(19) if VELOCITY[q][dimension] == sign]


XP, XM = going(0, 1), going(0, -1)
YP, YM = going(1, 1), going(1, -1)
ZP, ZM = going(2, 1), going(2, -1)

FACE, NEAR, FAR, FIELD, LEVEL, BUNDLE = 0, 5, 9, 15, 19, 23
SLOTS = 3
LINE_ROWS, STRIP = 160, 176
MASS, INVERSE = 3, 4
EDGE_PLANES = (0, 1, 2, 3, 28, 29, 30, 31)
INNER = 16


def spline(distance):
    radius = np.abs(distance) / 6.0
    return np.where(radius < 1.0, (1.0 - radius) ** 4 * (1.0 + 4.0 * radius), 0.0)


def spline_along(dimension, shape, position):
    distance = lax.broadcasted_iota(jnp.int32, shape, dimension).astype(f32) - position
    radius = jnp.abs(distance) * (1.0 / 6.0)
    square = (1.0 - radius) * (1.0 - radius)
    return jnp.where(radius < 1.0, square * square * (1.0 + 4.0 * radius), 0.0)


def basis_along_z(count):
    places = lax.broadcasted_iota(jnp.int32, (count, 128), 0).astype(f32)
    return spline_along(1, (count, 128), 4.0 * places + 1.5)


def rim_along_z(core, count):
    return spline_along(1, (8, 128), jnp.where(core == 0, 4.0 * count + 1.5, -2.5))


def basis_along_y(j):
    return spline_along(0, (8, 128), 4.0 * j + 1.5)


def kernel_call(body, out_shape, scratch_shapes=(), aliases=None, **specs):
    return pl.pallas_call(
        body,
        out_shape=out_shape,
        scratch_shapes=list(scratch_shapes),
        compiler_params=pltpu.CompilerParams(vmem_limit_bytes=12 * 1024 * 1024),
        input_output_aliases=aliases or {},
        **specs,
    )


def iota(dimension):
    return lax.broadcasted_iota(jnp.int32, (8, 128), dimension)


def pulled_z(q, tile, x, columns):
    step = VELOCITY[q][2]
    if step == 0:
        return tile
    slot = (ZP if step > 0 else ZM).index(q) * 32
    group, lane = slot // 128, slot % 128
    lanes = iota(1)
    edge = columns[0 if step > 0 else 1, group]
    if step > 0:
        edge = pltpu.roll(edge, 127 - lane - x, 1)
        return jnp.where(lanes == 127, edge, pltpu.roll(tile, 127, 1))
    edge = pltpu.roll(edge, (128 - lane - x) & 127, 1)
    return jnp.where(lanes == 0, edge, pltpu.roll(tile, 1, 1))


def load_columns(core, received, columns):
    for group in range(2):
        tile = received[group]
        columns[0, group] = jnp.where(core == 0, tile, 0.0)
        columns[1, group] = jnp.where(core == 1, tile, 0.0)


def pair_moments(populations):
    sums, diffs = {}, {}
    for q in range(1, 19, 2):
        a, b = populations.get(q), populations.get(q + 1)
        if a is None and b is None:
            continue
        if b is None:
            sums[q], diffs[q] = a, a
        elif a is None:
            sums[q], diffs[q] = b, -b
        else:
            sums[q], diffs[q] = a + b, a - b

    def total(terms):
        value = None
        for sign, table, q in terms:
            if q not in table:
                continue
            item = table[q]
            if value is None:
                value = item if sign > 0 else -item
            else:
                value = value + item if sign > 0 else value - item
        return value

    def plus(a, b):
        return b if a is None else (a if b is None else a + b)

    def twice(a):
        return None if a is None else a + a

    xx = total([(1, sums, 7), (1, sums, 9), (1, sums, 11), (1, sums, 13)])
    edge_yz = total([(1, sums, 15), (1, sums, 17)])
    edge_xy = total([(1, sums, 7), (1, sums, 9)])
    edge_xz = total([(1, sums, 11), (1, sums, 13)])
    sx, sy, sz = (twice(sums.get(q)) for q in (1, 3, 5))
    zeroth = plus(plus(xx, edge_yz), plus(plus(sx, sy), sz))
    if 0 in populations:
        zeroth = zeroth + 12.0 * populations[0]
    mx = plus(twice(diffs.get(1)), total([(1, diffs, 7), (1, diffs, 9), (1, diffs, 11), (1, diffs, 13)]))
    my = plus(twice(diffs.get(3)), total([(1, diffs, 7), (-1, diffs, 9), (1, diffs, 15), (1, diffs, 17)]))
    mz = plus(twice(diffs.get(5)), total([(1, diffs, 11), (-1, diffs, 13), (1, diffs, 15), (-1, diffs, 17)]))
    mxx = plus(sx, xx)
    myy = plus(sy, plus(edge_xy, edge_yz))
    mzz = plus(sz, plus(edge_xz, edge_yz))
    mxy = total([(1, sums, 7), (-1, sums, 9)])
    mxz = total([(1, sums, 11), (-1, sums, 13)])
    myz = total([(1, sums, 15), (-1, sums, 17)])
    return zeroth, (mx, my, mz), (mxx, myy, mzz, mxy, mxz, myz)


def flow_moments(populations):
    sums = {q: populations[q] + populations[q + 1] for q in range(1, 19, 2)}
    diffs = {q: populations[q] - populations[q + 1] for q in range(1, 19, 2)}
    rho = populations[0]
    for q in range(1, 19, 2):
        rho = rho + sums[q]
    jx = (diffs[1] + diffs[7]) + (diffs[9] + diffs[11]) + diffs[13]
    jy = (diffs[3] + diffs[7]) + (diffs[15] - diffs[9]) + diffs[17]
    jz = (diffs[5] + diffs[11]) + (diffs[15] - diffs[13]) - diffs[17]
    return rho, (jx, jy, jz)


def dot3(a, b):
    return a[0] * b[0] + a[1] * b[1] + a[2] * b[2]


def second_times(second, v):
    mxx, myy, mzz, mxy, mxz, myz = second

    def row(terms):
        value = None
        for coefficient, component in terms:
            if coefficient is None:
                continue
            product = coefficient * component
            value = product if value is None else value + product
        return value

    return (
        row([(mxx, v[0]), (mxy, v[1]), (mxz, v[2])]),
        row([(mxy, v[0]), (myy, v[1]), (myz, v[2])]),
        row([(mxz, v[0]), (myz, v[1]), (mzz, v[2])]),
    )


def alpha_beta(moments, flow, flow_mass):
    zeroth, first, second = moments
    scale = flow_mass * (-1.6 / 36.0)
    alpha = scale * 3.0 * dot3(first, flow)
    beta = scale * (9.0 * dot3(second_times(second, flow), flow) - 3.0 * zeroth * dot3(flow, flow))
    return alpha, beta


def rows_of(x):
    return pl.ds(pl.multiple_of(x * 8, 8), 8) if not isinstance(x, int) else slice(x * 8, x * 8 + 8)


def pack_z(adjoint, coefficients, out, faces, coarse, semaphores):
    core = lax.axis_index("gz")
    copies = [pltpu.make_async_copy(coefficients, coarse, semaphores.at[5])]
    for k in range(5):
        q = ZM[k] + core * (ZP[k] - ZM[k])
        copies.append(pltpu.make_async_copy(adjoint.at[q], faces.at[k], semaphores.at[k]))
    for copy in copies:
        copy.start()
    lanes = iota(1)
    count = coefficients.shape[2]
    out[2] = jnp.zeros((8, 128), f32)
    out[3] = jnp.zeros((8, 128), f32)
    for copy in copies:
        copy.wait()
    for j in range(2):
        out[2 + j, :, 0:count] = coarse[:, j, :]
    for which, source in enumerate((127, 0)):

        @pl.when(core == which)
        def _():
            chains = {}
            for k in range(5):
                for x in range(32):
                    group, lane = divmod(k * 32 + x, 128)
                    column = pltpu.roll(faces[k, x].astype(f32), (lane - source) % 128, 1)
                    chain = group, lane // 16
                    if chain in chains:
                        column = jnp.where(lanes >= lane, column, chains[chain])
                    chains[chain] = column
            for group in range(2):
                tile = chains[group, 0]
                for part in range(1, 8 if group == 0 else 2):
                    tile = jnp.where(lanes >= part * 16, chains[group, part], tile)
                out[group] = tile


def y_sides(directions):
    return ((YM, 7), (YP, 0))


def gather_rows(directions, count, adjoint, sent, *refs):
    *outs, lines, plane = refs
    lines[...] = jnp.dot(
        jnp.concatenate([sent[2], sent[3]], axis=0),
        jnp.concatenate([basis_along_z(count), jnp.zeros((128 - count, 128), f32)], axis=0),
        precision=highest,
        preferred_element_type=f32,
    )
    lanes = lax.broadcasted_iota(jnp.int32, (32, 128), 1)

    def emit(components, row, out):
        for k, q in enumerate(components):
            for x in range(32):
                plane[x * 8 : x * 8 + 8, :] = adjoint[q, x].astype(f32)
            rows = plane[pl.ds(row, 32, stride=8), :]
            step = VELOCITY[q][2]
            if step > 0:
                rows = jnp.where(lanes == 127, 0.0, pltpu.roll(rows, 127, 1))
            elif step < 0:
                rows = jnp.where(lanes == 0, 0.0, pltpu.roll(rows, 1, 1))
            out[k * 32 : k * 32 + 32, :] = rows

    sides = y_sides(directions)
    if directions == 1:
        side = lax.axis_index("gy")
        for n in range(2):
            pl.when(side == n)(functools.partial(emit, *sides[n], outs[0]))
    else:
        for n in range(2):
            emit(*sides[n], outs[n])


def pack_y(directions, count, received, own_lines, *refs):
    sources, outs, lines = refs[:directions], refs[directions:-1], refs[-1]
    core = lax.axis_index("gz")
    lanes = lax.broadcasted_iota(jnp.int32, (32, 128), 1)
    sublanes = lax.broadcasted_iota(jnp.int32, (32, 128), 0)
    rim_z = rim_along_z(core, count)
    at_rim = iota(1) == core * (count - 1)
    for j in range(2):
        rim = jnp.sum(jnp.where(at_rim, received[2 + j], 0.0), axis=1, keepdims=True)
        lines[8 * j : 8 * j + 8, :] = own_lines[8 * j : 8 * j + 8, :] + rim * rim_z

    def emit(components, row, j, source, out):
        for k, q in enumerate(components):
            rows = source[k * 32 : k * 32 + 32, :]
            step = VELOCITY[q][2]
            if step:
                slot = (ZP if step > 0 else ZM).index(q) * 32
                group, lane = slot // 128, slot % 128
                spread = jnp.broadcast_to(received[group, row : row + 1, :], (32, 128))
                column = jnp.sum(jnp.where(lanes == sublanes + lane, spread, 0.0), axis=1, keepdims=True)
                column = jnp.where(core == (0 if step > 0 else 1), column, 0.0)
                rows = rows + jnp.where(lanes == (127 if step > 0 else 0), column, 0.0)
            out[k * 32 : k * 32 + 32, :] = rows.astype(bf16)
        line = lines[8 * j : 8 * j + 8, :]
        high = line.astype(bf16)
        out[LINE_ROWS:STRIP, :] = jnp.concatenate(
            [high, (line - high.astype(f32)).astype(bf16)], axis=0
        )

    sides = y_sides(directions)
    if directions == 1:
        side = lax.axis_index("gy")
        for n in range(2):
            pl.when(side == n)(functools.partial(emit, *sides[n], 1 - n, sources[0], outs[0]))
    else:
        for n in range(2):
            emit(*sides[n], 1 - n, sources[n], outs[n])


def pull_zy(
    adjoint, forward_far, kind, received, pulled, flows, columns, forward, semaphores
):
    copies = [
        pltpu.make_async_copy(
            forward_far.at[:, pl.ds(8 * n, 8)], forward.at[:, pl.ds(8 * n, 8)], semaphores.at[n]
        )
        for n in range(4)
    ]
    for copy in copies:
        copy.start()
    core = lax.axis_index("gz")
    load_columns(core, received, columns)
    sublanes = iota(0)

    def step(x, carry):
        for q in range(19):
            tile = pulled_z(q, adjoint[q, x].astype(f32), x, columns)
            step_y = VELOCITY[q][1]
            if step_y > 0:
                tile = jnp.where(sublanes == 7, 0.0, pltpu.roll(tile, 7, 0))
            elif step_y < 0:
                tile = jnp.where(sublanes == 0, 0.0, pltpu.roll(tile, 1, 0))
            pulled[q, rows_of(x), :] = tile
        return carry

    def flow(x, carry):
        rho, mass = flow_moments([forward[q, x].astype(f32) for q in range(19)])
        inverse = 1.0 / rho
        for n in range(3):
            flows[n, x] = mass[n] * inverse
        flows[MASS, x] = jnp.where(kind[x] == 0, rho, 0.0)
        flows[INVERSE, x] = inverse
        return carry

    lax.fori_loop(0, 32, step, 0, unroll=4)
    for n, copy in enumerate(copies):
        copy.wait()
        lax.fori_loop(8 * n, 8 * n + 8, flow, 0, unroll=4)


def pack_x(directions, unpatched, flows, lines, *refs):
    received = refs[:directions]
    pulled, *outs, edges, levels, extra = refs[directions:]
    del unpatched
    side = lax.axis_index("gy")
    place = lax.rem(lax.axis_index("gx"), SLOTS)

    def patch(components, row, strip):
        for k, q in enumerate(components):
            pulled[q, pl.ds(row, 32, stride=8), :] = strip[k * 32 : k * 32 + 32, :].astype(f32)

    def outer_line(strip):
        parts = strip[LINE_ROWS:STRIP, :].astype(f32)
        return parts[0:8] + parts[8:16]

    if directions == 1:
        pl.when(side == 0)(lambda: patch(YP, 7, received[0]))
        pl.when(side == 1)(lambda: patch(YM, 0, received[0]))
        outer = [(outer_line(received[0]), basis_along_y(jnp.where(side == 0, 2.0, -1.0)))]
    else:
        patch(YM, 0, received[0])
        patch(YP, 7, received[1])
        outer = [(outer_line(received[0]), basis_along_y(-1)), (outer_line(received[1]), basis_along_y(2))]
    terms = [(lines[0:8, :], basis_along_y(0)), (lines[8:16, :], basis_along_y(1))] + outer
    for n, (line, _) in enumerate(terms):
        extra[n * 8 : n * 8 + 8, :] = line
    for i in range(8):
        level = None
        for n, (_, weight) in enumerate(terms):
            term = weight * jnp.broadcast_to(extra[n * 8 + i : n * 8 + i + 1, :], (8, 128))
            level = term if level is None else level + term
        levels[i] = level

    def put(slot, low, high):
        for n, out in enumerate(outs):
            out[slot] = jnp.where(place == n, high, low).astype(bf16)

    def put_split(slot, low, high):
        put(slot, low, high)
        put(slot + 2, low - low.astype(bf16).astype(f32), high - high.astype(bf16).astype(f32))

    for k in range(5):
        put(FACE + k, pulled[XP[k], rows_of(0), :], pulled[XM[k], rows_of(31), :])
    for n in range(4):
        put(FIELD + n, flows[n, 0], flows[n, 31])
    for n in range(2):
        put_split(LEVEL + n, levels[n], levels[7 - n])
    results = []
    for x in EDGE_PLANES:
        values = {}
        for q in range(19):
            target = x + VELOCITY[q][0]
            if 0 <= target < 32:
                values[q] = pulled[q, rows_of(target), :]
        flow = tuple(flows[n, x] for n in range(3))
        results.append(alpha_beta(pair_moments(values), flow, flows[MASS, x]))
    for away in range(4):
        for n in range(2):
            low, high = results[away][n], results[7 - away][n]
            edges[n, away] = low
            edges[n, 7 - away] = high
            if away == 0:
                put_split(NEAR + n, low, high)
            else:
                put(FAR + 2 * (away - 1) + n, low, high)


def slope_of(bent):
    return -1.8 * (1.0 - bent * bent)


def bent_level(around, position):
    value = None
    for shift, level in zip((-1, 0, 1), around):
        term = float(spline(position - 4.0 * shift - 1.5)) * level
        value = term if value is None else value + term
    return jnp.tanh(4.0 * value)


def weight_of(position, shift):
    return float(spline(position - 4.0 * shift - 1.5))


def prior_fields(bent, here, flow, inverse, moments):
    zeroth, first, second = moments
    fluid = here == 0
    retained = 0.55 + 0.45 * bent
    share = jnp.where(fluid, retained, 1.0)
    speed = tuple(share * component for component in flow)
    curved = second_times(second, speed)
    slopes = tuple(3.0 * first[n] + 9.0 * curved[n] - 3.0 * zeroth * speed[n] for n in range(3))
    along = dot3(slopes, flow)
    value = zeroth + 0.5 * (3.0 * dot3(first, speed) + dot3(slopes, speed))
    factor = jnp.where(
        fluid, (1.6 / 36.0) * retained, jnp.where(here == 3, inverse * (1.0 / 36.0), 0.0)
    )
    base = jnp.where(fluid, (1.6 / 36.0) * value, 0.0) - factor * along
    return (base,) + tuple(factor * slope for slope in slopes), along


def emit_prior(stage, slot, here, values, result):
    solid = here == 1
    keep = jnp.where(here == 0, -0.6, 0.0)
    base, bx, by, bz = result
    shifts = {}
    for step_x in (-1, 0, 1):
        row = base if step_x == 0 else (base + bx if step_x > 0 else base - bx)
        for step_y in (-1, 0, 1):
            both = row if step_y == 0 else (row + by if step_y > 0 else row - by)
            shifts[step_x, step_y] = both
    for q in range(19):
        step_x, step_y, step_z = VELOCITY[q]
        shift = shifts[step_x, step_y]
        if step_z:
            shift = shift + bz if step_z > 0 else shift - bz
        kept = jnp.where(solid, values[OPPOSITE[q]], keep * values[q])
        stage[q, slot] = (kept + shift).astype(bf16)


def collide_inside(pulled, flows, kind, levels, out, totals, stage, semaphores):
    totals[...] = jnp.zeros((8, 8, 128), f32)

    def middle(with_prior, block, carry):
        around = [levels[block - 1], levels[block], levels[block + 1]]
        sums = [None] * 3
        for position in range(4):
            x = block * 4 + position
            bent = bent_level(around, position)
            flow = tuple(flows[n, x] for n in range(3))
            values = {q: pulled[q, rows_of(x + VELOCITY[q][0]), :] for q in range(19)}
            moments = pair_moments(values)
            if with_prior:
                result, along = prior_fields(bent, kind[x], flow, flows[INVERSE, x], moments)
                emit_prior(stage, x - 4, kind[x], values, result)
                sensitivity = (-1.6 / 36.0) * flows[MASS, x] * along
            else:
                alpha, beta = alpha_beta(moments, flow, flows[MASS, x])
                sensitivity = alpha + (0.55 + 0.45 * bent) * beta
            sensitivity = sensitivity * slope_of(bent)
            for n in range(3):
                term = weight_of(position, n - 1) * sensitivity
                sums[n] = term if sums[n] is None else sums[n] + term
        for n in range(3):
            totals[block + n - 1] += sums[n]
        return carry

    copies = []
    for part in range(INNER // 8):
        lax.fori_loop(1 + 2 * part, 3 + 2 * part, functools.partial(middle, True), 0)
        copies.append(
            pltpu.make_async_copy(
                stage.at[:, pl.ds(8 * part, 8)], out.at[:, pl.ds(4 + 8 * part, 8)], semaphores.at[part]
            )
        )
        copies[part].start()
    lax.fori_loop(1 + INNER // 4, 7, functools.partial(middle, False), 0)
    for copy in copies:
        copy.wait()


def along_x(received):
    place = lax.axis_index("gx")
    has_low, has_high = place > 0, place < lax.axis_size("gx") - 1
    turn = lax.rem(place, SLOTS)

    def reader(present, first):
        def read(slot):
            value = received[first][slot].astype(f32)
            for n in range(1, SLOTS):
                value = jnp.where(turn == n, received[(n + first) % SLOTS][slot].astype(f32), value)
            return jnp.where(present, value, 0.0)

        return read

    return reader(has_low, SLOTS - 1), reader(has_high, 0)


def levels_along_x(read):
    return [read(LEVEL + n) + read(LEVEL + 2 + n) for n in range(2)]


def fold_rows(tiles, weight):
    sublanes = iota(0)
    tiles = [weight * tile for tile in tiles]
    for bit in (4, 2, 1):
        half = len(tiles) // 2
        tiles = [
            jnp.where(
                sublanes & bit == 0,
                tiles[i] + pltpu.roll(tiles[i], 8 - bit, 0),
                tiles[i + half] + pltpu.roll(tiles[i + half], bit, 0),
            )
            for i in range(half)
        ]
    return tiles[0]


def project(pulled, flows, edges, levels, *refs):
    inner, folded, rim = refs[SLOTS:]
    core = lax.axis_index("gz")
    low, high = along_x(refs[:SLOTS])
    totals = [inner[i] for i in range(8)]
    lower = levels_along_x(low)[::-1] + [levels[i] for i in range(3)]
    upper = [levels[i] for i in range(5, 8)] + levels_along_x(high)

    def add(block, position, alpha, beta):
        start = block + 1 if block < 4 else block - 6
        around = (lower if block < 4 else upper)[start : start + 3]
        bent = bent_level(around, position)
        sensitivity = (alpha + (0.55 + 0.45 * bent) * beta) * slope_of(bent)
        for shift in (-1, 0, 1):
            if 0 <= block + shift < 8:
                totals[block + shift] = totals[block + shift] + weight_of(position, shift) * sensitivity

    def faces(ref, components):
        return pair_moments({q: ref(FACE + k) for k, q in enumerate(components)})

    def own(x, components):
        return pair_moments({q: pulled[q, rows_of(x), :] for q in components})

    def flow_at(x):
        return tuple(flows[n, x] for n in range(3))

    missing = {
        (0, 0): alpha_beta(faces(low, XM), flow_at(0), flows[MASS, 0]),
        (7, 3): alpha_beta(faces(high, XP), flow_at(31), flows[MASS, 31]),
        (-1, 3): alpha_beta(own(0, XP), tuple(low(FIELD + n) for n in range(3)), low(FIELD + 3)),
        (8, 0): alpha_beta(own(31, XM), tuple(high(FIELD + n) for n in range(3)), high(FIELD + 3)),
    }
    for block in (-1, 0, 7, 8):
        for position in range(4):
            if block in (0, 7):
                index = position + (4 if block else 0)
                alpha, beta = edges[0, index], edges[1, index]
            else:
                ref, away = (low, 3 - position) if block < 0 else (high, position)
                alpha, beta = (
                    ref(NEAR + n) + ref(NEAR + 2 + n) if away == 0 else ref(FAR + 2 * (away - 1) + n)
                    for n in range(2)
                )
            if (block, position) in missing:
                more = missing[block, position]
                alpha, beta = alpha + more[0], beta + more[1]
            add(block, position, alpha, beta)
    lanes = iota(1)
    count = rim.shape[2]
    rim_z = rim_along_z(core, count)
    for j in range(4):
        sums = fold_rows(totals, basis_along_y(j - 1))
        folded[8 * j : 8 * j + 8, :] = sums
        across = jnp.sum(sums * rim_z, axis=1, keepdims=True)
        rim[j] = jnp.where(lanes == core * (count - 1), across, 0.0)[:, 0:count]


def fold_along_z(folded, out):
    result = lax.dot_general(
        folded[...],
        basis_along_z(out.shape[2]),
        (((1,), (1,)), ((), ())),
        precision=highest,
        preferred_element_type=f32,
    )
    for j in range(4):
        out[j] = result[8 * j : 8 * j + 8]


def collide_outside(pulled, flows, kind, levels, *refs):
    out, stage, semaphores = refs[SLOTS + 1 :]
    low, high = along_x(refs[:SLOTS])
    first = 4 + INNER

    def emit(x, slot, around, position, values):
        flow = tuple(flows[n, x] for n in range(3))
        result, _ = prior_fields(
            bent_level(around, position), kind[x], flow, flows[INVERSE, x], pair_moments(values)
        )
        emit_prior(stage, slot, kind[x], values, result)

    def middle(block, carry):
        around = [levels[block - 1], levels[block], levels[block + 1]]
        for position in range(4):
            x = block * 4 + position
            values = {q: pulled[q, rows_of(x + VELOCITY[q][0]), :] for q in range(19)}
            emit(x, x - first + 4, around, position, values)
        return carry

    def edge(x, around):
        values = {}
        for q in range(19):
            target = x + VELOCITY[q][0]
            if target < 0:
                values[q] = low(FACE + XM.index(q))
            elif target > 31:
                values[q] = high(FACE + XP.index(q))
            else:
                values[q] = pulled[q, rows_of(target), :]
        emit(x, x if x < 4 else x - first + 4, around, x % 4, values)

    lowest = [levels_along_x(low)[0], levels[0], levels[1]]
    highest_levels = [levels[6], levels[7], levels_along_x(high)[0]]
    lax.fori_loop(1 + INNER // 4, 7, middle, 0)
    for x in range(28, 32):
        edge(x, highest_levels)
    copies = [
        pltpu.make_async_copy(
            stage.at[:, pl.ds(4, 32 - first)], out.at[:, pl.ds(first, 32 - first)], semaphores.at[0]
        ),
        pltpu.make_async_copy(stage.at[:, pl.ds(0, 4)], out.at[:, pl.ds(0, 4)], semaphores.at[1]),
    ]
    copies[0].start()
    for x in range(4):
        edge(x, lowest)
    copies[1].start()
    for copy in copies:
        copy.wait()


def pairs(count, slot):
    partner = {}
    for i in range(slot, count - 1, SLOTS):
        partner[i], partner[i + 1] = i + 1, i
    result = []
    for i in range(count):
        for core in range(2):
            target = (partner[i], core) if i in partner else (i, 1 - core)
            result.append((i * 2 + core, target[0] * 2 + target[1]))
    return result


def per_device(forward, adjoint, coefficients, kind):
    count_y = lax.axis_size("gy")
    count_x = lax.axis_size("gx")
    swap = [(0, 1), (1, 0)]
    side = lax.axis_index("gy")
    directions = 1 if count_y == 2 else 2
    tile = (8, 128)
    shape = jax.ShapeDtypeStruct
    count = coefficients.shape[2]
    up = [(i, i + 1) for i in range(count_y - 1)]
    down = [(i + 1, i) for i in range(count_y - 1)]

    sent_z = kernel_call(
        pack_z,
        shape((4,) + tile, f32),
        [
            pltpu.VMEM((5,) + adjoint.shape[1:], bf16),
            pltpu.VMEM(coefficients.shape, f32),
            pltpu.SemaphoreType.DMA((6,)),
        ],
        in_specs=[pl.BlockSpec(memory_space=pltpu.HBM)] * 2,
    )(*(pltpu.with_memory_space_constraint(a, pltpu.HBM) for a in (adjoint, coefficients)))
    received_z = lax.ppermute(sent_z, "gz", swap)
    *rows, lines = kernel_call(
        functools.partial(gather_rows, directions, count),
        [shape((LINE_ROWS, 128), f32)] * directions + [shape((16, 128), f32)],
        [pltpu.VMEM((256, 128), f32)],
    )(adjoint, sent_z)
    *sent_y, lines = kernel_call(
        functools.partial(pack_y, directions, count),
        [shape((STRIP, 128), bf16)] * directions + [shape((16, 128), f32)],
    )(received_z, lines, *rows)
    if directions == 1:
        received_y = [lax.ppermute(sent_y[0], "gy", swap)]
    else:
        received_y = [lax.ppermute(sent_y[0], "gy", up), lax.ppermute(sent_y[1], "gy", down)]

    pulled, flows = kernel_call(
        pull_zy,
        [shape((19, 256, 128), f32), shape((5,) + kind.shape, f32)],
        [
            pltpu.VMEM((2, 2) + tile, f32),
            pltpu.VMEM(forward.shape, bf16),
            pltpu.SemaphoreType.DMA((4,)),
        ],
        in_specs=[
            pl.BlockSpec(memory_space=pltpu.HBM if n == 1 else pltpu.VMEM) for n in range(4)
        ],
    )(
        adjoint,
        pltpu.with_memory_space_constraint(forward, pltpu.HBM),
        kind,
        received_z,
    )

    pulled, *sent_x, edges, levels = kernel_call(
        functools.partial(pack_x, directions),
        [pulled]
        + [shape((BUNDLE,) + tile, bf16)] * SLOTS
        + [shape((2, 8) + tile, f32), shape((8,) + tile, f32)],
        [pltpu.VMEM((32, 128), f32)],
        aliases={0: 0},
    )(pulled, flows, lines, *received_y)
    received_x = [
        lax.ppermute(sent, ("gx", "gz"), pairs(count_x, slot)) for slot, sent in enumerate(sent_x)
    ]

    prior, totals = kernel_call(
        collide_inside,
        [shape(adjoint.shape, bf16), shape((8,) + tile, f32)],
        [pltpu.VMEM((19, INNER) + tile, bf16), pltpu.SemaphoreType.DMA((INNER // 8,))],
        out_specs=[pl.BlockSpec(memory_space=pltpu.HBM), pl.BlockSpec(memory_space=pltpu.VMEM)],
    )(pulled, flows, kind, levels)
    folded, rim = kernel_call(project, [shape((32, 128), f32), shape((4, 8, count), f32)])(
        pulled, flows, edges, levels, *received_x, totals
    )
    other_rim = lax.ppermute(rim, "gz", swap)
    whole = kernel_call(fold_along_z, shape(rim.shape, f32))(folded) + other_rim
    if directions == 1:
        other = lax.ppermute(jnp.where(side == 0, whole[3], whole[0]), "gy", swap)
        from_low = jnp.where(side == 1, other, 0.0)
        from_high = jnp.where(side == 0, other, 0.0)
    else:
        from_low = lax.ppermute(whole[3], "gy", up)
        from_high = lax.ppermute(whole[0], "gy", down)
    in_hbm = pl.BlockSpec(memory_space=pltpu.HBM)
    prior = kernel_call(
        collide_outside,
        shape(adjoint.shape, bf16),
        [pltpu.VMEM((19, 32 - INNER) + tile, bf16), pltpu.SemaphoreType.DMA((2,))],
        aliases={4 + SLOTS: 0},
        in_specs=[pl.BlockSpec(memory_space=pltpu.VMEM)] * (4 + SLOTS) + [in_hbm],
        out_specs=in_hbm,
    )(pulled, flows, kind, levels, *received_x, prior)
    return prior, jnp.stack([whole[1] + from_low, whole[2] + from_high], axis=1)


def solution(mesh):
    in_specs = (
        P(None, ("parts", "gx"), "gy", "gz"),
        P(None, ("parts", "gx"), "gy", "gz"),
        P(("parts", "gx"), "gy", "gz"),
        P(("parts", "gx"), "gy", "gz"),
    )
    out_specs = (P(None, ("parts", "gx"), "gy", "gz"), P(("parts", "gx"), "gy", "gz"))
    return jax.shard_map(
        per_device, mesh=mesh, in_specs=in_specs, out_specs=out_specs, check_vma=False
    )
```

```python
import functools

import jax
import jax.numpy as jnp
import numpy as np
from jax import lax
from jax.experimental import pallas as pl
from jax.experimental.pallas import tpu as pltpu
from jax.sharding import PartitionSpec as P

VELOCITY = (
    (0, 0, 0),
    (1, 0, 0),
    (-1, 0, 0),
    (0, 1, 0),
    (0, -1, 0),
    (0, 0, 1),
    (0, 0, -1),
    (1, 1, 0),
    (-1, -1, 0),
    (1, -1, 0),
    (-1, 1, 0),
    (1, 0, 1),
    (-1, 0, -1),
    (1, 0, -1),
    (-1, 0, 1),
    (0, 1, 1),
    (0, -1, -1),
    (0, 1, -1),
    (0, -1, 1),
)
OPPOSITE = (0, 2, 1, 4, 3, 6, 5, 8, 7, 10, 9, 12, 11, 14, 13, 16, 15, 18, 17)
highest = lax.Precision.HIGHEST
f32 = jnp.float32
bf16 = jnp.bfloat16


def going(dimension, sign):
    return [q for q in range(19) if VELOCITY[q][dimension] == sign]


XP, XM = going(0, 1), going(0, -1)
YP, YM = going(1, 1), going(1, -1)
ZP, ZM = going(2, 1), going(2, -1)

FACE, NEAR, FAR, FIELD, LEVEL, BUNDLE = 0, 5, 9, 15, 19, 23
SLOTS = 3
LINE_ROWS, STRIP = 160, 176
MASS, INVERSE = 3, 4
EDGE_PLANES = (0, 1, 2, 3, 28, 29, 30, 31)
INNER = 16


def spline(distance):
    radius = np.abs(distance) / 6.0
    return np.where(radius < 1.0, (1.0 - radius) ** 4 * (1.0 + 4.0 * radius), 0.0)


def spline_along(dimension, shape, position):
    distance = lax.broadcasted_iota(jnp.int32, shape, dimension).astype(f32) - position
    radius = jnp.abs(distance) * (1.0 / 6.0)
    square = (1.0 - radius) * (1.0 - radius)
    return jnp.where(radius < 1.0, square * square * (1.0 + 4.0 * radius), 0.0)


def basis_along_z(count):
    places = lax.broadcasted_iota(jnp.int32, (count, 128), 0).astype(f32)
    return spline_along(1, (count, 128), 4.0 * places + 1.5)


def rim_along_z(core, count):
    return spline_along(1, (8, 128), jnp.where(core == 0, 4.0 * count + 1.5, -2.5))


def basis_along_y(j):
    return spline_along(0, (8, 128), 4.0 * j + 1.5)


def kernel_call(body, out_shape, scratch_shapes=(), aliases=None, **specs):
    return pl.pallas_call(
        body,
        out_shape=out_shape,
        scratch_shapes=list(scratch_shapes),
        compiler_params=pltpu.CompilerParams(vmem_limit_bytes=12 * 1024 * 1024),
        input_output_aliases=aliases or {},
        **specs,
    )


def iota(dimension):
    return lax.broadcasted_iota(jnp.int32, (8, 128), dimension)


def pulled_z(q, tile, x, columns):
    step = VELOCITY[q][2]
    if step == 0:
        return tile
    slot = (ZP if step > 0 else ZM).index(q) * 32
    group, lane = slot // 128, slot % 128
    lanes = iota(1)
    edge = columns[0 if step > 0 else 1, group]
    if step > 0:
        edge = pltpu.roll(edge, 127 - lane - x, 1)
        return jnp.where(lanes == 127, edge, pltpu.roll(tile, 127, 1))
    edge = pltpu.roll(edge, (128 - lane - x) & 127, 1)
    return jnp.where(lanes == 0, edge, pltpu.roll(tile, 1, 1))


def load_columns(core, received, columns):
    for group in range(2):
        tile = received[group]
        columns[0, group] = jnp.where(core == 0, tile, 0.0)
        columns[1, group] = jnp.where(core == 1, tile, 0.0)


def pair_moments(populations):
    sums, diffs = {}, {}
    for q in range(1, 19, 2):
        a, b = populations.get(q), populations.get(q + 1)
        if a is None and b is None:
            continue
        if b is None:
            sums[q], diffs[q] = a, a
        elif a is None:
            sums[q], diffs[q] = b, -b
        else:
            sums[q], diffs[q] = a + b, a - b

    def total(terms):
        value = None
        for sign, table, q in terms:
            if q not in table:
                continue
            item = table[q]
            if value is None:
                value = item if sign > 0 else -item
            else:
                value = value + item if sign > 0 else value - item
        return value

    def plus(a, b):
        return b if a is None else (a if b is None else a + b)

    def twice(a):
        return None if a is None else a + a

    xx = total([(1, sums, 7), (1, sums, 9), (1, sums, 11), (1, sums, 13)])
    edge_yz = total([(1, sums, 15), (1, sums, 17)])
    edge_xy = total([(1, sums, 7), (1, sums, 9)])
    edge_xz = total([(1, sums, 11), (1, sums, 13)])
    sx, sy, sz = (twice(sums.get(q)) for q in (1, 3, 5))
    zeroth = plus(plus(xx, edge_yz), plus(plus(sx, sy), sz))
    if 0 in populations:
        zeroth = zeroth + 12.0 * populations[0]
    mx = plus(twice(diffs.get(1)), total([(1, diffs, 7), (1, diffs, 9), (1, diffs, 11), (1, diffs, 13)]))
    my = plus(twice(diffs.get(3)), total([(1, diffs, 7), (-1, diffs, 9), (1, diffs, 15), (1, diffs, 17)]))
    mz = plus(twice(diffs.get(5)), total([(1, diffs, 11), (-1, diffs, 13), (1, diffs, 15), (-1, diffs, 17)]))
    mxx = plus(sx, xx)
    myy = plus(sy, plus(edge_xy, edge_yz))
    mzz = plus(sz, plus(edge_xz, edge_yz))
    mxy = total([(1, sums, 7), (-1, sums, 9)])
    mxz = total([(1, sums, 11), (-1, sums, 13)])
    myz = total([(1, sums, 15), (-1, sums, 17)])
    return zeroth, (mx, my, mz), (mxx, myy, mzz, mxy, mxz, myz)


def flow_moments(populations):
    sums = {q: populations[q] + populations[q + 1] for q in range(1, 19, 2)}
    diffs = {q: populations[q] - populations[q + 1] for q in range(1, 19, 2)}
    rho = populations[0]
    for q in range(1, 19, 2):
        rho = rho + sums[q]
    jx = (diffs[1] + diffs[7]) + (diffs[9] + diffs[11]) + diffs[13]
    jy = (diffs[3] + diffs[7]) + (diffs[15] - diffs[9]) + diffs[17]
    jz = (diffs[5] + diffs[11]) + (diffs[15] - diffs[13]) - diffs[17]
    return rho, (jx, jy, jz)


def dot3(a, b):
    return a[0] * b[0] + a[1] * b[1] + a[2] * b[2]


def second_times(second, v):
    mxx, myy, mzz, mxy, mxz, myz = second

    def row(terms):
        value = None
        for coefficient, component in terms:
            if coefficient is None:
                continue
            product = coefficient * component
            value = product if value is None else value + product
        return value

    return (
        row([(mxx, v[0]), (mxy, v[1]), (mxz, v[2])]),
        row([(mxy, v[0]), (myy, v[1]), (myz, v[2])]),
        row([(mxz, v[0]), (myz, v[1]), (mzz, v[2])]),
    )


def alpha_beta(moments, flow, flow_mass):
    zeroth, first, second = moments
    scale = flow_mass * (-1.6 / 36.0)
    alpha = scale * 3.0 * dot3(first, flow)
    beta = scale * (9.0 * dot3(second_times(second, flow), flow) - 3.0 * zeroth * dot3(flow, flow))
    return alpha, beta


def rows_of(x):
    return pl.ds(pl.multiple_of(x * 8, 8), 8) if not isinstance(x, int) else slice(x * 8, x * 8 + 8)


def y_sides():
    return ((YM, 7), (YP, 0))


def pack_z(directions, adjoint, coefficients, out, lines, strips, faces, coarse, semaphores):
    core, side = lax.axis_index("gz"), lax.axis_index("gy")
    copies = [pltpu.make_async_copy(coefficients, coarse, semaphores.at[0])]
    for k in range(5):
        q = ZM[k] + core * (ZP[k] - ZM[k])
        copies.append(pltpu.make_async_copy(adjoint.at[q], faces.at[k], semaphores.at[1 + k]))
    for n in range(directions):
        for k in range(5):
            q = YM[k] + (side if directions == 1 else n) * (YP[k] - YM[k])
            slot = 5 * n + k
            copies.append(
                pltpu.make_async_copy(adjoint.at[q], strips.at[slot], semaphores.at[6 + slot])
            )
    for copy in copies:
        copy.start()
    lanes = iota(1)
    count = coefficients.shape[2]
    copies[0].wait()
    out[2] = jnp.zeros((8, 128), f32)
    out[3] = jnp.zeros((8, 128), f32)
    for j in range(2):
        out[2 + j, :, 0:count] = coarse[:, j, :]
    lines[...] = jnp.dot(
        jnp.concatenate([out[2], out[3]], axis=0),
        jnp.concatenate([basis_along_z(count), jnp.zeros((128 - count, 128), f32)], axis=0),
        precision=highest,
        preferred_element_type=f32,
    )
    for copy in copies[1:]:
        copy.wait()
    for which, source in enumerate((127, 0)):

        @pl.when(core == which)
        def _():
            chains = {}
            for k in range(5):
                for x in range(32):
                    group, lane = divmod(k * 32 + x, 128)
                    column = pltpu.roll(faces[k, x].astype(f32), (lane - source) % 128, 1)
                    chain = group, lane // 16
                    if chain in chains:
                        column = jnp.where(lanes >= lane, column, chains[chain])
                    chains[chain] = column
            for group in range(2):
                tile = chains[group, 0]
                for part in range(1, 8 if group == 0 else 2):
                    tile = jnp.where(lanes >= part * 16, chains[group, part], tile)
                out[group] = tile


def pack_y(directions, strips, sent, lines, *refs):
    outs_y, outs_yz, plane = refs[:directions], refs[directions:-1], refs[-1]
    core, side = lax.axis_index("gz"), lax.axis_index("gy")
    lanes = lax.broadcasted_iota(jnp.int32, (32, 128), 1)

    def emit(components, row, j, first, out, out_yz):
        edges = {}
        for k, q in enumerate(components):
            for x in range(32):
                plane[k, x * 8 : x * 8 + 8, :] = strips[first + k, x].astype(f32)
        for k, q in enumerate(components):
            rows = plane[k, pl.ds(row, 32, stride=8), :]
            step = VELOCITY[q][2]
            if step:
                rows = pltpu.roll(rows, 127 if step > 0 else 1, 1)
                edge = lanes == (127 if step > 0 else 0)
                edges[step] = jnp.where(edge, rows, 0.0)
                rows = jnp.where(edge, 0.0, rows)
            out[k * 32 : k * 32 + 32, :] = rows.astype(bf16)
        out_yz[0:32, :] = jnp.where(core == 1, edges[1], edges[-1])
        out_yz[32:40, :] = sent[2 + j]
        line = lines[8 * j : 8 * j + 8, :]
        high = line.astype(bf16)
        out[LINE_ROWS:STRIP, :] = jnp.concatenate(
            [high, (line - high.astype(f32)).astype(bf16)], axis=0
        )

    for n, (components, row) in enumerate(y_sides()):
        if directions == 1:
            work = functools.partial(emit, components, row, 1 - n, 0, outs_y[0], outs_yz[0])
            pl.when(side == n)(work)
        else:
            emit(components, row, 1 - n, 5 * n, outs_y[n], outs_yz[n])


def add_rim(line, coarse, core, count):
    rim = jnp.sum(jnp.where(iota(1) == core * (count - 1), coarse, 0.0), axis=1, keepdims=True)
    return line + rim * rim_along_z(core, count)


def pull_zy(
    count, adjoint, forward_far, kind_far, received, own_lines,
    pulled, flows, lines, kind, columns, forward, semaphores,
):
    copies = [
        pltpu.make_async_copy(
            forward_far.at[:, pl.ds(8 * n, 8)], forward.at[:, pl.ds(8 * n, 8)], semaphores.at[n]
        )
        for n in range(4)
    ]
    copies.append(pltpu.make_async_copy(kind_far, kind, semaphores.at[4]))
    for copy in copies:
        copy.start()
    core = lax.axis_index("gz")
    load_columns(core, received, columns)
    for j in range(2):
        lines[8 * j : 8 * j + 8, :] = add_rim(
            own_lines[8 * j : 8 * j + 8, :], received[2 + j], core, count
        )
    sublanes = iota(0)

    def step(x, carry):
        for q in range(19):
            tile = pulled_z(q, adjoint[q, x].astype(f32), x, columns)
            step_y = VELOCITY[q][1]
            if step_y > 0:
                tile = jnp.where(sublanes == 7, 0.0, pltpu.roll(tile, 7, 0))
            elif step_y < 0:
                tile = jnp.where(sublanes == 0, 0.0, pltpu.roll(tile, 1, 0))
            pulled[q, rows_of(x), :] = tile
        return carry

    def flow(x, carry):
        rho, mass = flow_moments([forward[q, x].astype(f32) for q in range(19)])
        inverse = 1.0 / rho
        for n in range(3):
            flows[n, x] = mass[n] * inverse
        flows[MASS, x] = jnp.where(kind[x] == 0, rho, 0.0)
        flows[INVERSE, x] = inverse
        return carry

    lax.fori_loop(0, 32, step, 0, unroll=4)
    copies[4].wait()
    for n in range(4):
        copies[n].wait()
        lax.fori_loop(8 * n, 8 * n + 8, flow, 0, unroll=4)


def pack_x(directions, count, unpatched, flows, lines, *refs):
    received = list(zip(refs[:directions], refs[directions : 2 * directions]))
    pulled, *outs, edges, levels, extra = refs[2 * directions :]
    core = lax.axis_index("gz")
    del unpatched
    side = lax.axis_index("gy")
    place = lax.rem(lax.axis_index("gx"), SLOTS)

    def patch(components, row, buffers):
        strip, edge = buffers
        for k, q in enumerate(components):
            rows = strip[k * 32 : k * 32 + 32, :].astype(f32)
            step = VELOCITY[q][2]
            if step:
                rows = rows + jnp.where(core == (0 if step > 0 else 1), edge[0:32, :], 0.0)
            pulled[q, pl.ds(row, 32, stride=8), :] = rows

    def outer_line(buffers):
        strip, edge = buffers
        parts = strip[LINE_ROWS:STRIP, :].astype(f32)
        return add_rim(parts[0:8] + parts[8:16], edge[32:40, :], core, count)

    if directions == 1:
        pl.when(side == 0)(lambda: patch(YP, 7, received[0]))
        pl.when(side == 1)(lambda: patch(YM, 0, received[0]))
        outer = [(outer_line(received[0]), basis_along_y(jnp.where(side == 0, 2.0, -1.0)))]
    else:
        patch(YM, 0, received[0])
        patch(YP, 7, received[1])
        outer = [(outer_line(received[0]), basis_along_y(-1)), (outer_line(received[1]), basis_along_y(2))]
    terms = [(lines[0:8, :], basis_along_y(0)), (lines[8:16, :], basis_along_y(1))] + outer
    for n, (line, _) in enumerate(terms):
        extra[n * 8 : n * 8 + 8, :] = line
    for i in range(8):
        level = None
        for n, (_, weight) in enumerate(terms):
            term = weight * jnp.broadcast_to(extra[n * 8 + i : n * 8 + i + 1, :], (8, 128))
            level = term if level is None else level + term
        levels[i] = level

    def put(slot, low, high):
        for n, out in enumerate(outs):
            out[slot] = jnp.where(place == n, high, low).astype(bf16)

    def put_split(slot, low, high):
        put(slot, low, high)
        put(slot + 2, low - low.astype(bf16).astype(f32), high - high.astype(bf16).astype(f32))

    for k in range(5):
        put(FACE + k, pulled[XP[k], rows_of(0), :], pulled[XM[k], rows_of(31), :])
    for n in range(4):
        put(FIELD + n, flows[n, 0], flows[n, 31])
    for n in range(2):
        put_split(LEVEL + n, levels[n], levels[7 - n])
    results = []
    for x in EDGE_PLANES:
        values = {}
        for q in range(19):
            target = x + VELOCITY[q][0]
            if 0 <= target < 32:
                values[q] = pulled[q, rows_of(target), :]
        flow = tuple(flows[n, x] for n in range(3))
        results.append(alpha_beta(pair_moments(values), flow, flows[MASS, x]))
    for away in range(4):
        for n in range(2):
            low, high = results[away][n], results[7 - away][n]
            edges[n, away] = low
            edges[n, 7 - away] = high
            if away == 0:
                put_split(NEAR + n, low, high)
            else:
                put(FAR + 2 * (away - 1) + n, low, high)


def slope_of(bent):
    return -1.8 * (1.0 - bent * bent)


def bent_level(around, position):
    value = None
    for shift, level in zip((-1, 0, 1), around):
        term = float(spline(position - 4.0 * shift - 1.5)) * level
        value = term if value is None else value + term
    return jnp.tanh(4.0 * value)


def weight_of(position, shift):
    return float(spline(position - 4.0 * shift - 1.5))


def prior_fields(bent, here, flow, inverse, moments):
    zeroth, first, second = moments
    fluid = here == 0
    retained = 0.55 + 0.45 * bent
    share = jnp.where(fluid, retained, 1.0)
    speed = tuple(share * component for component in flow)
    curved = second_times(second, speed)
    slopes = tuple(3.0 * first[n] + 9.0 * curved[n] - 3.0 * zeroth * speed[n] for n in range(3))
    along = dot3(slopes, flow)
    value = zeroth + 0.5 * (3.0 * dot3(first, speed) + dot3(slopes, speed))
    factor = jnp.where(
        fluid, (1.6 / 36.0) * retained, jnp.where(here == 3, inverse * (1.0 / 36.0), 0.0)
    )
    base = jnp.where(fluid, (1.6 / 36.0) * value, 0.0) - factor * along
    return (base,) + tuple(factor * slope for slope in slopes), along


def emit_prior(stage, slot, here, values, result):
    solid = here == 1
    keep = jnp.where(here == 0, -0.6, 0.0)
    base, bx, by, bz = result
    shifts = {}
    for step_x in (-1, 0, 1):
        row = base if step_x == 0 else (base + bx if step_x > 0 else base - bx)
        for step_y in (-1, 0, 1):
            both = row if step_y == 0 else (row + by if step_y > 0 else row - by)
            shifts[step_x, step_y] = both
    for q in range(19):
        step_x, step_y, step_z = VELOCITY[q]
        shift = shifts[step_x, step_y]
        if step_z:
            shift = shift + bz if step_z > 0 else shift - bz
        kept = jnp.where(solid, values[OPPOSITE[q]], keep * values[q])
        stage[q, slot] = (kept + shift).astype(bf16)


def collide_inside(pulled, flows, kind, levels, out, totals, stage, semaphores):
    totals[...] = jnp.zeros((8, 8, 128), f32)

    def middle(with_prior, block, carry):
        around = [levels[block - 1], levels[block], levels[block + 1]]
        sums = [None] * 3
        for position in range(4):
            x = block * 4 + position
            bent = bent_level(around, position)
            flow = tuple(flows[n, x] for n in range(3))
            values = {q: pulled[q, rows_of(x + VELOCITY[q][0]), :] for q in range(19)}
            moments = pair_moments(values)
            if with_prior:
                result, along = prior_fields(bent, kind[x], flow, flows[INVERSE, x], moments)
                emit_prior(stage, x - 4, kind[x], values, result)
                sensitivity = (-1.6 / 36.0) * flows[MASS, x] * along
            else:
                alpha, beta = alpha_beta(moments, flow, flows[MASS, x])
                sensitivity = alpha + (0.55 + 0.45 * bent) * beta
            sensitivity = sensitivity * slope_of(bent)
            for n in range(3):
                term = weight_of(position, n - 1) * sensitivity
                sums[n] = term if sums[n] is None else sums[n] + term
        for n in range(3):
            totals[block + n - 1] += sums[n]
        return carry

    copies = []
    for part in range(INNER // 8):
        lax.fori_loop(1 + 2 * part, 3 + 2 * part, functools.partial(middle, True), 0)
        copies.append(
            pltpu.make_async_copy(
                stage.at[:, pl.ds(8 * part, 8)], out.at[:, pl.ds(4 + 8 * part, 8)], semaphores.at[part]
            )
        )
        copies[part].start()
    lax.fori_loop(1 + INNER // 4, 7, functools.partial(middle, False), 0)
    for copy in copies:
        copy.wait()


def along_x(received):
    place = lax.axis_index("gx")
    has_low, has_high = place > 0, place < lax.axis_size("gx") - 1
    turn = lax.rem(place, SLOTS)

    def reader(present, first):
        def read(slot):
            value = received[first][slot].astype(f32)
            for n in range(1, SLOTS):
                value = jnp.where(turn == n, received[(n + first) % SLOTS][slot].astype(f32), value)
            return jnp.where(present, value, 0.0)

        return read

    return reader(has_low, SLOTS - 1), reader(has_high, 0)


def levels_along_x(read):
    return [read(LEVEL + n) + read(LEVEL + 2 + n) for n in range(2)]


def fold_rows(tiles, weight):
    sublanes = iota(0)
    tiles = [weight * tile for tile in tiles]
    for bit in (4, 2, 1):
        half = len(tiles) // 2
        tiles = [
            jnp.where(
                sublanes & bit == 0,
                tiles[i] + pltpu.roll(tiles[i], 8 - bit, 0),
                tiles[i + half] + pltpu.roll(tiles[i + half], bit, 0),
            )
            for i in range(half)
        ]
    return tiles[0]


def project(count, pulled, flows, edges, levels, *refs):
    inner, folded, handed = refs[SLOTS:]
    core = lax.axis_index("gz")
    low, high = along_x(refs[:SLOTS])
    totals = [inner[i] for i in range(8)]
    lower = levels_along_x(low)[::-1] + [levels[i] for i in range(3)]
    upper = [levels[i] for i in range(5, 8)] + levels_along_x(high)

    def add(block, position, alpha, beta):
        start = block + 1 if block < 4 else block - 6
        around = (lower if block < 4 else upper)[start : start + 3]
        bent = bent_level(around, position)
        sensitivity = (alpha + (0.55 + 0.45 * bent) * beta) * slope_of(bent)
        for shift in (-1, 0, 1):
            if 0 <= block + shift < 8:
                totals[block + shift] = totals[block + shift] + weight_of(position, shift) * sensitivity

    def faces(ref, components):
        return pair_moments({q: ref(FACE + k) for k, q in enumerate(components)})

    def own(x, components):
        return pair_moments({q: pulled[q, rows_of(x), :] for q in components})

    def flow_at(x):
        return tuple(flows[n, x] for n in range(3))

    missing = {
        (0, 0): alpha_beta(faces(low, XM), flow_at(0), flows[MASS, 0]),
        (7, 3): alpha_beta(faces(high, XP), flow_at(31), flows[MASS, 31]),
        (-1, 3): alpha_beta(own(0, XP), tuple(low(FIELD + n) for n in range(3)), low(FIELD + 3)),
        (8, 0): alpha_beta(own(31, XM), tuple(high(FIELD + n) for n in range(3)), high(FIELD + 3)),
    }
    for block in (-1, 0, 7, 8):
        for position in range(4):
            if block in (0, 7):
                index = position + (4 if block else 0)
                alpha, beta = edges[0, index], edges[1, index]
            else:
                ref, away = (low, 3 - position) if block < 0 else (high, position)
                alpha, beta = (
                    ref(NEAR + n) + ref(NEAR + 2 + n) if away == 0 else ref(FAR + 2 * (away - 1) + n)
                    for n in range(2)
                )
            if (block, position) in missing:
                more = missing[block, position]
                alpha, beta = alpha + more[0], beta + more[1]
            add(block, position, alpha, beta)
    lanes = iota(1)
    rim_z = rim_along_z(core, count)
    for j in range(4):
        sums = fold_rows(totals, basis_along_y(j - 1))
        folded[8 * j : 8 * j + 8, :] = sums
        across = jnp.sum(sums * rim_z, axis=1, keepdims=True)
        handed[j] = jnp.where(lanes == core * (count - 1), across, 0.0)
        if j in (0, 3):
            handed[4 + j // 3] = sums


def collide_outside(pulled, flows, kind, levels, *refs):
    out, stage, semaphores = refs[SLOTS + 1 :]
    low, high = along_x(refs[:SLOTS])
    first = 4 + INNER

    def emit(x, slot, around, position, values):
        flow = tuple(flows[n, x] for n in range(3))
        result, _ = prior_fields(
            bent_level(around, position), kind[x], flow, flows[INVERSE, x], pair_moments(values)
        )
        emit_prior(stage, slot, kind[x], values, result)

    def middle(block, carry):
        around = [levels[block - 1], levels[block], levels[block + 1]]
        for position in range(4):
            x = block * 4 + position
            values = {q: pulled[q, rows_of(x + VELOCITY[q][0]), :] for q in range(19)}
            emit(x, x - first + 4, around, position, values)
        return carry

    def edge(x, around):
        values = {}
        for q in range(19):
            target = x + VELOCITY[q][0]
            if target < 0:
                values[q] = low(FACE + XM.index(q))
            elif target > 31:
                values[q] = high(FACE + XP.index(q))
            else:
                values[q] = pulled[q, rows_of(target), :]
        emit(x, x if x < 4 else x - first + 4, around, x % 4, values)

    lowest = [levels_along_x(low)[0], levels[0], levels[1]]
    highest_levels = [levels[6], levels[7], levels_along_x(high)[0]]
    lax.fori_loop(1 + INNER // 4, 7, middle, 0)
    for x in range(28, 32):
        edge(x, highest_levels)
    copies = [
        pltpu.make_async_copy(
            stage.at[:, pl.ds(4, 32 - first)], out.at[:, pl.ds(first, 32 - first)], semaphores.at[0]
        ),
        pltpu.make_async_copy(stage.at[:, pl.ds(0, 4)], out.at[:, pl.ds(0, 4)], semaphores.at[1]),
    ]
    copies[0].start()
    for x in range(4):
        edge(x, lowest)
    copies[1].start()
    for copy in copies:
        copy.wait()


def relay(directions, taken, handed, *outs):
    if directions == 1:
        side = lax.axis_index("gy")
        outs[0][0] = taken[5 - side]
        outs[0][1] = handed[3 - 3 * side]
    else:
        for n in range(2):
            outs[n][0] = taken[5 - n]
            outs[n][1] = handed[3 - 3 * n]


def finish(folded, rims, *refs):
    others, out = refs[:-1], refs[-1]
    count = out.shape[2]
    if len(others) == 1:
        side = lax.axis_index("gy")
        from_low = [jnp.where(side == 1, others[0][n], 0.0) for n in range(2)]
        from_high = [jnp.where(side == 0, others[0][n], 0.0) for n in range(2)]
    else:
        from_low, from_high = [[other[n] for n in range(2)] for other in others]
    sums = jnp.concatenate([folded[8:16, :] + from_low[0], folded[16:24, :] + from_high[0]], axis=0)
    result = lax.dot_general(
        sums,
        basis_along_z(count),
        (((1,), (1,)), ((), ())),
        precision=highest,
        preferred_element_type=f32,
    )
    out[:, 0, :] = result[0:8] + (rims[1] + from_low[1])[:, 0:count]
    out[:, 1, :] = result[8:16] + (rims[2] + from_high[1])[:, 0:count]


def pairs(count, slot):
    partner = {}
    for i in range(slot, count - 1, SLOTS):
        partner[i], partner[i + 1] = i + 1, i
    result = []
    for i in range(count):
        for core in range(2):
            target = (partner[i], core) if i in partner else (i, 1 - core)
            result.append((i * 2 + core, target[0] * 2 + target[1]))
    return result


def per_device(forward, adjoint, coefficients, kind):
    count_y = lax.axis_size("gy")
    count_x = lax.axis_size("gx")
    swap = [(0, 1), (1, 0)]
    side = lax.axis_index("gy")
    directions = 1 if count_y == 2 else 2
    tile = (8, 128)
    shape = jax.ShapeDtypeStruct
    count = coefficients.shape[2]
    up = [(i, i + 1) for i in range(count_y - 1)]
    down = [(i + 1, i) for i in range(count_y - 1)]

    strips = shape((5 * directions,) + adjoint.shape[1:], bf16)
    sent_z, lines, strips = kernel_call(
        functools.partial(pack_z, directions),
        [shape((4,) + tile, f32), shape((16, 128), f32), strips],
        [
            pltpu.VMEM((5,) + adjoint.shape[1:], bf16),
            pltpu.VMEM(coefficients.shape, f32),
            pltpu.SemaphoreType.DMA((6 + 5 * directions,)),
        ],
        in_specs=[pl.BlockSpec(memory_space=pltpu.HBM)] * 2,
    )(*(pltpu.with_memory_space_constraint(a, pltpu.HBM) for a in (adjoint, coefficients)))
    sent = kernel_call(
        functools.partial(pack_y, directions),
        [shape((STRIP, 128), bf16)] * directions + [shape((40, 128), f32)] * directions,
        [pltpu.VMEM((5, 256, 128), f32)],
    )(strips, sent_z, lines)
    received_z = lax.ppermute(sent_z, "gz", swap)
    routes = [swap] if directions == 1 else [up, down]
    crossed = [
        [(a * 2 + core, b * 2 + 1 - core) for a, b in route for core in range(2)] for route in routes
    ]
    received_y = [lax.ppermute(sent[n], "gy", route) for n, route in enumerate(routes)]
    received_yz = [
        lax.ppermute(sent[directions + n], ("gy", "gz"), route) for n, route in enumerate(crossed)
    ]

    pulled, flows, lines, kind = kernel_call(
        functools.partial(pull_zy, count),
        [
            shape((19, 256, 128), f32),
            shape((5,) + kind.shape, f32),
            shape((16, 128), f32),
            shape(kind.shape, jnp.int32),
        ],
        [
            pltpu.VMEM((2, 2) + tile, f32),
            pltpu.VMEM(forward.shape, bf16),
            pltpu.SemaphoreType.DMA((5,)),
        ],
        in_specs=[
            pl.BlockSpec(memory_space=pltpu.HBM if n in (1, 2) else pltpu.VMEM) for n in range(5)
        ],
    )(
        adjoint,
        pltpu.with_memory_space_constraint(forward, pltpu.HBM),
        pltpu.with_memory_space_constraint(kind, pltpu.HBM),
        received_z,
        lines,
    )

    pulled, *sent_x, edges, levels = kernel_call(
        functools.partial(pack_x, directions, count),
        [pulled]
        + [shape((BUNDLE,) + tile, bf16)] * SLOTS
        + [shape((2, 8) + tile, f32), shape((8,) + tile, f32)],
        [pltpu.VMEM((32, 128), f32)],
        aliases={0: 0},
    )(pulled, flows, lines, *received_y, *received_yz)
    received_x = [
        lax.ppermute(sent, ("gx", "gz"), pairs(count_x, slot)) for slot, sent in enumerate(sent_x)
    ]

    prior, totals = kernel_call(
        collide_inside,
        [shape(adjoint.shape, bf16), shape((8,) + tile, f32)],
        [pltpu.VMEM((19, INNER) + tile, bf16), pltpu.SemaphoreType.DMA((INNER // 8,))],
        out_specs=[pl.BlockSpec(memory_space=pltpu.HBM), pl.BlockSpec(memory_space=pltpu.VMEM)],
    )(pulled, flows, kind, levels)
    folded, handed = kernel_call(
        functools.partial(project, count), [shape((32, 128), f32), shape((6,) + tile, f32)]
    )(pulled, flows, edges, levels, *received_x, totals)
    taken = lax.ppermute(handed, "gz", swap)
    relayed = kernel_call(
        functools.partial(relay, directions), [shape((2,) + tile, f32)] * directions
    )(taken, handed)
    crossed = [[(a * 2 + c, b * 2 + 1 - c) for a, b in route for c in range(2)] for route in routes]
    others = [lax.ppermute(sent, ("gy", "gz"), route) for sent, route in zip(relayed, crossed)]
    in_hbm = pl.BlockSpec(memory_space=pltpu.HBM)
    prior = kernel_call(
        collide_outside,
        shape(adjoint.shape, bf16),
        [pltpu.VMEM((19, 32 - INNER) + tile, bf16), pltpu.SemaphoreType.DMA((2,))],
        aliases={4 + SLOTS: 0},
        in_specs=[pl.BlockSpec(memory_space=pltpu.VMEM)] * (4 + SLOTS) + [in_hbm],
        out_specs=in_hbm,
    )(pulled, flows, kind, levels, *received_x, prior)
    gradient = kernel_call(finish, shape(coefficients.shape, f32))(
        folded, taken, *others
    )
    return prior, gradient


def solution(mesh):
    in_specs = (
        P(None, ("parts", "gx"), "gy", "gz"),
        P(None, ("parts", "gx"), "gy", "gz"),
        P(("parts", "gx"), "gy", "gz"),
        P(("parts", "gx"), "gy", "gz"),
    )
    out_specs = (P(None, ("parts", "gx"), "gy", "gz"), P(("parts", "gx"), "gy", "gz"))
    return jax.shard_map(
        per_device, mesh=mesh, in_specs=in_specs, out_specs=out_specs, check_vma=False
    )
```

```python
import functools

import jax
import jax.numpy as jnp
import numpy as np
from jax import lax
from jax.experimental import pallas as pl
from jax.experimental.pallas import tpu as pltpu
from jax.sharding import PartitionSpec as P

VELOCITY = (
    (0, 0, 0),
    (1, 0, 0),
    (-1, 0, 0),
    (0, 1, 0),
    (0, -1, 0),
    (0, 0, 1),
    (0, 0, -1),
    (1, 1, 0),
    (-1, -1, 0),
    (1, -1, 0),
    (-1, 1, 0),
    (1, 0, 1),
    (-1, 0, -1),
    (1, 0, -1),
    (-1, 0, 1),
    (0, 1, 1),
    (0, -1, -1),
    (0, 1, -1),
    (0, -1, 1),
)
OPPOSITE = (0, 2, 1, 4, 3, 6, 5, 8, 7, 10, 9, 12, 11, 14, 13, 16, 15, 18, 17)
highest = lax.Precision.HIGHEST
f32 = jnp.float32
bf16 = jnp.bfloat16


def going(dimension, sign):
    return [q for q in range(19) if VELOCITY[q][dimension] == sign]


XP, XM = going(0, 1), going(0, -1)
YP, YM = going(1, 1), going(1, -1)
ZP, ZM = going(2, 1), going(2, -1)

FACE, NEAR, FAR, FIELD, LEVEL, BUNDLE = 0, 5, 9, 15, 19, 23
SLOTS = 3
LINE_ROWS, STRIP = 160, 176
MASS, INVERSE = 3, 4
EDGE_PLANES = (0, 1, 2, 3, 28, 29, 30, 31)
INNER = 16


def spline(distance):
    radius = np.abs(distance) / 6.0
    return np.where(radius < 1.0, (1.0 - radius) ** 4 * (1.0 + 4.0 * radius), 0.0)


def spline_along(dimension, shape, position):
    distance = lax.broadcasted_iota(jnp.int32, shape, dimension).astype(f32) - position
    radius = jnp.abs(distance) * (1.0 / 6.0)
    square = (1.0 - radius) * (1.0 - radius)
    return jnp.where(radius < 1.0, square * square * (1.0 + 4.0 * radius), 0.0)


def basis_along_z(count):
    places = lax.broadcasted_iota(jnp.int32, (count, 128), 0).astype(f32)
    return spline_along(1, (count, 128), 4.0 * places + 1.5)


def rim_along_z(core, count):
    return spline_along(1, (8, 128), jnp.where(core == 0, 4.0 * count + 1.5, -2.5))


def basis_along_y(j):
    return spline_along(0, (8, 128), 4.0 * j + 1.5)


def kernel_call(body, out_shape, scratch_shapes=(), aliases=None, **specs):
    return pl.pallas_call(
        body,
        out_shape=out_shape,
        scratch_shapes=list(scratch_shapes),
        compiler_params=pltpu.CompilerParams(vmem_limit_bytes=12 * 1024 * 1024),
        input_output_aliases=aliases or {},
        **specs,
    )


def iota(dimension):
    return lax.broadcasted_iota(jnp.int32, (8, 128), dimension)


def pulled_z(q, tile, x, columns):
    step = VELOCITY[q][2]
    if step == 0:
        return tile
    slot = (ZP if step > 0 else ZM).index(q) * 32
    group, lane = slot // 128, slot % 128
    lanes = iota(1)
    edge = columns[0 if step > 0 else 1, group]
    if step > 0:
        edge = pltpu.roll(edge, 127 - lane - x, 1)
        return jnp.where(lanes == 127, edge, pltpu.roll(tile, 127, 1))
    edge = pltpu.roll(edge, (128 - lane - x) & 127, 1)
    return jnp.where(lanes == 0, edge, pltpu.roll(tile, 1, 1))


def load_columns(core, received, columns):
    for group in range(2):
        tile = received[group]
        columns[0, group] = jnp.where(core == 0, tile, 0.0)
        columns[1, group] = jnp.where(core == 1, tile, 0.0)


def pair_moments(populations):
    sums, diffs = {}, {}
    for q in range(1, 19, 2):
        a, b = populations.get(q), populations.get(q + 1)
        if a is None and b is None:
            continue
        if b is None:
            sums[q], diffs[q] = a, a
        elif a is None:
            sums[q], diffs[q] = b, -b
        else:
            sums[q], diffs[q] = a + b, a - b

    def total(terms):
        value = None
        for sign, table, q in terms:
            if q not in table:
                continue
            item = table[q]
            if value is None:
                value = item if sign > 0 else -item
            else:
                value = value + item if sign > 0 else value - item
        return value

    def plus(a, b):
        return b if a is None else (a if b is None else a + b)

    def twice(a):
        return None if a is None else a + a

    xx = total([(1, sums, 7), (1, sums, 9), (1, sums, 11), (1, sums, 13)])
    edge_yz = total([(1, sums, 15), (1, sums, 17)])
    edge_xy = total([(1, sums, 7), (1, sums, 9)])
    edge_xz = total([(1, sums, 11), (1, sums, 13)])
    sx, sy, sz = (twice(sums.get(q)) for q in (1, 3, 5))
    zeroth = plus(plus(xx, edge_yz), plus(plus(sx, sy), sz))
    if 0 in populations:
        zeroth = zeroth + 12.0 * populations[0]
    mx = plus(twice(diffs.get(1)), total([(1, diffs, 7), (1, diffs, 9), (1, diffs, 11), (1, diffs, 13)]))
    my = plus(twice(diffs.get(3)), total([(1, diffs, 7), (-1, diffs, 9), (1, diffs, 15), (1, diffs, 17)]))
    mz = plus(twice(diffs.get(5)), total([(1, diffs, 11), (-1, diffs, 13), (1, diffs, 15), (-1, diffs, 17)]))
    mxx = plus(sx, xx)
    myy = plus(sy, plus(edge_xy, edge_yz))
    mzz = plus(sz, plus(edge_xz, edge_yz))
    mxy = total([(1, sums, 7), (-1, sums, 9)])
    mxz = total([(1, sums, 11), (-1, sums, 13)])
    myz = total([(1, sums, 15), (-1, sums, 17)])
    return zeroth, (mx, my, mz), (mxx, myy, mzz, mxy, mxz, myz)


def flow_moments(populations):
    sums = {q: populations[q] + populations[q + 1] for q in range(1, 19, 2)}
    diffs = {q: populations[q] - populations[q + 1] for q in range(1, 19, 2)}
    rho = populations[0]
    for q in range(1, 19, 2):
        rho = rho + sums[q]
    jx = (diffs[1] + diffs[7]) + (diffs[9] + diffs[11]) + diffs[13]
    jy = (diffs[3] + diffs[7]) + (diffs[15] - diffs[9]) + diffs[17]
    jz = (diffs[5] + diffs[11]) + (diffs[15] - diffs[13]) - diffs[17]
    return rho, (jx, jy, jz)


def dot3(a, b):
    return a[0] * b[0] + a[1] * b[1] + a[2] * b[2]


def second_times(second, v):
    mxx, myy, mzz, mxy, mxz, myz = second

    def row(terms):
        value = None
        for coefficient, component in terms:
            if coefficient is None:
                continue
            product = coefficient * component
            value = product if value is None else value + product
        return value

    return (
        row([(mxx, v[0]), (mxy, v[1]), (mxz, v[2])]),
        row([(mxy, v[0]), (myy, v[1]), (myz, v[2])]),
        row([(mxz, v[0]), (myz, v[1]), (mzz, v[2])]),
    )


def alpha_beta(moments, flow, flow_mass):
    zeroth, first, second = moments
    scale = flow_mass * (-1.6 / 36.0)
    alpha = scale * 3.0 * dot3(first, flow)
    beta = scale * (9.0 * dot3(second_times(second, flow), flow) - 3.0 * zeroth * dot3(flow, flow))
    return alpha, beta


def rows_of(x):
    return pl.ds(pl.multiple_of(x * 8, 8), 8) if not isinstance(x, int) else slice(x * 8, x * 8 + 8)


def y_sides():
    return ((YM, 7), (YP, 0))


def pack_rows(directions, adjoint, coefficients, out, lines, coarse, strips, near, plane, semaphores):
    side = lax.axis_index("gy")
    copies = [pltpu.make_async_copy(coefficients, near, semaphores.at[0])]
    for n in range(directions):
        for k in range(5):
            q = YM[k] + (side if directions == 1 else n) * (YP[k] - YM[k])
            slot = 5 * n + k
            copies.append(
                pltpu.make_async_copy(adjoint.at[q], strips.at[slot], semaphores.at[1 + slot])
            )
    for copy in copies:
        copy.start()
    count = coefficients.shape[2]
    copies[0].wait()
    coarse[...] = jnp.zeros((2, 8, 128), f32)
    for j in range(2):
        coarse[j, :, 0:count] = near[:, j, :]
    line = jnp.dot(
        jnp.concatenate([coarse[0], coarse[1]], axis=0),
        jnp.concatenate([basis_along_z(count), jnp.zeros((128 - count, 128), f32)], axis=0),
        precision=highest,
        preferred_element_type=f32,
    )
    lines[...] = line
    high = line.astype(bf16)
    first = LINE_ROWS * directions
    out[first : first + 16, :] = high
    out[first + 16 : first + 32, :] = (line - high.astype(f32)).astype(bf16)
    for copy in copies[1:]:
        copy.wait()

    def emit(row, n):
        for k in range(5 * n, 5 * n + 5):
            for x in range(32):
                plane[k - 5 * n, x * 8 : x * 8 + 8, :] = strips[k, x].astype(f32)
        for k in range(5 * n, 5 * n + 5):
            out[k * 32 : k * 32 + 32, :] = plane[k - 5 * n, pl.ds(row, 32, stride=8), :].astype(bf16)

    for n, (_, row) in enumerate(y_sides()):
        if directions == 1:
            pl.when(side == n)(functools.partial(emit, row, 0))
        else:
            emit(row, n)


def pack_z(adjoint, coarse, out):
    core = lax.axis_index("gz")
    lanes = iota(1)
    for j in range(2):
        out[2 + j] = coarse[j]
    for which, (components, source) in enumerate(((ZM, 127), (ZP, 0))):

        @pl.when(core == which)
        def _():
            chains = {}
            for k, q in enumerate(components):
                for x in range(32):
                    group, lane = divmod(k * 32 + x, 128)
                    column = pltpu.roll(adjoint[q, x].astype(f32), (lane - source) % 128, 1)
                    chain = group, lane // 16
                    if chain in chains:
                        column = jnp.where(lanes >= lane, column, chains[chain])
                    chains[chain] = column
            for group in range(2):
                tile = chains[group, 0]
                for part in range(1, 8 if group == 0 else 2):
                    tile = jnp.where(lanes >= part * 16, chains[group, part], tile)
                out[group] = tile


def pack_y(directions, count, own, taken, coarse, *outs):
    core, side = lax.axis_index("gz"), lax.axis_index("gy")
    lanes = lax.broadcasted_iota(jnp.int32, (32, 128), 1)

    def emit(components, j, n, out):
        for k, q in enumerate(components):
            place = slice((5 * n + k) * 32, (5 * n + k) * 32 + 32)
            step = VELOCITY[q][2]
            if not step:
                out[k * 32 : k * 32 + 32, :] = taken[place, :]
                continue
            shift, edge, holder = (127, 127, 1) if step > 0 else (1, 0, 0)
            rows = pltpu.roll(taken[place, :].astype(f32), shift, 1)
            border = jnp.where(core == holder, pltpu.roll(own[place, :].astype(f32), shift, 1), 0.0)
            out[k * 32 : k * 32 + 32, :] = jnp.where(lanes == edge, border, rows).astype(bf16)
        first = LINE_ROWS * directions
        line = taken[first : first + 16, :].astype(f32) + taken[first + 16 : first + 32, :].astype(f32)
        line = add_rim(line[8 * j : 8 * j + 8, :], coarse[j], 1 - core, count)
        high = line.astype(bf16)
        out[LINE_ROWS:STRIP, :] = jnp.concatenate(
            [high, (line - high.astype(f32)).astype(bf16)], axis=0
        )

    for n, (components, _) in enumerate(y_sides()):
        if directions == 1:
            pl.when(side == n)(functools.partial(emit, components, 1 - n, 0, outs[0]))
        else:
            emit(components, 1 - n, n, outs[n])


def add_rim(line, coarse, core, count):
    rim = jnp.sum(jnp.where(iota(1) == core * (count - 1), coarse, 0.0), axis=1, keepdims=True)
    return line + rim * rim_along_z(core, count)


def pull_zy(
    count, adjoint, forward_far, kind_far, received, own_lines,
    pulled, flows, lines, kind, columns, forward, semaphores,
):
    copies = [
        pltpu.make_async_copy(
            forward_far.at[:, pl.ds(8 * n, 8)], forward.at[:, pl.ds(8 * n, 8)], semaphores.at[n]
        )
        for n in range(4)
    ]
    copies.append(pltpu.make_async_copy(kind_far, kind, semaphores.at[4]))
    for copy in copies:
        copy.start()
    core = lax.axis_index("gz")
    load_columns(core, received, columns)
    for j in range(2):
        lines[8 * j : 8 * j + 8, :] = add_rim(
            own_lines[8 * j : 8 * j + 8, :], received[2 + j], core, count
        )
    sublanes = iota(0)

    def step(x, carry):
        for q in range(19):
            tile = pulled_z(q, adjoint[q, x].astype(f32), x, columns)
            step_y = VELOCITY[q][1]
            if step_y > 0:
                tile = jnp.where(sublanes == 7, 0.0, pltpu.roll(tile, 7, 0))
            elif step_y < 0:
                tile = jnp.where(sublanes == 0, 0.0, pltpu.roll(tile, 1, 0))
            pulled[q, rows_of(x), :] = tile
        return carry

    def flow(x, carry):
        rho, mass = flow_moments([forward[q, x].astype(f32) for q in range(19)])
        inverse = 1.0 / rho
        for n in range(3):
            flows[n, x] = mass[n] * inverse
        flows[MASS, x] = jnp.where(kind[x] == 0, rho, 0.0)
        flows[INVERSE, x] = inverse
        return carry

    lax.fori_loop(0, 32, step, 0, unroll=4)
    copies[4].wait()
    for n in range(4):
        copies[n].wait()
        lax.fori_loop(8 * n, 8 * n + 8, flow, 0, unroll=4)


def pack_x(directions, unpatched, flows, lines, *refs):
    received = refs[:directions]
    pulled, *outs, edges, levels, extra = refs[directions:]
    del unpatched
    side = lax.axis_index("gy")
    place = lax.rem(lax.axis_index("gx"), SLOTS)

    def patch(components, row, strip):
        for k, q in enumerate(components):
            pulled[q, pl.ds(row, 32, stride=8), :] = strip[k * 32 : k * 32 + 32, :].astype(f32)

    def outer_line(strip):
        parts = strip[LINE_ROWS:STRIP, :].astype(f32)
        return parts[0:8] + parts[8:16]

    if directions == 1:
        pl.when(side == 0)(lambda: patch(YP, 7, received[0]))
        pl.when(side == 1)(lambda: patch(YM, 0, received[0]))
        outer = [(outer_line(received[0]), basis_along_y(jnp.where(side == 0, 2.0, -1.0)))]
    else:
        patch(YM, 0, received[0])
        patch(YP, 7, received[1])
        outer = [(outer_line(received[0]), basis_along_y(-1)), (outer_line(received[1]), basis_along_y(2))]
    terms = [(lines[0:8, :], basis_along_y(0)), (lines[8:16, :], basis_along_y(1))] + outer
    for n, (line, _) in enumerate(terms):
        extra[n * 8 : n * 8 + 8, :] = line
    for i in range(8):
        level = None
        for n, (_, weight) in enumerate(terms):
            term = weight * jnp.broadcast_to(extra[n * 8 + i : n * 8 + i + 1, :], (8, 128))
            level = term if level is None else level + term
        levels[i] = level

    def put(slot, low, high):
        for n, out in enumerate(outs):
            out[slot] = jnp.where(place == n, high, low).astype(bf16)

    def put_split(slot, low, high):
        put(slot, low, high)
        put(slot + 2, low - low.astype(bf16).astype(f32), high - high.astype(bf16).astype(f32))

    for k in range(5):
        put(FACE + k, pulled[XP[k], rows_of(0), :], pulled[XM[k], rows_of(31), :])
    for n in range(4):
        put(FIELD + n, flows[n, 0], flows[n, 31])
    for n in range(2):
        put_split(LEVEL + n, levels[n], levels[7 - n])
    results = []
    for x in EDGE_PLANES:
        values = {}
        for q in range(19):
            target = x + VELOCITY[q][0]
            if 0 <= target < 32:
                values[q] = pulled[q, rows_of(target), :]
        flow = tuple(flows[n, x] for n in range(3))
        results.append(alpha_beta(pair_moments(values), flow, flows[MASS, x]))
    for away in range(4):
        for n in range(2):
            low, high = results[away][n], results[7 - away][n]
            edges[n, away] = low
            edges[n, 7 - away] = high
            if away == 0:
                put_split(NEAR + n, low, high)
            else:
                put(FAR + 2 * (away - 1) + n, low, high)


def slope_of(bent):
    return -1.8 * (1.0 - bent * bent)


def bent_level(around, position):
    value = None
    for shift, level in zip((-1, 0, 1), around):
        term = float(spline(position - 4.0 * shift - 1.5)) * level
        value = term if value is None else value + term
    return jnp.tanh(4.0 * value)


def weight_of(position, shift):
    return float(spline(position - 4.0 * shift - 1.5))


def prior_fields(bent, here, flow, inverse, moments):
    zeroth, first, second = moments
    fluid = here == 0
    retained = 0.55 + 0.45 * bent
    share = jnp.where(fluid, retained, 1.0)
    speed = tuple(share * component for component in flow)
    curved = second_times(second, speed)
    slopes = tuple(3.0 * first[n] + 9.0 * curved[n] - 3.0 * zeroth * speed[n] for n in range(3))
    along = dot3(slopes, flow)
    value = zeroth + 0.5 * (3.0 * dot3(first, speed) + dot3(slopes, speed))
    factor = jnp.where(
        fluid, (1.6 / 36.0) * retained, jnp.where(here == 3, inverse * (1.0 / 36.0), 0.0)
    )
    base = jnp.where(fluid, (1.6 / 36.0) * value, 0.0) - factor * along
    return (base,) + tuple(factor * slope for slope in slopes), along


def emit_prior(stage, slot, here, values, result):
    solid = here == 1
    keep = jnp.where(here == 0, -0.6, 0.0)
    base, bx, by, bz = result
    shifts = {}
    for step_x in (-1, 0, 1):
        row = base if step_x == 0 else (base + bx if step_x > 0 else base - bx)
        for step_y in (-1, 0, 1):
            both = row if step_y == 0 else (row + by if step_y > 0 else row - by)
            shifts[step_x, step_y] = both
    for q in range(19):
        step_x, step_y, step_z = VELOCITY[q]
        shift = shifts[step_x, step_y]
        if step_z:
            shift = shift + bz if step_z > 0 else shift - bz
        kept = jnp.where(solid, values[OPPOSITE[q]], keep * values[q])
        stage[q, slot] = (kept + shift).astype(bf16)


def collide_inside(pulled, flows, kind, levels, out, totals, stage, semaphores):
    totals[...] = jnp.zeros((8, 8, 128), f32)

    def middle(with_prior, block, carry):
        around = [levels[block - 1], levels[block], levels[block + 1]]
        sums = [None] * 3
        for position in range(4):
            x = block * 4 + position
            bent = bent_level(around, position)
            flow = tuple(flows[n, x] for n in range(3))
            values = {q: pulled[q, rows_of(x + VELOCITY[q][0]), :] for q in range(19)}
            moments = pair_moments(values)
            if with_prior:
                result, along = prior_fields(bent, kind[x], flow, flows[INVERSE, x], moments)
                emit_prior(stage, x - 4, kind[x], values, result)
                sensitivity = (-1.6 / 36.0) * flows[MASS, x] * along
            else:
                alpha, beta = alpha_beta(moments, flow, flows[MASS, x])
                sensitivity = alpha + (0.55 + 0.45 * bent) * beta
            sensitivity = sensitivity * slope_of(bent)
            for n in range(3):
                term = weight_of(position, n - 1) * sensitivity
                sums[n] = term if sums[n] is None else sums[n] + term
        for n in range(3):
            totals[block + n - 1] += sums[n]
        return carry

    copies = []
    for part in range(INNER // 8):
        lax.fori_loop(1 + 2 * part, 3 + 2 * part, functools.partial(middle, True), 0)
        copies.append(
            pltpu.make_async_copy(
                stage.at[:, pl.ds(8 * part, 8)], out.at[:, pl.ds(4 + 8 * part, 8)], semaphores.at[part]
            )
        )
        copies[part].start()
    lax.fori_loop(1 + INNER // 4, 7, functools.partial(middle, False), 0)
    for copy in copies:
        copy.wait()


def along_x(received):
    place = lax.axis_index("gx")
    has_low, has_high = place > 0, place < lax.axis_size("gx") - 1
    turn = lax.rem(place, SLOTS)

    def reader(present, first):
        def read(slot):
            value = received[first][slot].astype(f32)
            for n in range(1, SLOTS):
                value = jnp.where(turn == n, received[(n + first) % SLOTS][slot].astype(f32), value)
            return jnp.where(present, value, 0.0)

        return read

    return reader(has_low, SLOTS - 1), reader(has_high, 0)


def levels_along_x(read):
    return [read(LEVEL + n) + read(LEVEL + 2 + n) for n in range(2)]


def fold_rows(tiles, weight):
    sublanes = iota(0)
    tiles = [weight * tile for tile in tiles]
    for bit in (4, 2, 1):
        half = len(tiles) // 2
        tiles = [
            jnp.where(
                sublanes & bit == 0,
                tiles[i] + pltpu.roll(tiles[i], 8 - bit, 0),
                tiles[i + half] + pltpu.roll(tiles[i + half], bit, 0),
            )
            for i in range(half)
        ]
    return tiles[0]


def project(count, pulled, flows, edges, levels, *refs):
    inner, folded, handed = refs[SLOTS:]
    core = lax.axis_index("gz")
    low, high = along_x(refs[:SLOTS])
    totals = [inner[i] for i in range(8)]
    lower = levels_along_x(low)[::-1] + [levels[i] for i in range(3)]
    upper = [levels[i] for i in range(5, 8)] + levels_along_x(high)

    def add(block, position, alpha, beta):
        start = block + 1 if block < 4 else block - 6
        around = (lower if block < 4 else upper)[start : start + 3]
        bent = bent_level(around, position)
        sensitivity = (alpha + (0.55 + 0.45 * bent) * beta) * slope_of(bent)
        for shift in (-1, 0, 1):
            if 0 <= block + shift < 8:
                totals[block + shift] = totals[block + shift] + weight_of(position, shift) * sensitivity

    def faces(ref, components):
        return pair_moments({q: ref(FACE + k) for k, q in enumerate(components)})

    def own(x, components):
        return pair_moments({q: pulled[q, rows_of(x), :] for q in components})

    def flow_at(x):
        return tuple(flows[n, x] for n in range(3))

    missing = {
        (0, 0): alpha_beta(faces(low, XM), flow_at(0), flows[MASS, 0]),
        (7, 3): alpha_beta(faces(high, XP), flow_at(31), flows[MASS, 31]),
        (-1, 3): alpha_beta(own(0, XP), tuple(low(FIELD + n) for n in range(3)), low(FIELD + 3)),
        (8, 0): alpha_beta(own(31, XM), tuple(high(FIELD + n) for n in range(3)), high(FIELD + 3)),
    }
    for block in (-1, 0, 7, 8):
        for position in range(4):
            if block in (0, 7):
                index = position + (4 if block else 0)
                alpha, beta = edges[0, index], edges[1, index]
            else:
                ref, away = (low, 3 - position) if block < 0 else (high, position)
                alpha, beta = (
                    ref(NEAR + n) + ref(NEAR + 2 + n) if away == 0 else ref(FAR + 2 * (away - 1) + n)
                    for n in range(2)
                )
            if (block, position) in missing:
                more = missing[block, position]
                alpha, beta = alpha + more[0], beta + more[1]
            add(block, position, alpha, beta)
    lanes = iota(1)
    rim_z = rim_along_z(core, count)
    for j in range(4):
        sums = fold_rows(totals, basis_along_y(j - 1))
        folded[8 * j : 8 * j + 8, :] = sums
        across = jnp.sum(sums * rim_z, axis=1, keepdims=True)
        handed[j] = jnp.where(lanes == core * (count - 1), across, 0.0)
        if j in (0, 3):
            handed[4 + j // 3] = sums


def collide_outside(pulled, flows, kind, levels, *refs):
    out, stage, semaphores = refs[SLOTS + 1 :]
    low, high = along_x(refs[:SLOTS])
    first = 4 + INNER

    def emit(x, slot, around, position, values):
        flow = tuple(flows[n, x] for n in range(3))
        result, _ = prior_fields(
            bent_level(around, position), kind[x], flow, flows[INVERSE, x], pair_moments(values)
        )
        emit_prior(stage, slot, kind[x], values, result)

    def middle(block, carry):
        around = [levels[block - 1], levels[block], levels[block + 1]]
        for position in range(4):
            x = block * 4 + position
            values = {q: pulled[q, rows_of(x + VELOCITY[q][0]), :] for q in range(19)}
            emit(x, x - first + 4, around, position, values)
        return carry

    def edge(x, around):
        values = {}
        for q in range(19):
            target = x + VELOCITY[q][0]
            if target < 0:
                values[q] = low(FACE + XM.index(q))
            elif target > 31:
                values[q] = high(FACE + XP.index(q))
            else:
                values[q] = pulled[q, rows_of(target), :]
        emit(x, x if x < 4 else x - first + 4, around, x % 4, values)

    lowest = [levels_along_x(low)[0], levels[0], levels[1]]
    highest_levels = [levels[6], levels[7], levels_along_x(high)[0]]
    lax.fori_loop(1 + INNER // 4, 7, middle, 0)
    for x in range(28, 32):
        edge(x, highest_levels)
    copies = [
        pltpu.make_async_copy(
            stage.at[:, pl.ds(4, 32 - first)], out.at[:, pl.ds(first, 32 - first)], semaphores.at[0]
        ),
        pltpu.make_async_copy(stage.at[:, pl.ds(0, 4)], out.at[:, pl.ds(0, 4)], semaphores.at[1]),
    ]
    copies[0].start()
    for x in range(4):
        edge(x, lowest)
    copies[1].start()
    for copy in copies:
        copy.wait()


def relay(directions, taken, handed, *outs):
    if directions == 1:
        side = lax.axis_index("gy")
        outs[0][0] = taken[5 - side]
        outs[0][1] = handed[3 - 3 * side]
    else:
        for n in range(2):
            outs[n][0] = taken[5 - n]
            outs[n][1] = handed[3 - 3 * n]


def finish(folded, rims, *refs):
    others, out = refs[:-1], refs[-1]
    count = out.shape[2]
    if len(others) == 1:
        side = lax.axis_index("gy")
        from_low = [jnp.where(side == 1, others[0][n], 0.0) for n in range(2)]
        from_high = [jnp.where(side == 0, others[0][n], 0.0) for n in range(2)]
    else:
        from_low, from_high = [[other[n] for n in range(2)] for other in others]
    sums = jnp.concatenate([folded[8:16, :] + from_low[0], folded[16:24, :] + from_high[0]], axis=0)
    result = lax.dot_general(
        sums,
        basis_along_z(count),
        (((1,), (1,)), ((), ())),
        precision=highest,
        preferred_element_type=f32,
    )
    out[:, 0, :] = result[0:8] + (rims[1] + from_low[1])[:, 0:count]
    out[:, 1, :] = result[8:16] + (rims[2] + from_high[1])[:, 0:count]


def pairs(count, slot):
    partner = {}
    for i in range(slot, count - 1, SLOTS):
        partner[i], partner[i + 1] = i + 1, i
    result = []
    for i in range(count):
        for core in range(2):
            target = (partner[i], core) if i in partner else (i, 1 - core)
            result.append((i * 2 + core, target[0] * 2 + target[1]))
    return result


def per_device(forward, adjoint, coefficients, kind):
    count_y = lax.axis_size("gy")
    count_x = lax.axis_size("gx")
    swap = [(0, 1), (1, 0)]
    side = lax.axis_index("gy")
    directions = 1 if count_y == 2 else 2
    tile = (8, 128)
    shape = jax.ShapeDtypeStruct
    count = coefficients.shape[2]
    up = [(i, i + 1) for i in range(count_y - 1)]
    down = [(i + 1, i) for i in range(count_y - 1)]

    routes = [swap] if directions == 1 else [up, down]
    crossed = [[(a * 2 + c, b * 2 + 1 - c) for a, b in route for c in range(2)] for route in routes]

    own, lines, coarse = kernel_call(
        functools.partial(pack_rows, directions),
        [
            shape((LINE_ROWS * directions + 32, 128), bf16),
            shape((16, 128), f32),
            shape((2,) + tile, f32),
        ],
        [
            pltpu.VMEM((5 * directions,) + adjoint.shape[1:], bf16),
            pltpu.VMEM(coefficients.shape, f32),
            pltpu.VMEM((5, 256, 128), f32),
            pltpu.SemaphoreType.DMA((1 + 5 * directions,)),
        ],
        in_specs=[pl.BlockSpec(memory_space=pltpu.HBM)] * 2,
    )(*(pltpu.with_memory_space_constraint(a, pltpu.HBM) for a in (adjoint, coefficients)))
    taken_rows = lax.ppermute(own, "gz", swap)
    sent_z = kernel_call(pack_z, shape((4,) + tile, f32))(adjoint, coarse)
    received_z = lax.ppermute(sent_z, "gz", swap)
    sent_y = kernel_call(
        functools.partial(pack_y, directions, count), [shape((STRIP, 128), bf16)] * directions
    )(own, taken_rows, coarse)
    received_y = [lax.ppermute(sent, ("gy", "gz"), route) for sent, route in zip(sent_y, crossed)]

    pulled, flows, lines, kind = kernel_call(
        functools.partial(pull_zy, count),
        [
            shape((19, 256, 128), f32),
            shape((5,) + kind.shape, f32),
            shape((16, 128), f32),
            shape(kind.shape, jnp.int32),
        ],
        [
            pltpu.VMEM((2, 2) + tile, f32),
            pltpu.VMEM(forward.shape, bf16),
            pltpu.SemaphoreType.DMA((5,)),
        ],
        cost_estimate=pl.CostEstimate(flops=10**10, bytes_accessed=10**7, transcendentals=0),
        in_specs=[
            pl.BlockSpec(memory_space=pltpu.HBM if n in (1, 2) else pltpu.VMEM) for n in range(5)
        ],
    )(
        adjoint,
        pltpu.with_memory_space_constraint(forward, pltpu.HBM),
        pltpu.with_memory_space_constraint(kind, pltpu.HBM),
        received_z,
        lines,
    )

    pulled, *sent_x, edges, levels = kernel_call(
        functools.partial(pack_x, directions),
        [pulled]
        + [shape((BUNDLE,) + tile, bf16)] * SLOTS
        + [shape((2, 8) + tile, f32), shape((8,) + tile, f32)],
        [pltpu.VMEM((32, 128), f32)],
        aliases={0: 0},
    )(pulled, flows, lines, *received_y)
    received_x = [
        lax.ppermute(sent, ("gx", "gz"), pairs(count_x, slot)) for slot, sent in enumerate(sent_x)
    ]

    prior, totals = kernel_call(
        collide_inside,
        [shape(adjoint.shape, bf16), shape((8,) + tile, f32)],
        [pltpu.VMEM((19, INNER) + tile, bf16), pltpu.SemaphoreType.DMA((INNER // 8,))],
        out_specs=[pl.BlockSpec(memory_space=pltpu.HBM), pl.BlockSpec(memory_space=pltpu.VMEM)],
    )(pulled, flows, kind, levels)
    folded, handed = kernel_call(
        functools.partial(project, count), [shape((32, 128), f32), shape((6,) + tile, f32)]
    )(pulled, flows, edges, levels, *received_x, totals)
    taken = lax.ppermute(handed, "gz", swap)
    relayed = kernel_call(
        functools.partial(relay, directions), [shape((2,) + tile, f32)] * directions
    )(taken, handed)
    others = [lax.ppermute(sent, ("gy", "gz"), route) for sent, route in zip(relayed, crossed)]
    in_hbm = pl.BlockSpec(memory_space=pltpu.HBM)
    prior = kernel_call(
        collide_outside,
        shape(adjoint.shape, bf16),
        [pltpu.VMEM((19, 32 - INNER) + tile, bf16), pltpu.SemaphoreType.DMA((2,))],
        aliases={4 + SLOTS: 0},
        in_specs=[pl.BlockSpec(memory_space=pltpu.VMEM)] * (4 + SLOTS) + [in_hbm],
        out_specs=in_hbm,
    )(pulled, flows, kind, levels, *received_x, prior)
    gradient = kernel_call(finish, shape(coefficients.shape, f32))(
        folded, taken, *others
    )
    return prior, gradient


def solution(mesh):
    in_specs = (
        P(None, ("parts", "gx"), "gy", "gz"),
        P(None, ("parts", "gx"), "gy", "gz"),
        P(("parts", "gx"), "gy", "gz"),
        P(("parts", "gx"), "gy", "gz"),
    )
    out_specs = (P(None, ("parts", "gx"), "gy", "gz"), P(("parts", "gx"), "gy", "gz"))
    return jax.shard_map(
        per_device, mesh=mesh, in_specs=in_specs, out_specs=out_specs, check_vma=False
    )
```

```python
import functools

import jax
import jax.numpy as jnp
import numpy as np
from jax import lax
from jax.experimental import pallas as pl
from jax.experimental.pallas import tpu as pltpu
from jax.sharding import PartitionSpec as P

VELOCITY = (
    (0, 0, 0),
    (1, 0, 0),
    (-1, 0, 0),
    (0, 1, 0),
    (0, -1, 0),
    (0, 0, 1),
    (0, 0, -1),
    (1, 1, 0),
    (-1, -1, 0),
    (1, -1, 0),
    (-1, 1, 0),
    (1, 0, 1),
    (-1, 0, -1),
    (1, 0, -1),
    (-1, 0, 1),
    (0, 1, 1),
    (0, -1, -1),
    (0, 1, -1),
    (0, -1, 1),
)
OPPOSITE = (0, 2, 1, 4, 3, 6, 5, 8, 7, 10, 9, 12, 11, 14, 13, 16, 15, 18, 17)
highest = lax.Precision.HIGHEST
f32 = jnp.float32
bf16 = jnp.bfloat16


def going(dimension, sign):
    return [q for q in range(19) if VELOCITY[q][dimension] == sign]


XP, XM = going(0, 1), going(0, -1)
YP, YM = going(1, 1), going(1, -1)
ZP, ZM = going(2, 1), going(2, -1)

FACE, NEAR, FAR, FIELD, LEVEL, BUNDLE = 0, 5, 9, 15, 19, 23
SLOTS = 3
LINE_ROWS, STRIP = 160, 176
MASS, INVERSE = 3, 4
EDGE_PLANES = (0, 1, 2, 3, 28, 29, 30, 31)
INNER = 16


def spline(distance):
    radius = np.abs(distance) / 6.0
    return np.where(radius < 1.0, (1.0 - radius) ** 4 * (1.0 + 4.0 * radius), 0.0)


def spline_along(dimension, shape, position):
    distance = lax.broadcasted_iota(jnp.int32, shape, dimension).astype(f32) - position
    radius = jnp.abs(distance) * (1.0 / 6.0)
    square = (1.0 - radius) * (1.0 - radius)
    return jnp.where(radius < 1.0, square * square * (1.0 + 4.0 * radius), 0.0)


def basis_along_z(count):
    places = lax.broadcasted_iota(jnp.int32, (count, 128), 0).astype(f32)
    return spline_along(1, (count, 128), 4.0 * places + 1.5)


def rim_along_z(core, count):
    return spline_along(1, (8, 128), jnp.where(core == 0, 4.0 * count + 1.5, -2.5))


def basis_along_y(j):
    return spline_along(0, (8, 128), 4.0 * j + 1.5)


def kernel_call(body, out_shape, scratch_shapes=(), aliases=None, **specs):
    return pl.pallas_call(
        body,
        out_shape=out_shape,
        scratch_shapes=list(scratch_shapes),
        compiler_params=pltpu.CompilerParams(vmem_limit_bytes=12 * 1024 * 1024),
        input_output_aliases=aliases or {},
        **specs,
    )


def iota(dimension):
    return lax.broadcasted_iota(jnp.int32, (8, 128), dimension)


def pulled_z(q, tile, x, columns):
    step = VELOCITY[q][2]
    if step == 0:
        return tile
    slot = (ZP if step > 0 else ZM).index(q) * 32
    group, lane = slot // 128, slot % 128
    lanes = iota(1)
    edge = columns[0 if step > 0 else 1, group]
    if step > 0:
        edge = pltpu.roll(edge, 127 - lane - x, 1)
        return jnp.where(lanes == 127, edge, pltpu.roll(tile, 127, 1))
    edge = pltpu.roll(edge, (128 - lane - x) & 127, 1)
    return jnp.where(lanes == 0, edge, pltpu.roll(tile, 1, 1))


def load_columns(core, received, columns):
    for group in range(2):
        tile = received[group]
        columns[0, group] = jnp.where(core == 0, tile, 0.0)
        columns[1, group] = jnp.where(core == 1, tile, 0.0)


def pair_moments(populations):
    sums, diffs = {}, {}
    for q in range(1, 19, 2):
        a, b = populations.get(q), populations.get(q + 1)
        if a is None and b is None:
            continue
        if b is None:
            sums[q], diffs[q] = a, a
        elif a is None:
            sums[q], diffs[q] = b, -b
        else:
            sums[q], diffs[q] = a + b, a - b

    def total(terms):
        value = None
        for sign, table, q in terms:
            if q not in table:
                continue
            item = table[q]
            if value is None:
                value = item if sign > 0 else -item
            else:
                value = value + item if sign > 0 else value - item
        return value

    def plus(a, b):
        return b if a is None else (a if b is None else a + b)

    def twice(a):
        return None if a is None else a + a

    xx = total([(1, sums, 7), (1, sums, 9), (1, sums, 11), (1, sums, 13)])
    edge_yz = total([(1, sums, 15), (1, sums, 17)])
    edge_xy = total([(1, sums, 7), (1, sums, 9)])
    edge_xz = total([(1, sums, 11), (1, sums, 13)])
    sx, sy, sz = (twice(sums.get(q)) for q in (1, 3, 5))
    zeroth = plus(plus(xx, edge_yz), plus(plus(sx, sy), sz))
    if 0 in populations:
        zeroth = zeroth + 12.0 * populations[0]
    mx = plus(twice(diffs.get(1)), total([(1, diffs, 7), (1, diffs, 9), (1, diffs, 11), (1, diffs, 13)]))
    my = plus(twice(diffs.get(3)), total([(1, diffs, 7), (-1, diffs, 9), (1, diffs, 15), (1, diffs, 17)]))
    mz = plus(twice(diffs.get(5)), total([(1, diffs, 11), (-1, diffs, 13), (1, diffs, 15), (-1, diffs, 17)]))
    mxx = plus(sx, xx)
    myy = plus(sy, plus(edge_xy, edge_yz))
    mzz = plus(sz, plus(edge_xz, edge_yz))
    mxy = total([(1, sums, 7), (-1, sums, 9)])
    mxz = total([(1, sums, 11), (-1, sums, 13)])
    myz = total([(1, sums, 15), (-1, sums, 17)])
    return zeroth, (mx, my, mz), (mxx, myy, mzz, mxy, mxz, myz)


def flow_moments(populations):
    sums = {q: populations[q] + populations[q + 1] for q in range(1, 19, 2)}
    diffs = {q: populations[q] - populations[q + 1] for q in range(1, 19, 2)}
    rho = populations[0]
    for q in range(1, 19, 2):
        rho = rho + sums[q]
    jx = (diffs[1] + diffs[7]) + (diffs[9] + diffs[11]) + diffs[13]
    jy = (diffs[3] + diffs[7]) + (diffs[15] - diffs[9]) + diffs[17]
    jz = (diffs[5] + diffs[11]) + (diffs[15] - diffs[13]) - diffs[17]
    return rho, (jx, jy, jz)


def dot3(a, b):
    return a[0] * b[0] + a[1] * b[1] + a[2] * b[2]


def second_times(second, v):
    mxx, myy, mzz, mxy, mxz, myz = second

    def row(terms):
        value = None
        for coefficient, component in terms:
            if coefficient is None:
                continue
            product = coefficient * component
            value = product if value is None else value + product
        return value

    return (
        row([(mxx, v[0]), (mxy, v[1]), (mxz, v[2])]),
        row([(mxy, v[0]), (myy, v[1]), (myz, v[2])]),
        row([(mxz, v[0]), (myz, v[1]), (mzz, v[2])]),
    )


def alpha_beta(moments, flow, flow_mass):
    zeroth, first, second = moments
    scale = flow_mass * (-1.6 / 36.0)
    alpha = scale * 3.0 * dot3(first, flow)
    beta = scale * (9.0 * dot3(second_times(second, flow), flow) - 3.0 * zeroth * dot3(flow, flow))
    return alpha, beta


def rows_of(x):
    return pl.ds(pl.multiple_of(x * 8, 8), 8) if not isinstance(x, int) else slice(x * 8, x * 8 + 8)


def y_sides():
    return ((YM, 7), (YP, 0))


def pack_rows(directions, adjoint, coefficients, out, lines, coarse, strips, near, plane, semaphores):
    side = lax.axis_index("gy")
    copies = [pltpu.make_async_copy(coefficients, near, semaphores.at[0])]
    for n in range(directions):
        for k in range(5):
            q = YM[k] + (side if directions == 1 else n) * (YP[k] - YM[k])
            slot = 5 * n + k
            copies.append(
                pltpu.make_async_copy(adjoint.at[q], strips.at[slot], semaphores.at[1 + slot])
            )
    for copy in copies:
        copy.start()
    count = coefficients.shape[2]
    copies[0].wait()
    coarse[...] = jnp.zeros((2, 8, 128), f32)
    for j in range(2):
        coarse[j, :, 0:count] = near[:, j, :]
    line = jnp.dot(
        jnp.concatenate([coarse[0], coarse[1]], axis=0),
        jnp.concatenate([basis_along_z(count), jnp.zeros((128 - count, 128), f32)], axis=0),
        precision=highest,
        preferred_element_type=f32,
    )
    lines[...] = line
    high = line.astype(bf16)
    first = LINE_ROWS * directions
    out[first : first + 16, :] = high
    out[first + 16 : first + 32, :] = (line - high.astype(f32)).astype(bf16)
    for copy in copies[1:]:
        copy.wait()

    def emit(row, n):
        for k in range(5 * n, 5 * n + 5):
            for x in range(32):
                plane[k - 5 * n, x * 8 : x * 8 + 8, :] = strips[k, x].astype(f32)
        for k in range(5 * n, 5 * n + 5):
            out[k * 32 : k * 32 + 32, :] = plane[k - 5 * n, pl.ds(row, 32, stride=8), :].astype(bf16)

    for n, (_, row) in enumerate(y_sides()):
        if directions == 1:
            pl.when(side == n)(functools.partial(emit, row, 0))
        else:
            emit(row, n)


def pack_z(adjoint, coarse, out):
    core = lax.axis_index("gz")
    lanes = iota(1)
    for j in range(2):
        out[2 + j] = coarse[j]
    for which, (components, source) in enumerate(((ZM, 127), (ZP, 0))):

        @pl.when(core == which)
        def _():
            chains = {}
            for k, q in enumerate(components):
                for x in range(32):
                    group, lane = divmod(k * 32 + x, 128)
                    column = pltpu.roll(adjoint[q, x].astype(f32), (lane - source) % 128, 1)
                    chain = group, lane // 16
                    if chain in chains:
                        column = jnp.where(lanes >= lane, column, chains[chain])
                    chains[chain] = column
            for group in range(2):
                tile = chains[group, 0]
                for part in range(1, 8 if group == 0 else 2):
                    tile = jnp.where(lanes >= part * 16, chains[group, part], tile)
                out[group] = tile


def pack_y(directions, count, own, taken, coarse, *outs):
    core, side = lax.axis_index("gz"), lax.axis_index("gy")
    lanes = lax.broadcasted_iota(jnp.int32, (32, 128), 1)

    def emit(components, j, n, out):
        for k, q in enumerate(components):
            place = slice((5 * n + k) * 32, (5 * n + k) * 32 + 32)
            step = VELOCITY[q][2]
            if not step:
                out[k * 32 : k * 32 + 32, :] = taken[place, :]
                continue
            shift, edge, holder = (127, 127, 1) if step > 0 else (1, 0, 0)
            rows = pltpu.roll(taken[place, :].astype(f32), shift, 1)
            border = jnp.where(core == holder, pltpu.roll(own[place, :].astype(f32), shift, 1), 0.0)
            out[k * 32 : k * 32 + 32, :] = jnp.where(lanes == edge, border, rows).astype(bf16)
        first = LINE_ROWS * directions
        line = taken[first : first + 16, :].astype(f32) + taken[first + 16 : first + 32, :].astype(f32)
        line = add_rim(line[8 * j : 8 * j + 8, :], coarse[j], 1 - core, count)
        high = line.astype(bf16)
        out[LINE_ROWS:STRIP, :] = jnp.concatenate(
            [high, (line - high.astype(f32)).astype(bf16)], axis=0
        )

    for n, (components, _) in enumerate(y_sides()):
        if directions == 1:
            pl.when(side == n)(functools.partial(emit, components, 1 - n, 0, outs[0]))
        else:
            emit(components, 1 - n, n, outs[n])


def add_rim(line, coarse, core, count):
    rim = jnp.sum(jnp.where(iota(1) == core * (count - 1), coarse, 0.0), axis=1, keepdims=True)
    return line + rim * rim_along_z(core, count)


def pull_zy(
    count, adjoint, forward_far, kind_far, received, own_lines,
    pulled, flows, lines, kind, columns, forward, semaphores,
):
    copies = [
        pltpu.make_async_copy(
            forward_far.at[:, pl.ds(8 * n, 8)], forward.at[:, pl.ds(8 * n, 8)], semaphores.at[n]
        )
        for n in range(4)
    ]
    copies.append(pltpu.make_async_copy(kind_far, kind, semaphores.at[4]))
    for copy in copies:
        copy.start()
    core = lax.axis_index("gz")
    load_columns(core, received, columns)
    for j in range(2):
        lines[8 * j : 8 * j + 8, :] = add_rim(
            own_lines[8 * j : 8 * j + 8, :], received[2 + j], core, count
        )
    sublanes = iota(0)

    def step(x, carry):
        for q in range(19):
            tile = pulled_z(q, adjoint[q, x].astype(f32), x, columns)
            step_y = VELOCITY[q][1]
            if step_y > 0:
                tile = jnp.where(sublanes == 7, 0.0, pltpu.roll(tile, 7, 0))
            elif step_y < 0:
                tile = jnp.where(sublanes == 0, 0.0, pltpu.roll(tile, 1, 0))
            pulled[q, rows_of(x), :] = tile
        return carry

    def flow(x, carry):
        rho, mass = flow_moments([forward[q, x].astype(f32) for q in range(19)])
        inverse = 1.0 / rho
        for n in range(3):
            flows[n, x] = mass[n] * inverse
        flows[MASS, x] = jnp.where(kind[x] == 0, rho, 0.0)
        flows[INVERSE, x] = inverse
        return carry

    lax.fori_loop(0, 32, step, 0, unroll=4)
    copies[4].wait()
    for n in range(4):
        copies[n].wait()
        lax.fori_loop(8 * n, 8 * n + 8, flow, 0, unroll=4)


def pack_x(directions, unpatched, flows, lines, *refs):
    received = refs[:directions]
    pulled, *outs, edges, levels, extra = refs[directions:]
    del unpatched
    side = lax.axis_index("gy")
    place = lax.rem(lax.axis_index("gx"), SLOTS)

    def patch(components, row, strip):
        for k, q in enumerate(components):
            pulled[q, pl.ds(row, 32, stride=8), :] = strip[k * 32 : k * 32 + 32, :].astype(f32)

    def outer_line(strip):
        parts = strip[LINE_ROWS:STRIP, :].astype(f32)
        return parts[0:8] + parts[8:16]

    if directions == 1:
        pl.when(side == 0)(lambda: patch(YP, 7, received[0]))
        pl.when(side == 1)(lambda: patch(YM, 0, received[0]))
        outer = [(outer_line(received[0]), basis_along_y(jnp.where(side == 0, 2.0, -1.0)))]
    else:
        patch(YM, 0, received[0])
        patch(YP, 7, received[1])
        outer = [(outer_line(received[0]), basis_along_y(-1)), (outer_line(received[1]), basis_along_y(2))]
    terms = [(lines[0:8, :], basis_along_y(0)), (lines[8:16, :], basis_along_y(1))] + outer
    for n, (line, _) in enumerate(terms):
        extra[n * 8 : n * 8 + 8, :] = line
    for i in range(8):
        level = None
        for n, (_, weight) in enumerate(terms):
            term = weight * jnp.broadcast_to(extra[n * 8 + i : n * 8 + i + 1, :], (8, 128))
            level = term if level is None else level + term
        levels[i] = level

    def put(slot, low, high):
        for n, out in enumerate(outs):
            out[slot] = jnp.where(place == n, high, low).astype(bf16)

    def put_split(slot, low, high):
        put(slot, low, high)
        put(slot + 2, low - low.astype(bf16).astype(f32), high - high.astype(bf16).astype(f32))

    for k in range(5):
        put(FACE + k, pulled[XP[k], rows_of(0), :], pulled[XM[k], rows_of(31), :])
    for n in range(4):
        put(FIELD + n, flows[n, 0], flows[n, 31])
    for n in range(2):
        put_split(LEVEL + n, levels[n], levels[7 - n])
    results = []
    for x in EDGE_PLANES:
        values = {}
        for q in range(19):
            target = x + VELOCITY[q][0]
            if 0 <= target < 32:
                values[q] = pulled[q, rows_of(target), :]
        flow = tuple(flows[n, x] for n in range(3))
        results.append(alpha_beta(pair_moments(values), flow, flows[MASS, x]))
    for away in range(4):
        for n in range(2):
            low, high = results[away][n], results[7 - away][n]
            edges[n, away] = low
            edges[n, 7 - away] = high
            if away == 0:
                put_split(NEAR + n, low, high)
            else:
                put(FAR + 2 * (away - 1) + n, low, high)


def slope_of(bent):
    return -1.8 * (1.0 - bent * bent)


def bent_level(around, position):
    value = None
    for shift, level in zip((-1, 0, 1), around):
        term = float(spline(position - 4.0 * shift - 1.5)) * level
        value = term if value is None else value + term
    return jnp.tanh(4.0 * value)


def weight_of(position, shift):
    return float(spline(position - 4.0 * shift - 1.5))


def prior_fields(bent, here, flow, inverse, moments):
    zeroth, first, second = moments
    fluid = here == 0
    retained = 0.55 + 0.45 * bent
    share = jnp.where(fluid, retained, 1.0)
    speed = tuple(share * component for component in flow)
    curved = second_times(second, speed)
    slopes = tuple(3.0 * first[n] + 9.0 * curved[n] - 3.0 * zeroth * speed[n] for n in range(3))
    along = dot3(slopes, flow)
    value = zeroth + 0.5 * (3.0 * dot3(first, speed) + dot3(slopes, speed))
    factor = jnp.where(
        fluid, (1.6 / 36.0) * retained, jnp.where(here == 3, inverse * (1.0 / 36.0), 0.0)
    )
    base = jnp.where(fluid, (1.6 / 36.0) * value, 0.0) - factor * along
    return (base,) + tuple(factor * slope for slope in slopes), along


def emit_prior(stage, slot, here, values, result):
    solid = here == 1
    keep = jnp.where(here == 0, -0.6, 0.0)
    base, bx, by, bz = result
    shifts = {}
    for step_x in (-1, 0, 1):
        row = base if step_x == 0 else (base + bx if step_x > 0 else base - bx)
        for step_y in (-1, 0, 1):
            both = row if step_y == 0 else (row + by if step_y > 0 else row - by)
            shifts[step_x, step_y] = both
    for q in range(19):
        step_x, step_y, step_z = VELOCITY[q]
        shift = shifts[step_x, step_y]
        if step_z:
            shift = shift + bz if step_z > 0 else shift - bz
        kept = jnp.where(solid, values[OPPOSITE[q]], keep * values[q])
        stage[q, slot] = (kept + shift).astype(bf16)


def collide_inside(pulled, flows, kind, levels, out, totals, stage, semaphores):
    totals[...] = jnp.zeros((8, 8, 128), f32)

    def middle(with_prior, block, carry):
        around = [levels[block - 1], levels[block], levels[block + 1]]
        sums = [None] * 3
        for position in range(4):
            x = block * 4 + position
            bent = bent_level(around, position)
            flow = tuple(flows[n, x] for n in range(3))
            values = {q: pulled[q, rows_of(x + VELOCITY[q][0]), :] for q in range(19)}
            moments = pair_moments(values)
            if with_prior:
                result, along = prior_fields(bent, kind[x], flow, flows[INVERSE, x], moments)
                emit_prior(stage, x - 4, kind[x], values, result)
                sensitivity = (-1.6 / 36.0) * flows[MASS, x] * along
            else:
                alpha, beta = alpha_beta(moments, flow, flows[MASS, x])
                sensitivity = alpha + (0.55 + 0.45 * bent) * beta
            sensitivity = sensitivity * slope_of(bent)
            for n in range(3):
                term = weight_of(position, n - 1) * sensitivity
                sums[n] = term if sums[n] is None else sums[n] + term
        for n in range(3):
            totals[block + n - 1] += sums[n]
        return carry

    copies = []
    for part in range(INNER // 8):
        lax.fori_loop(1 + 2 * part, 3 + 2 * part, functools.partial(middle, True), 0)
        copies.append(
            pltpu.make_async_copy(
                stage.at[:, pl.ds(8 * part, 8)], out.at[:, pl.ds(4 + 8 * part, 8)], semaphores.at[part]
            )
        )
        copies[part].start()
    lax.fori_loop(1 + INNER // 4, 7, functools.partial(middle, False), 0)
    for copy in copies:
        copy.wait()


def along_x(received):
    place = lax.axis_index("gx")
    has_low, has_high = place > 0, place < lax.axis_size("gx") - 1
    turn = lax.rem(place, SLOTS)

    def reader(present, first):
        def read(slot):
            value = received[first][slot].astype(f32)
            for n in range(1, SLOTS):
                value = jnp.where(turn == n, received[(n + first) % SLOTS][slot].astype(f32), value)
            return jnp.where(present, value, 0.0)

        return read

    return reader(has_low, SLOTS - 1), reader(has_high, 0)


def levels_along_x(read):
    return [read(LEVEL + n) + read(LEVEL + 2 + n) for n in range(2)]


def fold_rows(tiles, weight):
    sublanes = iota(0)
    tiles = [weight * tile for tile in tiles]
    for bit in (4, 2, 1):
        half = len(tiles) // 2
        tiles = [
            jnp.where(
                sublanes & bit == 0,
                tiles[i] + pltpu.roll(tiles[i], 8 - bit, 0),
                tiles[i + half] + pltpu.roll(tiles[i + half], bit, 0),
            )
            for i in range(half)
        ]
    return tiles[0]


def project(count, directions, pulled, flows, edges, levels, *refs):
    inner, folded, handed, kept = refs[SLOTS:]
    core = lax.axis_index("gz")
    low, high = along_x(refs[:SLOTS])
    totals = [inner[i] for i in range(8)]
    lower = levels_along_x(low)[::-1] + [levels[i] for i in range(3)]
    upper = [levels[i] for i in range(5, 8)] + levels_along_x(high)

    def add(block, position, alpha, beta):
        start = block + 1 if block < 4 else block - 6
        around = (lower if block < 4 else upper)[start : start + 3]
        bent = bent_level(around, position)
        sensitivity = (alpha + (0.55 + 0.45 * bent) * beta) * slope_of(bent)
        for shift in (-1, 0, 1):
            if 0 <= block + shift < 8:
                totals[block + shift] = totals[block + shift] + weight_of(position, shift) * sensitivity

    def faces(ref, components):
        return pair_moments({q: ref(FACE + k) for k, q in enumerate(components)})

    def own(x, components):
        return pair_moments({q: pulled[q, rows_of(x), :] for q in components})

    def flow_at(x):
        return tuple(flows[n, x] for n in range(3))

    missing = {
        (0, 0): alpha_beta(faces(low, XM), flow_at(0), flows[MASS, 0]),
        (7, 3): alpha_beta(faces(high, XP), flow_at(31), flows[MASS, 31]),
        (-1, 3): alpha_beta(own(0, XP), tuple(low(FIELD + n) for n in range(3)), low(FIELD + 3)),
        (8, 0): alpha_beta(own(31, XM), tuple(high(FIELD + n) for n in range(3)), high(FIELD + 3)),
    }
    for block in (-1, 0, 7, 8):
        for position in range(4):
            if block in (0, 7):
                index = position + (4 if block else 0)
                alpha, beta = edges[0, index], edges[1, index]
            else:
                ref, away = (low, 3 - position) if block < 0 else (high, position)
                alpha, beta = (
                    ref(NEAR + n) + ref(NEAR + 2 + n) if away == 0 else ref(FAR + 2 * (away - 1) + n)
                    for n in range(2)
                )
            if (block, position) in missing:
                more = missing[block, position]
                alpha, beta = alpha + more[0], beta + more[1]
            add(block, position, alpha, beta)
    lanes = iota(1)
    rim_z = rim_along_z(core, count)
    sums, rims = [], []
    for j in range(4):
        sums.append(fold_rows(totals, basis_along_y(j - 1)))
        across = jnp.sum(sums[j] * rim_z, axis=1, keepdims=True)
        rims.append(jnp.where(lanes == core * (count - 1), across, 0.0))
    for j in (1, 2):
        folded[8 * j - 8 : 8 * j, :] = sums[j]
        handed[j - 1] = rims[j]
    if directions == 1:
        upper = lax.axis_index("gy") == 0
        handed[2] = jnp.where(upper, sums[3], sums[0])
        kept[0] = jnp.where(upper, rims[3], rims[0])
    else:
        for n, j in enumerate((3, 0)):
            handed[2 + n] = sums[j]
            kept[n] = rims[j]


def collide_outside(pulled, flows, kind, levels, *refs):
    out, stage, semaphores = refs[SLOTS + 1 :]
    low, high = along_x(refs[:SLOTS])
    first = 4 + INNER

    def emit(x, slot, around, position, values):
        flow = tuple(flows[n, x] for n in range(3))
        result, _ = prior_fields(
            bent_level(around, position), kind[x], flow, flows[INVERSE, x], pair_moments(values)
        )
        emit_prior(stage, slot, kind[x], values, result)

    def middle(block, carry):
        around = [levels[block - 1], levels[block], levels[block + 1]]
        for position in range(4):
            x = block * 4 + position
            values = {q: pulled[q, rows_of(x + VELOCITY[q][0]), :] for q in range(19)}
            emit(x, x - first + 4, around, position, values)
        return carry

    def edge(x, around):
        values = {}
        for q in range(19):
            target = x + VELOCITY[q][0]
            if target < 0:
                values[q] = low(FACE + XM.index(q))
            elif target > 31:
                values[q] = high(FACE + XP.index(q))
            else:
                values[q] = pulled[q, rows_of(target), :]
        emit(x, x if x < 4 else x - first + 4, around, x % 4, values)

    lowest = [levels_along_x(low)[0], levels[0], levels[1]]
    highest_levels = [levels[6], levels[7], levels_along_x(high)[0]]
    lax.fori_loop(1 + INNER // 4, 7, middle, 0)
    for x in range(28, 32):
        edge(x, highest_levels)
    copies = [
        pltpu.make_async_copy(
            stage.at[:, pl.ds(4, 32 - first)], out.at[:, pl.ds(first, 32 - first)], semaphores.at[0]
        ),
        pltpu.make_async_copy(stage.at[:, pl.ds(0, 4)], out.at[:, pl.ds(0, 4)], semaphores.at[1]),
    ]
    copies[0].start()
    for x in range(4):
        edge(x, lowest)
    copies[1].start()
    for copy in copies:
        copy.wait()


def relay(taken, kept, *outs):
    for n, out in enumerate(outs):
        out[0] = taken[2 + n]
        out[1] = kept[n]


def finish(folded, rims, *refs):
    others, out = refs[:-1], refs[-1]
    count = out.shape[2]
    if len(others) == 1:
        side = lax.axis_index("gy")
        from_low = [jnp.where(side == 1, others[0][n], 0.0) for n in range(2)]
        from_high = [jnp.where(side == 0, others[0][n], 0.0) for n in range(2)]
    else:
        from_low, from_high = [[other[n] for n in range(2)] for other in others]
    sums = jnp.concatenate([folded[0:8, :] + from_low[0], folded[8:16, :] + from_high[0]], axis=0)
    result = lax.dot_general(
        sums,
        basis_along_z(count),
        (((1,), (1,)), ((), ())),
        precision=highest,
        preferred_element_type=f32,
    )
    out[:, 0, :] = result[0:8] + (rims[0] + from_low[1])[:, 0:count]
    out[:, 1, :] = result[8:16] + (rims[1] + from_high[1])[:, 0:count]


def pairs(count, slot):
    partner = {}
    for i in range(slot, count - 1, SLOTS):
        partner[i], partner[i + 1] = i + 1, i
    result = []
    for i in range(count):
        for core in range(2):
            target = (partner[i], core) if i in partner else (i, 1 - core)
            result.append((i * 2 + core, target[0] * 2 + target[1]))
    return result


def per_device(forward, adjoint, coefficients, kind):
    count_y = lax.axis_size("gy")
    count_x = lax.axis_size("gx")
    swap = [(0, 1), (1, 0)]
    side = lax.axis_index("gy")
    directions = 1 if count_y == 2 else 2
    tile = (8, 128)
    shape = jax.ShapeDtypeStruct
    count = coefficients.shape[2]
    up = [(i, i + 1) for i in range(count_y - 1)]
    down = [(i + 1, i) for i in range(count_y - 1)]

    routes = [swap] if directions == 1 else [up, down]
    crossed = [[(a * 2 + c, b * 2 + 1 - c) for a, b in route for c in range(2)] for route in routes]

    own, lines, coarse = kernel_call(
        functools.partial(pack_rows, directions),
        [
            shape((LINE_ROWS * directions + 32, 128), bf16),
            shape((16, 128), f32),
            shape((2,) + tile, f32),
        ],
        [
            pltpu.VMEM((5 * directions,) + adjoint.shape[1:], bf16),
            pltpu.VMEM(coefficients.shape, f32),
            pltpu.VMEM((5, 256, 128), f32),
            pltpu.SemaphoreType.DMA((1 + 5 * directions,)),
        ],
        in_specs=[pl.BlockSpec(memory_space=pltpu.HBM)] * 2,
    )(*(pltpu.with_memory_space_constraint(a, pltpu.HBM) for a in (adjoint, coefficients)))
    taken_rows = lax.ppermute(own, "gz", swap)
    sent_z = kernel_call(pack_z, shape((4,) + tile, f32))(adjoint, coarse)
    received_z = lax.ppermute(sent_z, "gz", swap)
    sent_y = kernel_call(
        functools.partial(pack_y, directions, count), [shape((STRIP, 128), bf16)] * directions
    )(own, taken_rows, coarse)
    received_y = [lax.ppermute(sent, ("gy", "gz"), route) for sent, route in zip(sent_y, crossed)]

    pulled, flows, lines, kind = kernel_call(
        functools.partial(pull_zy, count),
        [
            shape((19, 256, 128), f32),
            shape((5,) + kind.shape, f32),
            shape((16, 128), f32),
            shape(kind.shape, jnp.int32),
        ],
        [
            pltpu.VMEM((2, 2) + tile, f32),
            pltpu.VMEM(forward.shape, bf16),
            pltpu.SemaphoreType.DMA((5,)),
        ],
        cost_estimate=pl.CostEstimate(flops=10**10, bytes_accessed=10**7, transcendentals=0),
        in_specs=[
            pl.BlockSpec(memory_space=pltpu.HBM if n in (1, 2) else pltpu.VMEM) for n in range(5)
        ],
    )(
        adjoint,
        pltpu.with_memory_space_constraint(forward, pltpu.HBM),
        pltpu.with_memory_space_constraint(kind, pltpu.HBM),
        received_z,
        lines,
    )

    pulled, *sent_x, edges, levels = kernel_call(
        functools.partial(pack_x, directions),
        [pulled]
        + [shape((BUNDLE,) + tile, bf16)] * SLOTS
        + [shape((2, 8) + tile, f32), shape((8,) + tile, f32)],
        [pltpu.VMEM((32, 128), f32)],
        aliases={0: 0},
    )(pulled, flows, lines, *received_y)
    received_x = [
        lax.ppermute(sent, ("gx", "gz"), pairs(count_x, slot)) for slot, sent in enumerate(sent_x)
    ]

    prior, totals = kernel_call(
        collide_inside,
        [shape(adjoint.shape, bf16), shape((8,) + tile, f32)],
        [pltpu.VMEM((19, INNER) + tile, bf16), pltpu.SemaphoreType.DMA((INNER // 8,))],
        out_specs=[pl.BlockSpec(memory_space=pltpu.HBM), pl.BlockSpec(memory_space=pltpu.VMEM)],
    )(pulled, flows, kind, levels)
    folded, handed, kept = kernel_call(
        functools.partial(project, count, directions),
        [
            shape((16, 128), f32),
            shape((2 + directions,) + tile, f32),
            shape((directions,) + tile, f32),
        ],
    )(pulled, flows, edges, levels, *received_x, totals)
    taken = lax.ppermute(handed, "gz", swap)
    relayed = kernel_call(relay, [shape((2,) + tile, f32)] * directions)(taken, kept)
    others = [lax.ppermute(sent, ("gy", "gz"), route) for sent, route in zip(relayed, crossed)]
    in_hbm = pl.BlockSpec(memory_space=pltpu.HBM)
    prior = kernel_call(
        collide_outside,
        shape(adjoint.shape, bf16),
        [pltpu.VMEM((19, 32 - INNER) + tile, bf16), pltpu.SemaphoreType.DMA((2,))],
        aliases={4 + SLOTS: 0},
        in_specs=[pl.BlockSpec(memory_space=pltpu.VMEM)] * (4 + SLOTS) + [in_hbm],
        out_specs=in_hbm,
    )(pulled, flows, kind, levels, *received_x, prior)
    gradient = kernel_call(finish, shape(coefficients.shape, f32))(
        folded, taken, *others
    )
    return prior, gradient


def solution(mesh):
    in_specs = (
        P(None, ("parts", "gx"), "gy", "gz"),
        P(None, ("parts", "gx"), "gy", "gz"),
        P(("parts", "gx"), "gy", "gz"),
        P(("parts", "gx"), "gy", "gz"),
    )
    out_specs = (P(None, ("parts", "gx"), "gy", "gz"), P(("parts", "gx"), "gy", "gz"))
    return jax.shard_map(
        per_device, mesh=mesh, in_specs=in_specs, out_specs=out_specs, check_vma=False
    )
```

```python
import functools

import jax
import jax.numpy as jnp
import numpy as np
from jax import lax
from jax.experimental import pallas as pl
from jax.experimental.pallas import tpu as pltpu
from jax.sharding import PartitionSpec as P

VELOCITY = (
    (0, 0, 0),
    (1, 0, 0),
    (-1, 0, 0),
    (0, 1, 0),
    (0, -1, 0),
    (0, 0, 1),
    (0, 0, -1),
    (1, 1, 0),
    (-1, -1, 0),
    (1, -1, 0),
    (-1, 1, 0),
    (1, 0, 1),
    (-1, 0, -1),
    (1, 0, -1),
    (-1, 0, 1),
    (0, 1, 1),
    (0, -1, -1),
    (0, 1, -1),
    (0, -1, 1),
)
OPPOSITE = (0, 2, 1, 4, 3, 6, 5, 8, 7, 10, 9, 12, 11, 14, 13, 16, 15, 18, 17)
highest = lax.Precision.HIGHEST
f32 = jnp.float32
bf16 = jnp.bfloat16


def going(dimension, sign):
    return [q for q in range(19) if VELOCITY[q][dimension] == sign]


XP, XM = going(0, 1), going(0, -1)
YP, YM = going(1, 1), going(1, -1)
ZP, ZM = going(2, 1), going(2, -1)

FACE, NEAR, FAR, FIELD, LEVEL, BUNDLE = 0, 5, 9, 15, 19, 23
SLOTS = 3
LINE_ROWS, STRIP = 160, 176
AHEAD, LATE = 80, 112
MASS, INVERSE = 3, 4
EDGE_PLANES = (0, 1, 2, 3, 28, 29, 30, 31)
INNER = 16


def spline(distance):
    radius = np.abs(distance) / 6.0
    return np.where(radius < 1.0, (1.0 - radius) ** 4 * (1.0 + 4.0 * radius), 0.0)


def spline_along(dimension, shape, position):
    distance = lax.broadcasted_iota(jnp.int32, shape, dimension).astype(f32) - position
    radius = jnp.abs(distance) * (1.0 / 6.0)
    square = (1.0 - radius) * (1.0 - radius)
    return jnp.where(radius < 1.0, square * square * (1.0 + 4.0 * radius), 0.0)


def basis_along_z(count):
    places = lax.broadcasted_iota(jnp.int32, (count, 128), 0).astype(f32)
    return spline_along(1, (count, 128), 4.0 * places + 1.5)


def rim_along_z(core, count):
    return spline_along(1, (8, 128), jnp.where(core == 0, 4.0 * count + 1.5, -2.5))


def basis_along_y(j):
    return spline_along(0, (8, 128), 4.0 * j + 1.5)


def kernel_call(body, out_shape, scratch_shapes=(), aliases=None, **specs):
    return pl.pallas_call(
        body,
        out_shape=out_shape,
        scratch_shapes=list(scratch_shapes),
        compiler_params=pltpu.CompilerParams(vmem_limit_bytes=12 * 1024 * 1024),
        input_output_aliases=aliases or {},
        **specs,
    )


def iota(dimension):
    return lax.broadcasted_iota(jnp.int32, (8, 128), dimension)


def pulled_z(q, tile, x, columns):
    step = VELOCITY[q][2]
    if step == 0:
        return tile
    slot = (ZP if step > 0 else ZM).index(q) * 32
    group, lane = slot // 128, slot % 128
    lanes = iota(1)
    edge = columns[0 if step > 0 else 1, group]
    if step > 0:
        edge = pltpu.roll(edge, 127 - lane - x, 1)
        return jnp.where(lanes == 127, edge, pltpu.roll(tile, 127, 1))
    edge = pltpu.roll(edge, (128 - lane - x) & 127, 1)
    return jnp.where(lanes == 0, edge, pltpu.roll(tile, 1, 1))


def load_columns(core, received, columns):
    for group in range(2):
        tile = received[group]
        columns[0, group] = jnp.where(core == 0, tile, 0.0)
        columns[1, group] = jnp.where(core == 1, tile, 0.0)


def pair_moments(populations):
    sums, diffs = {}, {}
    for q in range(1, 19, 2):
        a, b = populations.get(q), populations.get(q + 1)
        if a is None and b is None:
            continue
        if b is None:
            sums[q], diffs[q] = a, a
        elif a is None:
            sums[q], diffs[q] = b, -b
        else:
            sums[q], diffs[q] = a + b, a - b

    def total(terms):
        value = None
        for sign, table, q in terms:
            if q not in table:
                continue
            item = table[q]
            if value is None:
                value = item if sign > 0 else -item
            else:
                value = value + item if sign > 0 else value - item
        return value

    def plus(a, b):
        return b if a is None else (a if b is None else a + b)

    def twice(a):
        return None if a is None else a + a

    xx = total([(1, sums, 7), (1, sums, 9), (1, sums, 11), (1, sums, 13)])
    edge_yz = total([(1, sums, 15), (1, sums, 17)])
    edge_xy = total([(1, sums, 7), (1, sums, 9)])
    edge_xz = total([(1, sums, 11), (1, sums, 13)])
    sx, sy, sz = (twice(sums.get(q)) for q in (1, 3, 5))
    zeroth = plus(plus(xx, edge_yz), plus(plus(sx, sy), sz))
    if 0 in populations:
        zeroth = zeroth + 12.0 * populations[0]
    mx = plus(twice(diffs.get(1)), total([(1, diffs, 7), (1, diffs, 9), (1, diffs, 11), (1, diffs, 13)]))
    my = plus(twice(diffs.get(3)), total([(1, diffs, 7), (-1, diffs, 9), (1, diffs, 15), (1, diffs, 17)]))
    mz = plus(twice(diffs.get(5)), total([(1, diffs, 11), (-1, diffs, 13), (1, diffs, 15), (-1, diffs, 17)]))
    mxx = plus(sx, xx)
    myy = plus(sy, plus(edge_xy, edge_yz))
    mzz = plus(sz, plus(edge_xz, edge_yz))
    mxy = total([(1, sums, 7), (-1, sums, 9)])
    mxz = total([(1, sums, 11), (-1, sums, 13)])
    myz = total([(1, sums, 15), (-1, sums, 17)])
    return zeroth, (mx, my, mz), (mxx, myy, mzz, mxy, mxz, myz)


def flow_moments(populations):
    sums = {q: populations[q] + populations[q + 1] for q in range(1, 19, 2)}
    diffs = {q: populations[q] - populations[q + 1] for q in range(1, 19, 2)}
    rho = populations[0]
    for q in range(1, 19, 2):
        rho = rho + sums[q]
    jx = (diffs[1] + diffs[7]) + (diffs[9] + diffs[11]) + diffs[13]
    jy = (diffs[3] + diffs[7]) + (diffs[15] - diffs[9]) + diffs[17]
    jz = (diffs[5] + diffs[11]) + (diffs[15] - diffs[13]) - diffs[17]
    return rho, (jx, jy, jz)


def dot3(a, b):
    return a[0] * b[0] + a[1] * b[1] + a[2] * b[2]


def second_times(second, v):
    mxx, myy, mzz, mxy, mxz, myz = second

    def row(terms):
        value = None
        for coefficient, component in terms:
            if coefficient is None:
                continue
            product = coefficient * component
            value = product if value is None else value + product
        return value

    return (
        row([(mxx, v[0]), (mxy, v[1]), (mxz, v[2])]),
        row([(mxy, v[0]), (myy, v[1]), (myz, v[2])]),
        row([(mxz, v[0]), (myz, v[1]), (mzz, v[2])]),
    )


def alpha_beta(moments, flow, flow_mass):
    zeroth, first, second = moments
    scale = flow_mass * (-1.6 / 36.0)
    alpha = scale * 3.0 * dot3(first, flow)
    beta = scale * (9.0 * dot3(second_times(second, flow), flow) - 3.0 * zeroth * dot3(flow, flow))
    return alpha, beta


def rows_of(x, shift=0):
    return pl.ds(x * 8 + 8 - shift, 8)


def rows_at(row, first=0, count=32):
    return pl.ds(8 * first + 8 + row, count, stride=8)


def y_sides():
    return ((YM, 7), (YP, 0))


def pack_rows(directions, adjoint, coefficients, out, lines, coarse, strips, near, plane, semaphores):
    side = lax.axis_index("gy")
    copies = [pltpu.make_async_copy(coefficients, near, semaphores.at[0])]
    for n in range(directions):
        for k in range(5):
            q = YM[k] + (side if directions == 1 else n) * (YP[k] - YM[k])
            slot = 5 * n + k
            copies.append(
                pltpu.make_async_copy(adjoint.at[q], strips.at[slot], semaphores.at[1 + slot])
            )
    for copy in copies:
        copy.start()
    count = coefficients.shape[2]
    copies[0].wait()
    coarse[...] = jnp.zeros((2, 8, 128), f32)
    for j in range(2):
        coarse[j, :, 0:count] = near[:, j, :]
    line = jnp.dot(
        jnp.concatenate([coarse[0], coarse[1]], axis=0),
        jnp.concatenate([basis_along_z(count), jnp.zeros((128 - count, 128), f32)], axis=0),
        precision=highest,
        preferred_element_type=f32,
    )
    lines[...] = line
    high = line.astype(bf16)
    first = LINE_ROWS * directions
    out[first : first + 16, :] = high
    out[first + 16 : first + 32, :] = (line - high.astype(f32)).astype(bf16)
    for copy in copies[1:]:
        copy.wait()

    def emit(row, n):
        for k in range(5 * n, 5 * n + 5):
            for x in range(32):
                plane[k - 5 * n, x * 8 : x * 8 + 8, :] = strips[k, x].astype(f32)
        for k in range(5 * n, 5 * n + 5):
            out[k * 32 : k * 32 + 32, :] = plane[k - 5 * n, pl.ds(row, 32, stride=8), :].astype(bf16)

    for n, (_, row) in enumerate(y_sides()):
        if directions == 1:
            pl.when(side == n)(functools.partial(emit, row, 0))
        else:
            emit(row, n)


def pack_z(adjoint, coarse, out):
    core = lax.axis_index("gz")
    lanes = iota(1)
    for j in range(2):
        out[2 + j] = coarse[j]
    for which, (components, source) in enumerate(((ZM, 127), (ZP, 0))):

        @pl.when(core == which)
        def _():
            chains = {}
            for k, q in enumerate(components):
                for x in range(32):
                    group, lane = divmod(k * 32 + x, 128)
                    column = pltpu.roll(adjoint[q, x].astype(f32), (lane - source) % 128, 1)
                    chain = group, lane // 16
                    if chain in chains:
                        column = jnp.where(lanes >= lane, column, chains[chain])
                    chains[chain] = column
            for group in range(2):
                tile = chains[group, 0]
                for part in range(1, 8 if group == 0 else 2):
                    tile = jnp.where(lanes >= part * 16, chains[group, part], tile)
                out[group] = tile


def pack_y(directions, count, own, taken, coarse, *refs):
    outs, lates, plane = refs[:directions], refs[directions:-1], refs[-1]
    core, side = lax.axis_index("gz"), lax.axis_index("gy")
    lanes = lax.broadcasted_iota(jnp.int32, (32, 128), 1)

    def emit(components, j, n, out, late):
        plane[...] = jnp.zeros((AHEAD + LATE, 128), f32)
        for k, q in enumerate(components):
            place = slice((5 * n + k) * 32, (5 * n + k) * 32 + 32)
            rows = taken[place, :].astype(f32)
            step = VELOCITY[q][2]
            if step:
                shift, edge, holder = (127, 127, 1) if step > 0 else (1, 0, 0)
                border = jnp.where(core == holder, pltpu.roll(own[place, :].astype(f32), shift, 1), 0.0)
                rows = jnp.where(lanes == edge, border, pltpu.roll(rows, shift, 1))
            plane[10 * k : 10 * k + 5, :] = rows[0:5]
            plane[10 * k + 5 : 10 * k + 10, :] = rows[27:32]
            plane[AHEAD + 22 * k : AHEAD + 22 * k + 22, :] = rows[5:27]
        first = LINE_ROWS * directions
        line = taken[first : first + 16, :].astype(f32) + taken[first + 16 : first + 32, :].astype(f32)
        line = add_rim(line[8 * j : 8 * j + 8, :], coarse[j], 1 - core, count)
        high = line.astype(bf16)
        plane[64:72, :] = high.astype(f32)
        plane[72:80, :] = line - high.astype(f32)
        out[...] = plane[0:AHEAD, :].astype(bf16)
        late[...] = plane[AHEAD : AHEAD + LATE, :].astype(bf16)

    for n, (components, _) in enumerate(y_sides()):
        if directions == 1:
            pl.when(side == n)(functools.partial(emit, components, 1 - n, 0, outs[0], lates[0]))
        else:
            emit(components, 1 - n, n, outs[n], lates[n])


def add_rim(line, coarse, core, count):
    rim = jnp.sum(jnp.where(iota(1) == core * (count - 1), coarse, 0.0), axis=1, keepdims=True)
    return line + rim * rim_along_z(core, count)


def pull_zy(
    count, adjoint, forward, kind_far, received, own_lines,
    pulled, flows, lines, kind, columns, semaphores,
):
    copy = pltpu.make_async_copy(kind_far, kind, semaphores.at[0])
    copy.start()
    core = lax.axis_index("gz")
    load_columns(core, received, columns)
    for j in range(2):
        lines[8 * j : 8 * j + 8, :] = add_rim(
            own_lines[8 * j : 8 * j + 8, :], received[2 + j], core, count
        )

    def step(x, carry):
        for q in range(19):
            tile = pulled_z(q, adjoint[q, x].astype(f32), x, columns)
            pulled[q, rows_of(x, VELOCITY[q][1]), :] = tile
        return carry

    def flow(x, carry):
        rho, mass = flow_moments([forward[q, x].astype(f32) for q in range(19)])
        inverse = 1.0 / rho
        for n in range(3):
            flows[n, x] = mass[n] * inverse
        flows[MASS, x] = jnp.where(kind[x] == 0, rho, 0.0)
        flows[INVERSE, x] = inverse
        return carry

    lax.fori_loop(0, 32, step, 0, unroll=4)
    for k in range(5):
        pulled[YP[k], rows_at(7), :] = jnp.zeros((32, 128), f32)
        pulled[YM[k], rows_at(0), :] = jnp.zeros((32, 128), f32)
    copy.wait()
    lax.fori_loop(0, 32, flow, 0, unroll=4)


def pack_x(directions, unpatched, flows, lines, *refs):
    received = refs[:directions]
    pulled, *outs, edges, levels, extra = refs[directions:]
    del unpatched
    side = lax.axis_index("gy")
    place = lax.rem(lax.axis_index("gx"), SLOTS)

    def patch(components, row, strip):
        rows = strip[0:64, :].astype(f32)
        for k, q in enumerate(components):
            pulled[q, rows_at(row, 0, 5), :] = rows[10 * k : 10 * k + 5]
            pulled[q, rows_at(row, 27, 5), :] = rows[10 * k + 5 : 10 * k + 10]

    def outer_line(strip):
        parts = strip[64:80, :].astype(f32)
        return parts[0:8] + parts[8:16]

    if directions == 1:
        pl.when(side == 0)(lambda: patch(YP, 7, received[0]))
        pl.when(side == 1)(lambda: patch(YM, 0, received[0]))
        outer = [(outer_line(received[0]), basis_along_y(jnp.where(side == 0, 2.0, -1.0)))]
    else:
        patch(YM, 0, received[0])
        patch(YP, 7, received[1])
        outer = [(outer_line(received[0]), basis_along_y(-1)), (outer_line(received[1]), basis_along_y(2))]
    terms = [(lines[0:8, :], basis_along_y(0)), (lines[8:16, :], basis_along_y(1))] + outer
    for n, (line, _) in enumerate(terms):
        extra[n * 8 : n * 8 + 8, :] = line
    for i in range(8):
        level = None
        for n, (_, weight) in enumerate(terms):
            term = weight * jnp.broadcast_to(extra[n * 8 + i : n * 8 + i + 1, :], (8, 128))
            level = term if level is None else level + term
        levels[i] = level

    def put(slot, low, high):
        for n, out in enumerate(outs):
            out[slot] = jnp.where(place == n, high, low).astype(bf16)

    def put_split(slot, low, high):
        put(slot, low, high)
        put(slot + 2, low - low.astype(bf16).astype(f32), high - high.astype(bf16).astype(f32))

    for k in range(5):
        put(FACE + k, pulled[XP[k], rows_of(0), :], pulled[XM[k], rows_of(31), :])
    for n in range(4):
        put(FIELD + n, flows[n, 0], flows[n, 31])
    for n in range(2):
        put_split(LEVEL + n, levels[n], levels[7 - n])
    results = []
    for x in EDGE_PLANES:
        values = {}
        for q in range(19):
            target = x + VELOCITY[q][0]
            if 0 <= target < 32:
                values[q] = pulled[q, rows_of(target), :]
        flow = tuple(flows[n, x] for n in range(3))
        results.append(alpha_beta(pair_moments(values), flow, flows[MASS, x]))
    for away in range(4):
        for n in range(2):
            low, high = results[away][n], results[7 - away][n]
            edges[n, away] = low
            edges[n, 7 - away] = high
            if away == 0:
                put_split(NEAR + n, low, high)
            else:
                put(FAR + 2 * (away - 1) + n, low, high)


def slope_of(bent):
    return -1.8 * (1.0 - bent * bent)


def bent_level(around, position):
    value = None
    for shift, level in zip((-1, 0, 1), around):
        term = float(spline(position - 4.0 * shift - 1.5)) * level
        value = term if value is None else value + term
    return jnp.tanh(4.0 * value)


def weight_of(position, shift):
    return float(spline(position - 4.0 * shift - 1.5))


def prior_fields(bent, here, flow, inverse, moments):
    zeroth, first, second = moments
    fluid = here == 0
    retained = 0.55 + 0.45 * bent
    share = jnp.where(fluid, retained, 1.0)
    speed = tuple(share * component for component in flow)
    curved = second_times(second, speed)
    slopes = tuple(3.0 * first[n] + 9.0 * curved[n] - 3.0 * zeroth * speed[n] for n in range(3))
    along = dot3(slopes, flow)
    value = zeroth + 0.5 * (3.0 * dot3(first, speed) + dot3(slopes, speed))
    factor = jnp.where(
        fluid, (1.6 / 36.0) * retained, jnp.where(here == 3, inverse * (1.0 / 36.0), 0.0)
    )
    base = jnp.where(fluid, (1.6 / 36.0) * value, 0.0) - factor * along
    return (base,) + tuple(factor * slope for slope in slopes), along


def emit_prior(stage, slot, here, values, result):
    solid = here == 1
    keep = jnp.where(here == 0, -0.6, 0.0)
    base, bx, by, bz = result
    shifts = {}
    for step_x in (-1, 0, 1):
        row = base if step_x == 0 else (base + bx if step_x > 0 else base - bx)
        for step_y in (-1, 0, 1):
            both = row if step_y == 0 else (row + by if step_y > 0 else row - by)
            shifts[step_x, step_y] = both
    for q in range(19):
        step_x, step_y, step_z = VELOCITY[q]
        shift = shifts[step_x, step_y]
        if step_z:
            shift = shift + bz if step_z > 0 else shift - bz
        kept = jnp.where(solid, values[OPPOSITE[q]], keep * values[q])
        stage[q, slot] = (kept + shift).astype(bf16)


def collide_inside(directions, unpatched, flows, kind, levels, *refs):
    late, (pulled, out, totals, stage, semaphores) = refs[:directions], refs[directions:]
    del unpatched
    side = lax.axis_index("gy")

    def patch(components, row, strip):
        rows = strip[...].astype(f32)
        for k, q in enumerate(components):
            pulled[q, rows_at(row, 5, 22), :] = rows[22 * k : 22 * k + 22]

    if directions == 1:
        pl.when(side == 0)(lambda: patch(YP, 7, late[0]))
        pl.when(side == 1)(lambda: patch(YM, 0, late[0]))
    else:
        patch(YM, 0, late[0])
        patch(YP, 7, late[1])
    totals[...] = jnp.zeros((8, 8, 128), f32)

    def middle(with_prior, block, carry):
        around = [levels[block - 1], levels[block], levels[block + 1]]
        sums = [None] * 3
        for position in range(4):
            x = block * 4 + position
            bent = bent_level(around, position)
            flow = tuple(flows[n, x] for n in range(3))
            values = {q: pulled[q, rows_of(x + VELOCITY[q][0]), :] for q in range(19)}
            moments = pair_moments(values)
            if with_prior:
                result, along = prior_fields(bent, kind[x], flow, flows[INVERSE, x], moments)
                emit_prior(stage, x - 4, kind[x], values, result)
                sensitivity = (-1.6 / 36.0) * flows[MASS, x] * along
            else:
                alpha, beta = alpha_beta(moments, flow, flows[MASS, x])
                sensitivity = alpha + (0.55 + 0.45 * bent) * beta
            sensitivity = sensitivity * slope_of(bent)
            for n in range(3):
                term = weight_of(position, n - 1) * sensitivity
                sums[n] = term if sums[n] is None else sums[n] + term
        for n in range(3):
            totals[block + n - 1] += sums[n]
        return carry

    copies = []
    for part in range(INNER // 8):
        lax.fori_loop(1 + 2 * part, 3 + 2 * part, functools.partial(middle, True), 0)
        copies.append(
            pltpu.make_async_copy(
                stage.at[:, pl.ds(8 * part, 8)], out.at[:, pl.ds(4 + 8 * part, 8)], semaphores.at[part]
            )
        )
        copies[part].start()
    lax.fori_loop(1 + INNER // 4, 7, functools.partial(middle, False), 0)
    for copy in copies:
        copy.wait()


def along_x(received):
    place = lax.axis_index("gx")
    has_low, has_high = place > 0, place < lax.axis_size("gx") - 1
    turn = lax.rem(place, SLOTS)

    def reader(present, first):
        def read(slot):
            value = received[first][slot].astype(f32)
            for n in range(1, SLOTS):
                value = jnp.where(turn == n, received[(n + first) % SLOTS][slot].astype(f32), value)
            return jnp.where(present, value, 0.0)

        return read

    return reader(has_low, SLOTS - 1), reader(has_high, 0)


def levels_along_x(read):
    return [read(LEVEL + n) + read(LEVEL + 2 + n) for n in range(2)]


def fold_rows(tiles, weight):
    sublanes = iota(0)
    tiles = [weight * tile for tile in tiles]
    for bit in (4, 2, 1):
        half = len(tiles) // 2
        tiles = [
            jnp.where(
                sublanes & bit == 0,
                tiles[i] + pltpu.roll(tiles[i], 8 - bit, 0),
                tiles[i + half] + pltpu.roll(tiles[i + half], bit, 0),
            )
            for i in range(half)
        ]
    return tiles[0]


def project(count, directions, pulled, flows, edges, levels, *refs):
    inner, folded, handed, kept = refs[SLOTS:]
    core = lax.axis_index("gz")
    low, high = along_x(refs[:SLOTS])
    totals = [inner[i] for i in range(8)]
    lower = levels_along_x(low)[::-1] + [levels[i] for i in range(3)]
    upper = [levels[i] for i in range(5, 8)] + levels_along_x(high)

    def add(block, position, alpha, beta):
        start = block + 1 if block < 4 else block - 6
        around = (lower if block < 4 else upper)[start : start + 3]
        bent = bent_level(around, position)
        sensitivity = (alpha + (0.55 + 0.45 * bent) * beta) * slope_of(bent)
        for shift in (-1, 0, 1):
            if 0 <= block + shift < 8:
                totals[block + shift] = totals[block + shift] + weight_of(position, shift) * sensitivity

    def faces(ref, components):
        return pair_moments({q: ref(FACE + k) for k, q in enumerate(components)})

    def own(x, components):
        return pair_moments({q: pulled[q, rows_of(x), :] for q in components})

    def flow_at(x):
        return tuple(flows[n, x] for n in range(3))

    missing = {
        (0, 0): alpha_beta(faces(low, XM), flow_at(0), flows[MASS, 0]),
        (7, 3): alpha_beta(faces(high, XP), flow_at(31), flows[MASS, 31]),
        (-1, 3): alpha_beta(own(0, XP), tuple(low(FIELD + n) for n in range(3)), low(FIELD + 3)),
        (8, 0): alpha_beta(own(31, XM), tuple(high(FIELD + n) for n in range(3)), high(FIELD + 3)),
    }
    for block in (-1, 0, 7, 8):
        for position in range(4):
            if block in (0, 7):
                index = position + (4 if block else 0)
                alpha, beta = edges[0, index], edges[1, index]
            else:
                ref, away = (low, 3 - position) if block < 0 else (high, position)
                alpha, beta = (
                    ref(NEAR + n) + ref(NEAR + 2 + n) if away == 0 else ref(FAR + 2 * (away - 1) + n)
                    for n in range(2)
                )
            if (block, position) in missing:
                more = missing[block, position]
                alpha, beta = alpha + more[0], beta + more[1]
            add(block, position, alpha, beta)
    lanes = iota(1)
    rim_z = rim_along_z(core, count)
    sums, rims = [], []
    for j in range(4):
        sums.append(fold_rows(totals, basis_along_y(j - 1)))
        across = jnp.sum(sums[j] * rim_z, axis=1, keepdims=True)
        rims.append(jnp.where(lanes == core * (count - 1), across, 0.0))
    for j in (1, 2):
        folded[8 * j - 8 : 8 * j, :] = sums[j]
        handed[j - 1] = rims[j]
    if directions == 1:
        upper = lax.axis_index("gy") == 0
        handed[2] = jnp.where(upper, sums[3], sums[0])
        kept[0] = jnp.where(upper, rims[3], rims[0])
    else:
        for n, j in enumerate((3, 0)):
            handed[2 + n] = sums[j]
            kept[n] = rims[j]


def collide_outside(pulled, flows, kind, levels, *refs):
    out, stage, semaphores = refs[SLOTS + 1 :]
    low, high = along_x(refs[:SLOTS])
    first = 4 + INNER

    def emit(x, slot, around, position, values):
        flow = tuple(flows[n, x] for n in range(3))
        result, _ = prior_fields(
            bent_level(around, position), kind[x], flow, flows[INVERSE, x], pair_moments(values)
        )
        emit_prior(stage, slot, kind[x], values, result)

    def middle(block, carry):
        around = [levels[block - 1], levels[block], levels[block + 1]]
        for position in range(4):
            x = block * 4 + position
            values = {q: pulled[q, rows_of(x + VELOCITY[q][0]), :] for q in range(19)}
            emit(x, x - first + 4, around, position, values)
        return carry

    def edge(x, around):
        values = {}
        for q in range(19):
            target = x + VELOCITY[q][0]
            if target < 0:
                values[q] = low(FACE + XM.index(q))
            elif target > 31:
                values[q] = high(FACE + XP.index(q))
            else:
                values[q] = pulled[q, rows_of(target), :]
        emit(x, x if x < 4 else x - first + 4, around, x % 4, values)

    lowest = [levels_along_x(low)[0], levels[0], levels[1]]
    highest_levels = [levels[6], levels[7], levels_along_x(high)[0]]
    lax.fori_loop(1 + INNER // 4, 7, middle, 0)
    for x in range(28, 32):
        edge(x, highest_levels)
    copies = [
        pltpu.make_async_copy(
            stage.at[:, pl.ds(4, 32 - first)], out.at[:, pl.ds(first, 32 - first)], semaphores.at[0]
        ),
        pltpu.make_async_copy(stage.at[:, pl.ds(0, 4)], out.at[:, pl.ds(0, 4)], semaphores.at[1]),
    ]
    copies[0].start()
    for x in range(4):
        edge(x, lowest)
    copies[1].start()
    for copy in copies:
        copy.wait()


def relay(taken, kept, *outs):
    for n, out in enumerate(outs):
        out[0] = taken[2 + n]
        out[1] = kept[n]


def finish(folded, rims, *refs):
    others, out = refs[:-1], refs[-1]
    count = out.shape[2]
    if len(others) == 1:
        side = lax.axis_index("gy")
        from_low = [jnp.where(side == 1, others[0][n], 0.0) for n in range(2)]
        from_high = [jnp.where(side == 0, others[0][n], 0.0) for n in range(2)]
    else:
        from_low, from_high = [[other[n] for n in range(2)] for other in others]
    sums = jnp.concatenate([folded[0:8, :] + from_low[0], folded[8:16, :] + from_high[0]], axis=0)
    result = lax.dot_general(
        sums,
        basis_along_z(count),
        (((1,), (1,)), ((), ())),
        precision=highest,
        preferred_element_type=f32,
    )
    out[:, 0, :] = result[0:8] + (rims[0] + from_low[1])[:, 0:count]
    out[:, 1, :] = result[8:16] + (rims[1] + from_high[1])[:, 0:count]


def pairs(count, slot):
    partner = {}
    for i in range(slot, count - 1, SLOTS):
        partner[i], partner[i + 1] = i + 1, i
    result = []
    for i in range(count):
        for core in range(2):
            target = (partner[i], core) if i in partner else (i, 1 - core)
            result.append((i * 2 + core, target[0] * 2 + target[1]))
    return result


def per_device(forward, adjoint, coefficients, kind):
    count_y = lax.axis_size("gy")
    count_x = lax.axis_size("gx")
    swap = [(0, 1), (1, 0)]
    side = lax.axis_index("gy")
    directions = 1 if count_y == 2 else 2
    tile = (8, 128)
    shape = jax.ShapeDtypeStruct
    count = coefficients.shape[2]
    up = [(i, i + 1) for i in range(count_y - 1)]
    down = [(i + 1, i) for i in range(count_y - 1)]

    routes = [swap] if directions == 1 else [up, down]
    crossed = [[(a * 2 + c, b * 2 + 1 - c) for a, b in route for c in range(2)] for route in routes]

    own, lines, coarse = kernel_call(
        functools.partial(pack_rows, directions),
        [
            shape((LINE_ROWS * directions + 32, 128), bf16),
            shape((16, 128), f32),
            shape((2,) + tile, f32),
        ],
        [
            pltpu.VMEM((5 * directions,) + adjoint.shape[1:], bf16),
            pltpu.VMEM(coefficients.shape, f32),
            pltpu.VMEM((5, 256, 128), f32),
            pltpu.SemaphoreType.DMA((1 + 5 * directions,)),
        ],
        in_specs=[pl.BlockSpec(memory_space=pltpu.HBM)] * 2,
    )(*(pltpu.with_memory_space_constraint(a, pltpu.HBM) for a in (adjoint, coefficients)))
    taken_rows = lax.ppermute(own, "gz", swap)
    sent_z = kernel_call(pack_z, shape((4,) + tile, f32))(adjoint, coarse)
    received_z = lax.ppermute(sent_z, "gz", swap)
    sent_y = kernel_call(
        functools.partial(pack_y, directions, count),
        [shape((AHEAD, 128), bf16)] * directions + [shape((LATE, 128), bf16)] * directions,
        [pltpu.VMEM((AHEAD + LATE, 128), f32)],
    )(own, taken_rows, coarse)
    received = [lax.ppermute(sent, ("gy", "gz"), route) for sent, route in zip(sent_y, crossed * 2)]
    received_y, received_late = received[:directions], received[directions:]

    pulled, flows, lines, kind = kernel_call(
        functools.partial(pull_zy, count),
        [
            shape((19, 272, 128), f32),
            shape((5,) + kind.shape, f32),
            shape((16, 128), f32),
            shape(kind.shape, jnp.int32),
        ],
        [
            pltpu.VMEM((2, 2) + tile, f32),
            pltpu.SemaphoreType.DMA((1,)),
        ],
        cost_estimate=pl.CostEstimate(flops=10**10, bytes_accessed=10**7, transcendentals=0),
        in_specs=[
            pl.BlockSpec(memory_space=pltpu.HBM if n == 2 else pltpu.VMEM) for n in range(5)
        ],
    )(
        adjoint,
        forward,
        pltpu.with_memory_space_constraint(kind, pltpu.HBM),
        received_z,
        lines,
    )

    pulled, *sent_x, edges, levels = kernel_call(
        functools.partial(pack_x, directions),
        [pulled]
        + [shape((BUNDLE,) + tile, bf16)] * SLOTS
        + [shape((2, 8) + tile, f32), shape((8,) + tile, f32)],
        [pltpu.VMEM((32, 128), f32)],
        aliases={0: 0},
    )(pulled, flows, lines, *received_y)
    received_x = [
        lax.ppermute(sent, ("gx", "gz"), pairs(count_x, slot)) for slot, sent in enumerate(sent_x)
    ]

    pulled, prior, totals = kernel_call(
        functools.partial(collide_inside, directions),
        [pulled, shape(adjoint.shape, bf16), shape((8,) + tile, f32)],
        [pltpu.VMEM((19, INNER) + tile, bf16), pltpu.SemaphoreType.DMA((INNER // 8,))],
        aliases={0: 0},
        out_specs=[
            pl.BlockSpec(memory_space=space) for space in (pltpu.VMEM, pltpu.HBM, pltpu.VMEM)
        ],
        cost_estimate=pl.CostEstimate(flops=10**10, bytes_accessed=1, transcendentals=0),
    )(pulled, flows, kind, levels, *received_late)
    folded, handed, kept = kernel_call(
        functools.partial(project, count, directions),
        [
            shape((16, 128), f32),
            shape((2 + directions,) + tile, f32),
            shape((directions,) + tile, f32),
        ],
    )(pulled, flows, edges, levels, *received_x, totals)
    taken = lax.ppermute(handed, "gz", swap)
    relayed = kernel_call(relay, [shape((2,) + tile, f32)] * directions)(taken, kept)
    others = [lax.ppermute(sent, ("gy", "gz"), route) for sent, route in zip(relayed, crossed)]
    in_hbm = pl.BlockSpec(memory_space=pltpu.HBM)
    prior = kernel_call(
        collide_outside,
        shape(adjoint.shape, bf16),
        [pltpu.VMEM((19, 32 - INNER) + tile, bf16), pltpu.SemaphoreType.DMA((2,))],
        aliases={4 + SLOTS: 0},
        in_specs=[pl.BlockSpec(memory_space=pltpu.VMEM)] * (4 + SLOTS) + [in_hbm],
        out_specs=in_hbm,
    )(pulled, flows, kind, levels, *received_x, prior)
    gradient = kernel_call(finish, shape(coefficients.shape, f32))(
        folded, taken, *others
    )
    return prior, gradient


def solution(mesh):
    in_specs = (
        P(None, ("parts", "gx"), "gy", "gz"),
        P(None, ("parts", "gx"), "gy", "gz"),
        P(("parts", "gx"), "gy", "gz"),
        P(("parts", "gx"), "gy", "gz"),
    )
    out_specs = (P(None, ("parts", "gx"), "gy", "gz"), P(("parts", "gx"), "gy", "gz"))
    return jax.shard_map(
        per_device, mesh=mesh, in_specs=in_specs, out_specs=out_specs, check_vma=False
    )
```

```python
import functools

import jax
import jax.numpy as jnp
import numpy as np
from jax import lax
from jax.experimental import pallas as pl
from jax.experimental.pallas import tpu as pltpu
from jax.sharding import PartitionSpec as P

VELOCITY = (
    (0, 0, 0),
    (1, 0, 0),
    (-1, 0, 0),
    (0, 1, 0),
    (0, -1, 0),
    (0, 0, 1),
    (0, 0, -1),
    (1, 1, 0),
    (-1, -1, 0),
    (1, -1, 0),
    (-1, 1, 0),
    (1, 0, 1),
    (-1, 0, -1),
    (1, 0, -1),
    (-1, 0, 1),
    (0, 1, 1),
    (0, -1, -1),
    (0, 1, -1),
    (0, -1, 1),
)
OPPOSITE = (0, 2, 1, 4, 3, 6, 5, 8, 7, 10, 9, 12, 11, 14, 13, 16, 15, 18, 17)
highest = lax.Precision.HIGHEST
f32 = jnp.float32
bf16 = jnp.bfloat16


def going(dimension, sign):
    return [q for q in range(19) if VELOCITY[q][dimension] == sign]


XP, XM = going(0, 1), going(0, -1)
YP, YM = going(1, 1), going(1, -1)
ZP, ZM = going(2, 1), going(2, -1)

FACE, NEAR, FAR, FIELD, LEVEL, BUNDLE = 0, 5, 9, 15, 19, 23
SLOTS = 3
LINE_ROWS, STRIP = 160, 176
AHEAD, LATE = 80, 112
MASS, INVERSE = 3, 4
EDGE_PLANES = (0, 1, 2, 3, 28, 29, 30, 31)
INNER = 16


def spline(distance):
    radius = np.abs(distance) / 6.0
    return np.where(radius < 1.0, (1.0 - radius) ** 4 * (1.0 + 4.0 * radius), 0.0)


def spline_along(dimension, shape, position):
    distance = lax.broadcasted_iota(jnp.int32, shape, dimension).astype(f32) - position
    radius = jnp.abs(distance) * (1.0 / 6.0)
    square = (1.0 - radius) * (1.0 - radius)
    return jnp.where(radius < 1.0, square * square * (1.0 + 4.0 * radius), 0.0)


def basis_along_z(count):
    places = lax.broadcasted_iota(jnp.int32, (count, 128), 0).astype(f32)
    return spline_along(1, (count, 128), 4.0 * places + 1.5)


def rim_along_z(core, count):
    return spline_along(1, (8, 128), jnp.where(core == 0, 4.0 * count + 1.5, -2.5))


def basis_along_y(j):
    return spline_along(0, (8, 128), 4.0 * j + 1.5)


def kernel_call(body, out_shape, scratch_shapes=(), aliases=None, **specs):
    return pl.pallas_call(
        body,
        out_shape=out_shape,
        scratch_shapes=list(scratch_shapes),
        compiler_params=pltpu.CompilerParams(vmem_limit_bytes=12 * 1024 * 1024),
        input_output_aliases=aliases or {},
        **specs,
    )


def iota(dimension):
    return lax.broadcasted_iota(jnp.int32, (8, 128), dimension)


def pulled_z(q, tile, edges):
    step = VELOCITY[q][2]
    if step == 0:
        return tile
    if step > 0:
        return jnp.where(iota(1) == 127, edges[0][ZP.index(q)], pltpu.roll(tile, 127, 1))
    return jnp.where(iota(1) == 0, edges[1][ZM.index(q)], pltpu.roll(tile, 1, 1))


def pair_moments(populations):
    sums, diffs = {}, {}
    for q in range(1, 19, 2):
        a, b = populations.get(q), populations.get(q + 1)
        if a is None and b is None:
            continue
        if b is None:
            sums[q], diffs[q] = a, a
        elif a is None:
            sums[q], diffs[q] = b, -b
        else:
            sums[q], diffs[q] = a + b, a - b

    def total(terms):
        value = None
        for sign, table, q in terms:
            if q not in table:
                continue
            item = table[q]
            if value is None:
                value = item if sign > 0 else -item
            else:
                value = value + item if sign > 0 else value - item
        return value

    def plus(a, b):
        return b if a is None else (a if b is None else a + b)

    def twice(a):
        return None if a is None else a + a

    xx = total([(1, sums, 7), (1, sums, 9), (1, sums, 11), (1, sums, 13)])
    edge_yz = total([(1, sums, 15), (1, sums, 17)])
    edge_xy = total([(1, sums, 7), (1, sums, 9)])
    edge_xz = total([(1, sums, 11), (1, sums, 13)])
    sx, sy, sz = (twice(sums.get(q)) for q in (1, 3, 5))
    zeroth = plus(plus(xx, edge_yz), plus(plus(sx, sy), sz))
    if 0 in populations:
        zeroth = zeroth + 12.0 * populations[0]
    mx = plus(twice(diffs.get(1)), total([(1, diffs, 7), (1, diffs, 9), (1, diffs, 11), (1, diffs, 13)]))
    my = plus(twice(diffs.get(3)), total([(1, diffs, 7), (-1, diffs, 9), (1, diffs, 15), (1, diffs, 17)]))
    mz = plus(twice(diffs.get(5)), total([(1, diffs, 11), (-1, diffs, 13), (1, diffs, 15), (-1, diffs, 17)]))
    mxx = plus(sx, xx)
    myy = plus(sy, plus(edge_xy, edge_yz))
    mzz = plus(sz, plus(edge_xz, edge_yz))
    mxy = total([(1, sums, 7), (-1, sums, 9)])
    mxz = total([(1, sums, 11), (-1, sums, 13)])
    myz = total([(1, sums, 15), (-1, sums, 17)])
    return zeroth, (mx, my, mz), (mxx, myy, mzz, mxy, mxz, myz)


def flow_moments(populations):
    sums = {q: populations[q] + populations[q + 1] for q in range(1, 19, 2)}
    diffs = {q: populations[q] - populations[q + 1] for q in range(1, 19, 2)}
    rho = populations[0]
    for q in range(1, 19, 2):
        rho = rho + sums[q]
    jx = (diffs[1] + diffs[7]) + (diffs[9] + diffs[11]) + diffs[13]
    jy = (diffs[3] + diffs[7]) + (diffs[15] - diffs[9]) + diffs[17]
    jz = (diffs[5] + diffs[11]) + (diffs[15] - diffs[13]) - diffs[17]
    return rho, (jx, jy, jz)


def dot3(a, b):
    return a[0] * b[0] + a[1] * b[1] + a[2] * b[2]


def second_times(second, v):
    mxx, myy, mzz, mxy, mxz, myz = second

    def row(terms):
        value = None
        for coefficient, component in terms:
            if coefficient is None:
                continue
            product = coefficient * component
            value = product if value is None else value + product
        return value

    return (
        row([(mxx, v[0]), (mxy, v[1]), (mxz, v[2])]),
        row([(mxy, v[0]), (myy, v[1]), (myz, v[2])]),
        row([(mxz, v[0]), (myz, v[1]), (mzz, v[2])]),
    )


def alpha_beta(moments, flow, flow_mass):
    zeroth, first, second = moments
    scale = flow_mass * (-1.6 / 36.0)
    alpha = scale * 3.0 * dot3(first, flow)
    beta = scale * (9.0 * dot3(second_times(second, flow), flow) - 3.0 * zeroth * dot3(flow, flow))
    return alpha, beta


def rows_of(x, shift=0):
    return pl.ds(x * 8 + 8 - shift, 8)


def rows_at(row, first=0, count=32):
    return pl.ds(8 * first + 8 + row, count, stride=8)


def y_sides():
    return ((YM, 7), (YP, 0))


def pack_rows(directions, adjoint, coefficients, out, lines, coarse, strips, near, plane, semaphores):
    side = lax.axis_index("gy")
    copies = [pltpu.make_async_copy(coefficients, near, semaphores.at[0])]
    for n in range(directions):
        for k in range(5):
            q = YM[k] + (side if directions == 1 else n) * (YP[k] - YM[k])
            slot = 5 * n + k
            copies.append(
                pltpu.make_async_copy(adjoint.at[q], strips.at[slot], semaphores.at[1 + slot])
            )
    for copy in copies:
        copy.start()
    count = coefficients.shape[2]
    copies[0].wait()
    coarse[...] = jnp.zeros((2, 8, 128), f32)
    for j in range(2):
        coarse[j, :, 0:count] = near[:, j, :]
    line = jnp.dot(
        jnp.concatenate([coarse[0], coarse[1]], axis=0),
        jnp.concatenate([basis_along_z(count), jnp.zeros((128 - count, 128), f32)], axis=0),
        precision=highest,
        preferred_element_type=f32,
    )
    lines[...] = line
    high = line.astype(bf16)
    first = LINE_ROWS * directions
    out[first : first + 16, :] = high
    out[first + 16 : first + 32, :] = (line - high.astype(f32)).astype(bf16)
    for copy in copies[1:]:
        copy.wait()

    def emit(row, n):
        for k in range(5 * n, 5 * n + 5):
            for x in range(32):
                plane[k - 5 * n, x * 8 : x * 8 + 8, :] = strips[k, x].astype(f32)
        for k in range(5 * n, 5 * n + 5):
            out[k * 32 : k * 32 + 32, :] = plane[k - 5 * n, pl.ds(row, 32, stride=8), :].astype(bf16)

    for n, (_, row) in enumerate(y_sides()):
        if directions == 1:
            pl.when(side == n)(functools.partial(emit, row, 0))
        else:
            emit(row, n)


def pack_z(adjoint, coarse, out):
    core = lax.axis_index("gz")
    lanes = iota(1)
    for j in range(2):
        out[2 + j] = coarse[j]
    for which, (components, source) in enumerate(((ZM, 127), (ZP, 0))):

        @pl.when(core == which)
        def _():
            chains = {}
            for k, q in enumerate(components):
                for x in range(32):
                    group, lane = divmod(k * 32 + x, 128)
                    column = pltpu.roll(adjoint[q, x].astype(f32), (lane - source) % 128, 1)
                    chain = group, lane // 16
                    if chain in chains:
                        column = jnp.where(lanes >= lane, column, chains[chain])
                    chains[chain] = column
            for group in range(2):
                tile = chains[group, 0]
                for part in range(1, 8 if group == 0 else 2):
                    tile = jnp.where(lanes >= part * 16, chains[group, part], tile)
                out[group] = tile


def pack_y(directions, count, own, taken, coarse, *refs):
    outs, lates, plane = refs[:directions], refs[directions:-1], refs[-1]
    core, side = lax.axis_index("gz"), lax.axis_index("gy")
    lanes = lax.broadcasted_iota(jnp.int32, (32, 128), 1)

    def emit(components, j, n, out, late):
        plane[...] = jnp.zeros((AHEAD + LATE, 128), f32)
        for k, q in enumerate(components):
            place = slice((5 * n + k) * 32, (5 * n + k) * 32 + 32)
            rows = taken[place, :].astype(f32)
            step = VELOCITY[q][2]
            if step:
                shift, edge, holder = (127, 127, 1) if step > 0 else (1, 0, 0)
                border = jnp.where(core == holder, pltpu.roll(own[place, :].astype(f32), shift, 1), 0.0)
                rows = jnp.where(lanes == edge, border, pltpu.roll(rows, shift, 1))
            plane[10 * k : 10 * k + 5, :] = rows[0:5]
            plane[10 * k + 5 : 10 * k + 10, :] = rows[27:32]
            plane[AHEAD + 22 * k : AHEAD + 22 * k + 22, :] = rows[5:27]
        first = LINE_ROWS * directions
        line = taken[first : first + 16, :].astype(f32) + taken[first + 16 : first + 32, :].astype(f32)
        line = add_rim(line[8 * j : 8 * j + 8, :], coarse[j], 1 - core, count)
        high = line.astype(bf16)
        plane[64:72, :] = high.astype(f32)
        plane[72:80, :] = line - high.astype(f32)
        out[...] = plane[0:AHEAD, :].astype(bf16)
        late[...] = plane[AHEAD : AHEAD + LATE, :].astype(bf16)

    for n, (components, _) in enumerate(y_sides()):
        if directions == 1:
            pl.when(side == n)(functools.partial(emit, components, 1 - n, 0, outs[0], lates[0]))
        else:
            emit(components, 1 - n, n, outs[n], lates[n])


def add_rim(line, coarse, core, count):
    rim = jnp.sum(jnp.where(iota(1) == core * (count - 1), coarse, 0.0), axis=1, keepdims=True)
    return line + rim * rim_along_z(core, count)


def pull_zy(
    count, adjoint, forward, kind_far, received, own_lines,
    pulled, flows, lines, kind, semaphores,
):
    copy = pltpu.make_async_copy(kind_far, kind, semaphores.at[0])
    copy.start()
    core = lax.axis_index("gz")
    for j in range(2):
        lines[8 * j : 8 * j + 8, :] = add_rim(
            own_lines[8 * j : 8 * j + 8, :], received[2 + j], core, count
        )

    def step(x, carry):
        edges = [], []
        for k in range(5):
            group, lane = divmod(k * 32, 128)
            edge = pltpu.roll(received[group], (127 * (1 - core) - lane - x) & 127, 1)
            edges[0].append(jnp.where(core == 0, edge, 0.0))
            edges[1].append(jnp.where(core == 1, edge, 0.0))
        for q in range(19):
            tile = pulled_z(q, adjoint[q, x].astype(f32), edges)
            pulled[q, rows_of(x, VELOCITY[q][1]), :] = tile
        return carry

    def flow(x, carry):
        rho, mass = flow_moments([forward[q, x].astype(f32) for q in range(19)])
        inverse = 1.0 / rho
        for n in range(3):
            flows[n, x] = mass[n] * inverse
        flows[MASS, x] = jnp.where(kind[x] == 0, rho, 0.0)
        flows[INVERSE, x] = inverse
        return carry

    lax.fori_loop(0, 32, step, 0, unroll=8)
    for k in range(5):
        pulled[YP[k], rows_at(7), :] = jnp.zeros((32, 128), f32)
        pulled[YM[k], rows_at(0), :] = jnp.zeros((32, 128), f32)
    copy.wait()
    lax.fori_loop(0, 32, flow, 0, unroll=8)


def pack_x(directions, unpatched, flows, lines, *refs):
    received = refs[:directions]
    pulled, *outs, edges, levels, extra = refs[directions:]
    del unpatched
    side = lax.axis_index("gy")
    place = lax.rem(lax.axis_index("gx"), SLOTS)

    def patch(components, row, strip):
        rows = strip[0:64, :].astype(f32)
        for k, q in enumerate(components):
            pulled[q, rows_at(row, 0, 5), :] = rows[10 * k : 10 * k + 5]
            pulled[q, rows_at(row, 27, 5), :] = rows[10 * k + 5 : 10 * k + 10]

    def outer_line(strip):
        parts = strip[64:80, :].astype(f32)
        return parts[0:8] + parts[8:16]

    if directions == 1:
        pl.when(side == 0)(lambda: patch(YP, 7, received[0]))
        pl.when(side == 1)(lambda: patch(YM, 0, received[0]))
        outer = [(outer_line(received[0]), basis_along_y(jnp.where(side == 0, 2.0, -1.0)))]
    else:
        patch(YM, 0, received[0])
        patch(YP, 7, received[1])
        outer = [(outer_line(received[0]), basis_along_y(-1)), (outer_line(received[1]), basis_along_y(2))]
    terms = [(lines[0:8, :], basis_along_y(0)), (lines[8:16, :], basis_along_y(1))] + outer
    for n, (line, _) in enumerate(terms):
        extra[n * 8 : n * 8 + 8, :] = line
    for i in range(8):
        level = None
        for n, (_, weight) in enumerate(terms):
            term = weight * jnp.broadcast_to(extra[n * 8 + i : n * 8 + i + 1, :], (8, 128))
            level = term if level is None else level + term
        levels[i] = level

    def put(slot, low, high):
        for n, out in enumerate(outs):
            out[slot] = jnp.where(place == n, high, low).astype(bf16)

    def put_split(slot, low, high):
        put(slot, low, high)
        put(slot + 2, low - low.astype(bf16).astype(f32), high - high.astype(bf16).astype(f32))

    for k in range(5):
        put(FACE + k, pulled[XP[k], rows_of(0), :], pulled[XM[k], rows_of(31), :])
    for n in range(4):
        put(FIELD + n, flows[n, 0], flows[n, 31])
    for n in range(2):
        put_split(LEVEL + n, levels[n], levels[7 - n])
    results = []
    for x in EDGE_PLANES:
        values = {}
        for q in range(19):
            target = x + VELOCITY[q][0]
            if 0 <= target < 32:
                values[q] = pulled[q, rows_of(target), :]
        flow = tuple(flows[n, x] for n in range(3))
        results.append(alpha_beta(pair_moments(values), flow, flows[MASS, x]))
    for away in range(4):
        for n in range(2):
            low, high = results[away][n], results[7 - away][n]
            edges[n, away] = low
            edges[n, 7 - away] = high
            if away == 0:
                put_split(NEAR + n, low, high)
            else:
                put(FAR + 2 * (away - 1) + n, low, high)


def slope_of(bent):
    return -1.8 * (1.0 - bent * bent)


def bent_level(around, position):
    value = None
    for shift, level in zip((-1, 0, 1), around):
        term = float(spline(position - 4.0 * shift - 1.5)) * level
        value = term if value is None else value + term
    return jnp.tanh(4.0 * value)


def weight_of(position, shift):
    return float(spline(position - 4.0 * shift - 1.5))


def prior_fields(bent, here, flow, inverse, moments):
    zeroth, first, second = moments
    fluid = here == 0
    retained = 0.55 + 0.45 * bent
    share = jnp.where(fluid, retained, 1.0)
    speed = tuple(share * component for component in flow)
    curved = second_times(second, speed)
    slopes = tuple(3.0 * first[n] + 9.0 * curved[n] - 3.0 * zeroth * speed[n] for n in range(3))
    along = dot3(slopes, flow)
    value = zeroth + 0.5 * (3.0 * dot3(first, speed) + dot3(slopes, speed))
    factor = jnp.where(
        fluid, (1.6 / 36.0) * retained, jnp.where(here == 3, inverse * (1.0 / 36.0), 0.0)
    )
    base = jnp.where(fluid, (1.6 / 36.0) * value, 0.0) - factor * along
    return (base,) + tuple(factor * slope for slope in slopes), along


def emit_prior(stage, slot, here, values, result):
    solid = here == 1
    keep = jnp.where(here == 0, -0.6, 0.0)
    base, bx, by, bz = result
    shifts = {}
    for step_x in (-1, 0, 1):
        row = base if step_x == 0 else (base + bx if step_x > 0 else base - bx)
        for step_y in (-1, 0, 1):
            both = row if step_y == 0 else (row + by if step_y > 0 else row - by)
            shifts[step_x, step_y] = both
    for q in range(19):
        step_x, step_y, step_z = VELOCITY[q]
        shift = shifts[step_x, step_y]
        if step_z:
            shift = shift + bz if step_z > 0 else shift - bz
        kept = jnp.where(solid, values[OPPOSITE[q]], keep * values[q])
        stage[q, slot] = (kept + shift).astype(bf16)


def collide_inside(directions, unpatched, flows, kind, levels, *refs):
    late, (pulled, out, totals, stage, semaphores) = refs[:directions], refs[directions:]
    del unpatched
    side = lax.axis_index("gy")

    def patch(components, row, strip):
        rows = strip[...].astype(f32)
        for k, q in enumerate(components):
            pulled[q, rows_at(row, 5, 22), :] = rows[22 * k : 22 * k + 22]

    if directions == 1:
        pl.when(side == 0)(lambda: patch(YP, 7, late[0]))
        pl.when(side == 1)(lambda: patch(YM, 0, late[0]))
    else:
        patch(YM, 0, late[0])
        patch(YP, 7, late[1])
    totals[...] = jnp.zeros((8, 8, 128), f32)

    def middle(with_prior, block, carry):
        around = [levels[block - 1], levels[block], levels[block + 1]]
        sums = [None] * 3
        for position in range(4):
            x = block * 4 + position
            bent = bent_level(around, position)
            flow = tuple(flows[n, x] for n in range(3))
            values = {q: pulled[q, rows_of(x + VELOCITY[q][0]), :] for q in range(19)}
            moments = pair_moments(values)
            if with_prior:
                result, along = prior_fields(bent, kind[x], flow, flows[INVERSE, x], moments)
                emit_prior(stage, x - 4, kind[x], values, result)
                sensitivity = (-1.6 / 36.0) * flows[MASS, x] * along
            else:
                alpha, beta = alpha_beta(moments, flow, flows[MASS, x])
                sensitivity = alpha + (0.55 + 0.45 * bent) * beta
            sensitivity = sensitivity * slope_of(bent)
            for n in range(3):
                term = weight_of(position, n - 1) * sensitivity
                sums[n] = term if sums[n] is None else sums[n] + term
        for n in range(3):
            totals[block + n - 1] += sums[n]
        return carry

    copies = []
    for part in range(INNER // 8):
        lax.fori_loop(1 + 2 * part, 3 + 2 * part, functools.partial(middle, True), 0)
        copies.append(
            pltpu.make_async_copy(
                stage.at[:, pl.ds(8 * part, 8)], out.at[:, pl.ds(4 + 8 * part, 8)], semaphores.at[part]
            )
        )
        copies[part].start()
    lax.fori_loop(1 + INNER // 4, 7, functools.partial(middle, False), 0)
    for copy in copies:
        copy.wait()


def along_x(received):
    place = lax.axis_index("gx")
    has_low, has_high = place > 0, place < lax.axis_size("gx") - 1
    turn = lax.rem(place, SLOTS)

    def reader(present, first):
        def read(slot):
            value = received[first][slot].astype(f32)
            for n in range(1, SLOTS):
                value = jnp.where(turn == n, received[(n + first) % SLOTS][slot].astype(f32), value)
            return jnp.where(present, value, 0.0)

        return read

    return reader(has_low, SLOTS - 1), reader(has_high, 0)


def levels_along_x(read):
    return [read(LEVEL + n) + read(LEVEL + 2 + n) for n in range(2)]


def fold_rows(tiles, weight):
    sublanes = iota(0)
    tiles = [weight * tile for tile in tiles]
    for bit in (4, 2, 1):
        half = len(tiles) // 2
        tiles = [
            jnp.where(
                sublanes & bit == 0,
                tiles[i] + pltpu.roll(tiles[i], 8 - bit, 0),
                tiles[i + half] + pltpu.roll(tiles[i + half], bit, 0),
            )
            for i in range(half)
        ]
    return tiles[0]


def project(count, directions, pulled, flows, edges, levels, *refs):
    inner, folded, handed, kept = refs[SLOTS:]
    core = lax.axis_index("gz")
    low, high = along_x(refs[:SLOTS])
    totals = [inner[i] for i in range(8)]
    lower = levels_along_x(low)[::-1] + [levels[i] for i in range(3)]
    upper = [levels[i] for i in range(5, 8)] + levels_along_x(high)

    def add(block, position, alpha, beta):
        start = block + 1 if block < 4 else block - 6
        around = (lower if block < 4 else upper)[start : start + 3]
        bent = bent_level(around, position)
        sensitivity = (alpha + (0.55 + 0.45 * bent) * beta) * slope_of(bent)
        for shift in (-1, 0, 1):
            if 0 <= block + shift < 8:
                totals[block + shift] = totals[block + shift] + weight_of(position, shift) * sensitivity

    def faces(ref, components):
        return pair_moments({q: ref(FACE + k) for k, q in enumerate(components)})

    def own(x, components):
        return pair_moments({q: pulled[q, rows_of(x), :] for q in components})

    def flow_at(x):
        return tuple(flows[n, x] for n in range(3))

    missing = {
        (0, 0): alpha_beta(faces(low, XM), flow_at(0), flows[MASS, 0]),
        (7, 3): alpha_beta(faces(high, XP), flow_at(31), flows[MASS, 31]),
        (-1, 3): alpha_beta(own(0, XP), tuple(low(FIELD + n) for n in range(3)), low(FIELD + 3)),
        (8, 0): alpha_beta(own(31, XM), tuple(high(FIELD + n) for n in range(3)), high(FIELD + 3)),
    }
    for block in (-1, 0, 7, 8):
        for position in range(4):
            if block in (0, 7):
                index = position + (4 if block else 0)
                alpha, beta = edges[0, index], edges[1, index]
            else:
                ref, away = (low, 3 - position) if block < 0 else (high, position)
                alpha, beta = (
                    ref(NEAR + n) + ref(NEAR + 2 + n) if away == 0 else ref(FAR + 2 * (away - 1) + n)
                    for n in range(2)
                )
            if (block, position) in missing:
                more = missing[block, position]
                alpha, beta = alpha + more[0], beta + more[1]
            add(block, position, alpha, beta)
    lanes = iota(1)
    rim_z = rim_along_z(core, count)
    sums, rims = [], []
    for j in range(4):
        sums.append(fold_rows(totals, basis_along_y(j - 1)))
        across = jnp.sum(sums[j] * rim_z, axis=1, keepdims=True)
        rims.append(jnp.where(lanes == core * (count - 1), across, 0.0))
    for j in (1, 2):
        folded[8 * j - 8 : 8 * j, :] = sums[j]
        handed[j - 1] = rims[j]
    if directions == 1:
        upper = lax.axis_index("gy") == 0
        handed[2] = jnp.where(upper, sums[3], sums[0])
        kept[0] = jnp.where(upper, rims[3], rims[0])
    else:
        for n, j in enumerate((3, 0)):
            handed[2 + n] = sums[j]
            kept[n] = rims[j]


def collide_outside(pulled, flows, kind, levels, *refs):
    out, stage, semaphores = refs[SLOTS + 1 :]
    low, high = along_x(refs[:SLOTS])
    first = 4 + INNER

    def emit(x, slot, around, position, values):
        flow = tuple(flows[n, x] for n in range(3))
        result, _ = prior_fields(
            bent_level(around, position), kind[x], flow, flows[INVERSE, x], pair_moments(values)
        )
        emit_prior(stage, slot, kind[x], values, result)

    def middle(block, carry):
        around = [levels[block - 1], levels[block], levels[block + 1]]
        for position in range(4):
            x = block * 4 + position
            values = {q: pulled[q, rows_of(x + VELOCITY[q][0]), :] for q in range(19)}
            emit(x, x - first + 4, around, position, values)
        return carry

    def edge(x, around):
        values = {}
        for q in range(19):
            target = x + VELOCITY[q][0]
            if target < 0:
                values[q] = low(FACE + XM.index(q))
            elif target > 31:
                values[q] = high(FACE + XP.index(q))
            else:
                values[q] = pulled[q, rows_of(target), :]
        emit(x, x if x < 4 else x - first + 4, around, x % 4, values)

    lowest = [levels_along_x(low)[0], levels[0], levels[1]]
    highest_levels = [levels[6], levels[7], levels_along_x(high)[0]]
    lax.fori_loop(1 + INNER // 4, 7, middle, 0)
    for x in range(28, 32):
        edge(x, highest_levels)
    copies = [
        pltpu.make_async_copy(
            stage.at[:, pl.ds(4, 32 - first)], out.at[:, pl.ds(first, 32 - first)], semaphores.at[0]
        ),
        pltpu.make_async_copy(stage.at[:, pl.ds(0, 4)], out.at[:, pl.ds(0, 4)], semaphores.at[1]),
    ]
    copies[0].start()
    for x in range(4):
        edge(x, lowest)
    copies[1].start()
    for copy in copies:
        copy.wait()


def relay(taken, kept, *outs):
    for n, out in enumerate(outs):
        out[0] = taken[2 + n]
        out[1] = kept[n]


def finish(folded, rims, *refs):
    others, out = refs[:-1], refs[-1]
    count = out.shape[2]
    if len(others) == 1:
        side = lax.axis_index("gy")
        from_low = [jnp.where(side == 1, others[0][n], 0.0) for n in range(2)]
        from_high = [jnp.where(side == 0, others[0][n], 0.0) for n in range(2)]
    else:
        from_low, from_high = [[other[n] for n in range(2)] for other in others]
    sums = jnp.concatenate([folded[0:8, :] + from_low[0], folded[8:16, :] + from_high[0]], axis=0)
    result = lax.dot_general(
        sums,
        basis_along_z(count),
        (((1,), (1,)), ((), ())),
        precision=highest,
        preferred_element_type=f32,
    )
    out[:, 0, :] = result[0:8] + (rims[0] + from_low[1])[:, 0:count]
    out[:, 1, :] = result[8:16] + (rims[1] + from_high[1])[:, 0:count]


def pairs(count, slot):
    partner = {}
    for i in range(slot, count - 1, SLOTS):
        partner[i], partner[i + 1] = i + 1, i
    result = []
    for i in range(count):
        for core in range(2):
            target = (partner[i], core) if i in partner else (i, 1 - core)
            result.append((i * 2 + core, target[0] * 2 + target[1]))
    return result


def per_device(forward, adjoint, coefficients, kind):
    count_y = lax.axis_size("gy")
    count_x = lax.axis_size("gx")
    swap = [(0, 1), (1, 0)]
    side = lax.axis_index("gy")
    directions = 1 if count_y == 2 else 2
    tile = (8, 128)
    shape = jax.ShapeDtypeStruct
    count = coefficients.shape[2]
    up = [(i, i + 1) for i in range(count_y - 1)]
    down = [(i + 1, i) for i in range(count_y - 1)]

    routes = [swap] if directions == 1 else [up, down]
    crossed = [[(a * 2 + c, b * 2 + 1 - c) for a, b in route for c in range(2)] for route in routes]

    own, lines, coarse = kernel_call(
        functools.partial(pack_rows, directions),
        [
            shape((LINE_ROWS * directions + 32, 128), bf16),
            shape((16, 128), f32),
            shape((2,) + tile, f32),
        ],
        [
            pltpu.VMEM((5 * directions,) + adjoint.shape[1:], bf16),
            pltpu.VMEM(coefficients.shape, f32),
            pltpu.VMEM((5, 256, 128), f32),
            pltpu.SemaphoreType.DMA((1 + 5 * directions,)),
        ],
        in_specs=[pl.BlockSpec(memory_space=pltpu.HBM)] * 2,
    )(*(pltpu.with_memory_space_constraint(a, pltpu.HBM) for a in (adjoint, coefficients)))
    taken_rows = lax.ppermute(own, "gz", swap)
    sent_z = kernel_call(pack_z, shape((4,) + tile, f32))(adjoint, coarse)
    received_z = lax.ppermute(sent_z, "gz", swap)
    sent_y = kernel_call(
        functools.partial(pack_y, directions, count),
        [shape((AHEAD, 128), bf16)] * directions + [shape((LATE, 128), bf16)] * directions,
        [pltpu.VMEM((AHEAD + LATE, 128), f32)],
    )(own, taken_rows, coarse)
    received = [lax.ppermute(sent, ("gy", "gz"), route) for sent, route in zip(sent_y, crossed * 2)]
    received_y, received_late = received[:directions], received[directions:]

    pulled, flows, lines, kind = kernel_call(
        functools.partial(pull_zy, count),
        [
            shape((19, 272, 128), f32),
            shape((5,) + kind.shape, f32),
            shape((16, 128), f32),
            shape(kind.shape, jnp.int32),
        ],
        [
            pltpu.SemaphoreType.DMA((1,)),
        ],
        cost_estimate=pl.CostEstimate(flops=10**10, bytes_accessed=10**7, transcendentals=0),
        in_specs=[
            pl.BlockSpec(memory_space=pltpu.HBM if n == 2 else pltpu.VMEM) for n in range(5)
        ],
    )(
        adjoint,
        forward,
        pltpu.with_memory_space_constraint(kind, pltpu.HBM),
        received_z,
        lines,
    )

    pulled, *sent_x, edges, levels = kernel_call(
        functools.partial(pack_x, directions),
        [pulled]
        + [shape((BUNDLE,) + tile, bf16)] * SLOTS
        + [shape((2, 8) + tile, f32), shape((8,) + tile, f32)],
        [pltpu.VMEM((32, 128), f32)],
        aliases={0: 0},
    )(pulled, flows, lines, *received_y)
    received_x = [
        lax.ppermute(sent, ("gx", "gz"), pairs(count_x, slot)) for slot, sent in enumerate(sent_x)
    ]

    pulled, prior, totals = kernel_call(
        functools.partial(collide_inside, directions),
        [pulled, shape(adjoint.shape, bf16), shape((8,) + tile, f32)],
        [pltpu.VMEM((19, INNER) + tile, bf16), pltpu.SemaphoreType.DMA((INNER // 8,))],
        aliases={0: 0},
        out_specs=[
            pl.BlockSpec(memory_space=space) for space in (pltpu.VMEM, pltpu.HBM, pltpu.VMEM)
        ],
        cost_estimate=pl.CostEstimate(flops=10**10, bytes_accessed=1, transcendentals=0),
    )(pulled, flows, kind, levels, *received_late)
    folded, handed, kept = kernel_call(
        functools.partial(project, count, directions),
        [
            shape((16, 128), f32),
            shape((2 + directions,) + tile, f32),
            shape((directions,) + tile, f32),
        ],
    )(pulled, flows, edges, levels, *received_x, totals)
    taken = lax.ppermute(handed, "gz", swap)
    relayed = kernel_call(relay, [shape((2,) + tile, f32)] * directions)(taken, kept)
    others = [lax.ppermute(sent, ("gy", "gz"), route) for sent, route in zip(relayed, crossed)]
    in_hbm = pl.BlockSpec(memory_space=pltpu.HBM)
    prior = kernel_call(
        collide_outside,
        shape(adjoint.shape, bf16),
        [pltpu.VMEM((19, 32 - INNER) + tile, bf16), pltpu.SemaphoreType.DMA((2,))],
        aliases={4 + SLOTS: 0},
        in_specs=[pl.BlockSpec(memory_space=pltpu.VMEM)] * (4 + SLOTS) + [in_hbm],
        out_specs=in_hbm,
    )(pulled, flows, kind, levels, *received_x, prior)
    gradient = kernel_call(finish, shape(coefficients.shape, f32))(
        folded, taken, *others
    )
    return prior, gradient


def solution(mesh):
    in_specs = (
        P(None, ("parts", "gx"), "gy", "gz"),
        P(None, ("parts", "gx"), "gy", "gz"),
        P(("parts", "gx"), "gy", "gz"),
        P(("parts", "gx"), "gy", "gz"),
    )
    out_specs = (P(None, ("parts", "gx"), "gy", "gz"), P(("parts", "gx"), "gy", "gz"))
    return jax.shard_map(
        per_device, mesh=mesh, in_specs=in_specs, out_specs=out_specs, check_vma=False
    )
```
